128 devices in a mesh: row: 8 (over x_hi, y), col: 16 (over x_lo, z, core).
Axes of the slice: x: 4 (x_hi: 2, x_lo: 2; x = x_hi * 2 + x_lo), y: 4, z: 4, core: 2. Of those that a mesh axis runs over, the one named last changes fastest.
Arguments:
- tokens: bfloat16 [16384, 768], P(('row', 'col')), may hold values from -6 to 6
- expert_ids: int32 [16384, 2], P(('row', 'col')), may hold values from 0 to 31, all different within a row; in each aligned block of 128 rows (0 to 127, 128 to 255, ...) at most 16 rows name the same one
- text: bfloat16 [1024, 768], P(('row', 'col')), may hold values from -6 to 6
- w_gate: bfloat16 [32, 768, 3072], P('col', None, 'row'), may hold values from -0.21875 to 0.21875
- w_up: bfloat16 [32, 768, 3072], P('col', None, 'row'), may hold values from -0.21875 to 0.21875
- w_down: bfloat16 [32, 3072, 768], P('col', 'row'), may hold values from -0.109375 to 0.109375
- router: float32 [768, 32], replicated, may hold values from -0.21875 to 0.21875
- log_scale: float32 [1], replicated, may hold values from 1 to 2.3
- bias: float32 [1], replicated, may hold values from -1 to 0.5
- loss_scale: float32 [1], replicated, may hold values from 32768 to 524288
Outputs:
- d_text: float32 [1024, 768], P(('row', 'col'))
- d_tokens: float32 [16384, 768], P(('row', 'col'))
- d_gate: float32 [32, 768, 3072], P('col', None, 'row')
- d_up: float32 [32, 768, 3072], P('col', None, 'row')
- d_down: float32 [32, 3072, 768], P('col', 'row')
- d_router: float32 [768, 32], replicated
The draws below stay inside these ranges and needn't reach their ends.
Inputs may be any that keep to these rules, and one draw needn't show every extreme that they name: `expert_ids`: the two ids of a token differ. Among the 128 rows of one device no expert is named more than 16 times, a bound that some block reaches.
All inputs are finite; a program needn't handle non-finite values.
Results may differ from the reference program's by a relative error of at most 0.025.
Values may be sent and summed in bfloat16 or wider, within the bound.
A program may use at most 128 MiB of HBM per device.

```python
import math
import jax
import jax.numpy as jnp
import numpy as np
from jax import lax

D = 768
FF = 3072
SEQ = 16
EXPERTS = 32
TOK_DEV = 128
TOKENS = 16384
BATCH = 1024
CAP = 16
N_ROW = 8
N_COL = 16


def level_of(own_key, shape, cuts, smallest, high):
    loudness = 1.0
    for axis_at, blocks in cuts:
        draws = jax.random.uniform(jax.random.fold_in(jax.random.fold_in(own_key, 6), axis_at), (blocks,), jnp.float32, smallest / len(cuts), high / len(cuts))
        loudness = loudness * jnp.repeat(jnp.exp(draws), shape[axis_at] // blocks).reshape((-1,) + (1,) * (len(shape) - 1 - axis_at))
    return loudness


def deal_out(key, own, number, rows, amount, top, limit, skew):
    sequence = jax.random.permutation(key, amount)
    heavy_load, ordinary = load_shares(amount, rows * top, limit, skew, True), load_shares(amount, rows * top, limit, skew, False)
    places = jnp.arange(amount)

    def named(tallies, rotation):
        used = int((tallies > 0).sum())
        fixed = max(1, used // 4)
        passed = fixed + (places - fixed + rotation * (used - fixed)) % max(1, amount - fixed)
        return jnp.zeros((amount,), jnp.int32).at[sequence[jnp.where(places < fixed, places, passed)]].set(jnp.asarray(tallies, jnp.int32))

    tallies = jnp.where(number % 4 == 0, named(heavy_load, number // 4), named(ordinary, number - number // 4 - 1))
    mixed = jax.random.permutation(jax.random.fold_in(own, 3), amount)
    giver, sink = mixed[0:amount // 2 * 2:2], mixed[1:amount // 2 * 2:2]
    slack = jnp.minimum(tallies[giver] - 1, limit - tallies[sink]) // 2
    slack = jnp.where((giver == sequence[0]) | (sink == sequence[0]) | (tallies[sink] == 0), 0, jnp.maximum(slack, 0))
    passed = jax.random.randint(jax.random.fold_in(own, 4), (amount // 2,), 0, 1 << 20) % (slack + 1)
    tallies = tallies.at[giver].add(-passed).at[sink].add(passed)
    items = jnp.searchsorted(jnp.cumsum(tallies), jnp.arange(rows * top), side="right").astype(jnp.int32)
    grid = items.reshape(top, rows).T
    grid = grid[jax.random.permutation(jax.random.fold_in(own, 1), rows)]
    rotation = jax.random.randint(jax.random.fold_in(own, 2), (rows, 1), 0, top)
    return jnp.take_along_axis(grid, (jnp.arange(top)[None, :] + rotation) % top, axis=1)


def load_shares(count, total, bound, skew, full):
    weights = [(1 << 20) // math.isqrt(rank ** skew) + 1 for rank in range(1, count + 1)]
    largest = bound if full else min(bound, max(-(-total // count), total * weights[0] // sum(weights)))
    least = 1 if total - largest >= count - 1 else 0
    holding, rest = [largest] + [least] * (count - 1), total - largest - least * (count - 1)
    while rest > 0:
        movable = [i for i in range(1, count) if holding[i] < largest] or [i for i in range(1, count) if holding[i] < bound]
        pool, left = sum([weights[i] for i in movable]), rest
        for i in movable:
            addition = min(bound - holding[i], max(1, left * weights[i] // pool), rest)
            holding[i] = holding[i] + addition
            rest = rest - addition
    return np.array(holding)


def normal_values(key, shape, scale, bound, split=(), held_as=jnp.bfloat16):
    values = scale * jax.random.normal(key, shape, jnp.float32)
    if split:
        values = values * level_of(key, shape, split, -0.22, 0.18)
    return jnp.clip(values, -bound, bound).astype(held_as)


def setup_inputs(seed: int = 0) -> dict:
    arg_keys = jax.random.split(jax.random.key(seed), 11)
    tokens = normal_values(arg_keys[0], (TOKENS, D), 1.0, 6.0, ((0, 128),))
    expert_ids_keys = jax.random.split(jax.random.fold_in(arg_keys[1], 1), TOKENS // TOK_DEV)
    expert_ids_turns = jax.random.permutation(jax.random.fold_in(arg_keys[1], 3), TOKENS // TOK_DEV)
    expert_ids = jax.vmap(lambda own, number: deal_out(jax.random.fold_in(arg_keys[1], 2), own, number, TOK_DEV, EXPERTS, 2, CAP, 2))(expert_ids_keys, expert_ids_turns).reshape((TOKENS, 2))
    text = normal_values(arg_keys[2], (BATCH, D), 1.0, 6.0, ((0, 128),))
    w_gate = normal_values(arg_keys[3], (EXPERTS, D, FF), D ** -0.5, 0.21875, ((0, 16), (2, 8)))
    w_up = normal_values(arg_keys[4], (EXPERTS, D, FF), D ** -0.5, 0.21875, ((0, 16), (2, 8)))
    w_down = normal_values(arg_keys[5], (EXPERTS, FF, D), FF ** -0.5, 0.109375, ((0, 16), (1, 8)))
    router = normal_values(arg_keys[6], (D, EXPERTS), D ** -0.5, 0.21875, (), jnp.float32)
    log_scale = jnp.clip(jax.random.uniform(arg_keys[7], (1,), jnp.float32, 1.0, 2.3), 1.0, 2.3)
    bias = jnp.clip(jax.random.uniform(arg_keys[8], (1,), jnp.float32, -1.0, 0.5), -1.0, 0.5)
    loss_scale = jnp.clip(jnp.exp(jax.random.uniform(arg_keys[9], (1,), jnp.float32, math.log(32768.0), math.log(524288.0))), 32768.0, 524288.0)
    return {"tokens": tokens, "expert_ids": expert_ids, "text": text, "w_gate": w_gate, "w_up": w_up, "w_down": w_down, "router": router, "log_scale": log_scale, "bias": bias, "loss_scale": loss_scale}


def rounded_blocks(pieces):
    total = jnp.zeros(pieces[0].shape, jnp.float32)
    for piece in pieces:
        narrow = lax.optimization_barrier(piece.astype(jnp.bfloat16))
        total = total + narrow.astype(jnp.float32)
    return total.astype(jnp.bfloat16)

def reference(tokens, expert_ids, text, w_gate, w_up, w_down, router, log_scale, bias, loss_scale):
    block = FF // N_ROW
    token_wide = tokens.astype(jnp.float32)
    inverse_rms = lax.rsqrt(lax.optimization_barrier(jnp.mean(token_wide * token_wide, -1, keepdims=True)) + 1e-06)
    normed = token_wide * inverse_rms
    norm_in = normed.astype(jnp.bfloat16)
    norm_wide = norm_in.astype(jnp.float32)
    scores = jnp.dot(norm_wide, router, precision=lax.Precision.HIGHEST)
    choose = (expert_ids[:, :, None] == jnp.arange(EXPERTS, dtype=jnp.int32)[None, None, :]).astype(jnp.float32)
    chosen = lax.optimization_barrier(jnp.sum(choose * scores[:, None, :], -1))
    gates = jax.nn.sigmoid(chosen - chosen[:, ::-1])
    pair_count = 2 * TOKENS
    flat_expert = expert_ids.reshape(-1)
    room = N_ROW * N_COL * CAP

    def listing(expert):
        return jnp.nonzero(flat_expert == expert, size=room, fill_value=pair_count)[0].astype(jnp.int32)
    lists = lax.map(listing, jnp.arange(EXPERTS, dtype=jnp.int32))

    def gathered(index_list):
        return norm_in[jnp.minimum(index_list, pair_count - 1) // 2]

    def expert_forward(item):
        index_list, gate_mat, up_mat, down_mat = item
        rows = gathered(index_list)
        gate_pre = jnp.dot(rows, gate_mat, preferred_element_type=jnp.float32)
        up_pre = jnp.dot(rows, up_mat, preferred_element_type=jnp.float32)
        sigma = jax.nn.sigmoid(gate_pre)
        hidden = (gate_pre * sigma * up_pre).astype(jnp.bfloat16)
        pieces = [jnp.dot(hidden[:, b * block:(b + 1) * block], down_mat[b * block:(b + 1) * block], preferred_element_type=jnp.float32) for b in range(N_ROW)]
        return rounded_blocks(pieces)
    results = lax.map(expert_forward, (lists, w_gate, w_up, w_down))
    flat_lists = lists.reshape(-1)
    y_pairs = jnp.zeros((pair_count + 1, D), jnp.bfloat16).at[flat_lists].set(results.reshape(-1, D))[:pair_count]
    y_pairs = y_pairs.astype(jnp.float32).reshape(TOKENS, 2, D)
    moe_out = token_wide + gates[:, 0, None] * y_pairs[:, 0] + gates[:, 1, None] * y_pairs[:, 1]
    pooled = lax.optimization_barrier(jnp.mean(moe_out.reshape(BATCH, SEQ, D), 1))
    pooled_norm = jnp.sqrt(lax.optimization_barrier(jnp.sum(pooled * pooled, -1, keepdims=True)) + 1e-06)
    embed = pooled / pooled_norm
    embed_b = embed.astype(jnp.bfloat16)
    text_wide = text.astype(jnp.float32)
    text_norm = jnp.sqrt(lax.optimization_barrier(jnp.sum(text_wide * text_wide, -1, keepdims=True)) + 1e-06)
    text_unit = text_wide / text_norm
    text_b = text_unit.astype(jnp.bfloat16)
    scale = jnp.exp(log_scale[0])
    factor = loss_scale[0] * scale / BATCH
    logits = scale * jnp.dot(embed_b, text_b.T, preferred_element_type=jnp.float32) + bias[0]
    counter = jnp.arange(BATCH, dtype=jnp.int32)
    labels = jnp.where(counter[:, None] == counter[None, :], 1.0, -1.0).astype(jnp.float32)
    weights = (-factor * labels * jax.nn.sigmoid(-labels * logits)).astype(jnp.bfloat16)
    embed_grad = jnp.dot(weights, text_b, preferred_element_type=jnp.float32)
    text_grad = jnp.dot(weights.T, embed_b, preferred_element_type=jnp.float32)
    d_text = (text_grad - text_unit * lax.optimization_barrier(jnp.sum(text_unit * text_grad, -1, keepdims=True))) / text_norm
    pooled_grad = (embed_grad - embed * lax.optimization_barrier(jnp.sum(embed * embed_grad, -1, keepdims=True))) / pooled_norm
    out_grad = jnp.repeat(pooled_grad / SEQ, SEQ, axis=0)
    gate_grad = lax.optimization_barrier(jnp.sum(out_grad[:, None, :] * y_pairs, -1))
    down_in = (gates[:, :, None] * out_grad[:, None, :]).astype(jnp.bfloat16).reshape(pair_count, D)
    down_padded = jnp.concatenate([down_in, jnp.zeros((1, D), jnp.bfloat16)], 0)

    def expert_backward(item):
        index_list, gate_mat, up_mat, down_mat = item
        rows = gathered(index_list)
        gate_pre = jnp.dot(rows, gate_mat, preferred_element_type=jnp.float32)
        up_pre = jnp.dot(rows, up_mat, preferred_element_type=jnp.float32)
        sigma = jax.nn.sigmoid(gate_pre)
        silu_gate = gate_pre * sigma
        hidden = (silu_gate * up_pre).astype(jnp.bfloat16)
        incoming = down_padded[index_list]
        hidden_grad = jnp.dot(incoming, down_mat.T, preferred_element_type=jnp.float32)
        slope = sigma * (1.0 + gate_pre * (1.0 - sigma))
        gate_delta = (hidden_grad * up_pre * slope).astype(jnp.bfloat16)
        up_delta = (hidden_grad * silu_gate).astype(jnp.bfloat16)
        grad_down = jnp.dot(hidden.T, incoming, preferred_element_type=jnp.float32)
        grad_gate = jnp.dot(rows.T, gate_delta, preferred_element_type=jnp.float32)
        grad_up = jnp.dot(rows.T, up_delta, preferred_element_type=jnp.float32)
        pieces = []
        for b in range(N_ROW):
            low = b * block
            high = low + block
            pieces.append(jnp.dot(gate_delta[:, low:high], gate_mat[:, low:high].T, preferred_element_type=jnp.float32) + jnp.dot(up_delta[:, low:high], up_mat[:, low:high].T, preferred_element_type=jnp.float32))
        return (grad_gate, grad_up, grad_down, rounded_blocks(pieces))
    d_gate, d_up, d_down, input_rows = lax.map(expert_backward, (lists, w_gate, w_up, w_down))
    input_pairs = jnp.zeros((pair_count + 1, D), jnp.bfloat16).at[flat_lists].set(input_rows.reshape(-1, D))[:pair_count]
    input_pairs = input_pairs.astype(jnp.float32).reshape(TOKENS, 2, D)
    logit_grad = gates * (gate_grad - lax.optimization_barrier(jnp.sum(gates * gate_grad, -1, keepdims=True)))
    score_grad = lax.optimization_barrier(jnp.sum(logit_grad[:, :, None] * choose, 1))
    d_router = jnp.dot(norm_wide.T, score_grad, precision=lax.Precision.HIGHEST)
    norm_grad = input_pairs[:, 0] + input_pairs[:, 1] + jnp.dot(score_grad, router.T, precision=lax.Precision.HIGHEST)
    d_tokens = out_grad + inverse_rms * (norm_grad - normed * lax.optimization_barrier(jnp.mean(norm_grad * normed, -1, keepdims=True)))
    return (d_text, d_tokens, d_gate, d_up, d_down, d_router)
```

```python
import functools

import jax
import jax.numpy as jnp
from jax import lax
from jax.experimental import pallas as pl
from jax.experimental.pallas import tpu as pltpu
from jax.sharding import PartitionSpec as P

EXP_DEV = 2
SEQ = 16
F32 = jnp.float32
BF16 = jnp.bfloat16
MESH = pl.DeviceIdType.MESH
VMEM = pl.BlockSpec(memory_space=pltpu.VMEM)
SMEM = pl.BlockSpec(memory_space=pltpu.SMEM)
ANY = pl.BlockSpec(memory_space=pl.ANY)
N_ROW, N_COL, N_XZ = 8, 16, 8
GROUPS, PER_GROUP = 4, 4


def column_of(place):
    return (place % N_XZ) * 2 + place // N_XZ


def place_of(column):
    return (column % 2) * N_XZ + column // 2


def remote(src, dst, send_sem, recv_sem, row, col):
    return pltpu.make_async_remote_copy(
        src_ref=src, dst_ref=dst, send_sem=send_sem, recv_sem=recv_sem,
        device_id={"row": row, "col": col}, device_id_type=MESH,
    )


def here():
    row, col = lax.axis_index("row"), lax.axis_index("col")
    return row, col, col // 2, col % 2


def greet(all_columns, all_rows):
    row, col, xz, core = here()
    barrier = pltpu.get_barrier_semaphore()

    def signal(r, c):
        pl.semaphore_signal(barrier, inc=1, device_id={"row": r, "col": c}, device_id_type=MESH)

    count = 0
    if all_columns:
        def col_step(d, _):
            signal(row, (col + d) % N_COL)
            return 0
        lax.fori_loop(1, N_COL, col_step, 0)
        count += N_COL - 1
    else:
        def xz_step(d, _):
            signal(row, ((xz + d) % N_XZ) * 2 + core)
            return 0
        lax.fori_loop(1, N_XZ, xz_step, 0)
        signal(row, xz * 2 + 1 - core)
        count += N_XZ
    if all_rows:
        def row_step(d, _):
            signal((row + d) % N_ROW, col)
            return 0
        lax.fori_loop(1, N_ROW, row_step, 0)
        count += N_ROW - 1
    pl.semaphore_wait(barrier, count)


def loop(low, high, step):
    lax.fori_loop(low, high, lambda i, _: (step(i), 0)[1], 0)


class Gather:
    def __init__(self, stage, whole, sems):
        self.stage, self.whole = stage, whole
        self.s1, self.r1, self.s2, self.r2, self.s3, self.r3 = sems
        self.row, self.col, self.xz, self.core = here()

    def first(self, d):
        to = (self.row + d) % N_ROW
        mine = self.stage.at[self.row]
        return remote(mine, mine, self.s1.at[d - 1], self.r1.at[d - 1], to, self.col)

    def second(self, d):
        to = (self.xz + d) % N_XZ
        mine = self.whole.at[self.core, self.xz]
        return remote(mine, mine, self.s2.at[d - 1], self.r2.at[d - 1], self.row, to * 2 + self.core)

    def third(self):
        mine = self.whole.at[self.core]
        return remote(mine, mine, self.s3, self.r3, self.row, self.xz * 2 + 1 - self.core)

    def first_arrived(self, d):
        at = self.stage.at[(self.row + N_ROW - d) % N_ROW]
        remote(at, at, self.s1.at[d - 1], self.r1.at[d - 1], self.row, self.col).wait_recv()

    def second_arrived(self, d):
        at = self.whole.at[self.core, (self.xz + N_XZ - d) % N_XZ]
        remote(at, at, self.s2.at[d - 1], self.r2.at[d - 1], self.row, self.col).wait_recv()

    def start(self, rows):
        self.stage[self.row] = rows
        loop(1, N_ROW, lambda d: self.first(d).start())

    def spread(self):
        loop(1, N_ROW, self.first_arrived)
        block = self.stage[...]
        self.whole[self.core, self.xz] = block.reshape(-1, block.shape[-1]).astype(BF16)
        loop(1, N_XZ, lambda d: self.second(d).start())

    def swap(self):
        loop(1, N_XZ, self.second_arrived)
        self.third().start()

    def finish(self):
        at = self.whole.at[1 - self.core]
        remote(at, at, self.s3, self.r3, self.row, self.col).wait_recv()
        loop(1, N_ROW, lambda d: self.first(d).wait_send())
        loop(1, N_XZ, lambda d: self.second(d).wait_send())
        self.third().wait_send()


def gather_sems():
    dma = pltpu.SemaphoreType.DMA
    return [dma((N_ROW - 1,)), dma((N_ROW - 1,)), dma((N_XZ - 1,)), dma((N_XZ - 1,)), dma, dma]


def dispatch_kernel(
    rows_ref, meta_ref, text_ref, grid_ref, table_ref, everyone_ref,
    stage, own_sem, a_send, a_recv, m_send, m_recv, t_send, t_recv,
    x_send, x_recv, near_send, near_recv, far_send, far_recv, *sems,
):
    row, col, xz, core = here()
    place = core * N_XZ + xz
    y, high = row % 4, row // 4
    other_row = (1 - high) * 4 + y
    greet(True, True)
    texts = Gather(stage, everyone_ref, sems)
    texts.start(text_ref[...])

    def row_of(rel, step):
        return ((high + rel) % 2) * 4 + (y + step + 4) % 4

    def part(d):
        to = (place + d) % N_COL
        return remote(rows_ref.at[to], grid_ref.at[:, place, row], a_send.at[d - 1], a_recv.at[place], row, column_of(to))

    def meta_part(d):
        to = (place + d) % N_COL
        return remote(meta_ref.at[to], table_ref.at[row, place], m_send.at[d - 1], m_recv.at[d - 1], row, column_of(to))

    def meta_arrived(d):
        at = table_ref.at[row, (place + N_COL - d) % N_COL]
        remote(at, at, m_send.at[d - 1], m_recv.at[d - 1], row, col).wait_recv()

    own = pltpu.make_async_copy(rows_ref.at[place], grid_ref.at[:, place, row], own_sem.at[0])
    own_meta = pltpu.make_async_copy(meta_ref.at[place], table_ref.at[row, place], own_sem.at[1])
    own.start()
    own_meta.start()
    loop(1, N_COL, lambda d: part(d).start())
    loop(1, N_COL, lambda d: meta_part(d).start())

    def piece(group, at_row):
        return grid_ref.at[:, pl.ds(group * PER_GROUP, PER_GROUP), at_row]

    def across(group):
        at = piece(group, row)
        return remote(at, at, x_send.at[group], x_recv.at[group], other_row, col)

    def near(way, rel, group):
        at = piece(group, row_of(rel, 0))
        step = 1 - 2 * way
        return remote(at, at, near_send.at[way, rel, group], near_recv.at[way, rel, group], row_of(0, step), col)

    def far(way, rel, half):
        step = 1 - 2 * way
        at = piece(2 * way + half, row_of(rel, -step))
        return remote(at, at, far_send.at[way, rel, half], far_recv.at[way, rel, half], row_of(0, step), col)

    def arrived(at, sem):
        remote(at, at, x_send.at[0], sem, row, col).wait_recv()

    own.wait()
    for group in range(GROUPS):
        def one(i, group=group):
            from_place = group * PER_GROUP + i

            @pl.when(from_place != place)
            def _():
                at = grid_ref.at[:, from_place, row]
                remote(at, at, a_send.at[0], a_recv.at[from_place], row, col).wait_recv()
        loop(0, PER_GROUP, one)
        across(group).start()
        near(0, 0, group).start()
        near(1, 0, group).start()

    def neighbour(way, rel, group):
        step = 1 - 2 * way
        arrived(piece(group, row_of(rel, -step)), near_recv.at[way, rel, group])
        if group // 2 == way:
            far(way, rel, group % 2).start()

    for group in range(GROUPS):
        arrived(piece(group, other_row), x_recv.at[group])
        near(0, 1, group).start()
        near(1, 1, group).start()
        neighbour(0, 0, group)
        neighbour(1, 0, group)
    texts.spread()
    own_meta.wait()
    loop(1, N_COL, meta_arrived)

    def table_copy(d):
        at = table_ref.at[row]
        return remote(at, at, t_send.at[d - 1], t_recv.at[d - 1], (row + d) % N_ROW, col)

    loop(1, N_ROW, lambda d: table_copy(d).start())
    texts.swap()
    for group in range(GROUPS):
        neighbour(0, 1, group)
        neighbour(1, 1, group)
    for rel in range(2):
        for half in range(2):
            for way in range(2):
                arrived(piece(2 * way + half, row_of(rel, 2)), far_recv.at[way, rel, half])

    def table_arrived(d):
        at = table_ref.at[(row + N_ROW - d) % N_ROW]
        remote(at, at, t_send.at[d - 1], t_recv.at[d - 1], row, col).wait_recv()

    loop(1, N_ROW, table_arrived)
    texts.finish()
    loop(1, N_COL, lambda d: part(d).wait_send())
    loop(1, N_COL, lambda d: meta_part(d).wait_send())
    loop(1, N_ROW, lambda d: table_copy(d).wait_send())
    for group in range(GROUPS):
        across(group).wait_send()
        for way in range(2):
            for rel in range(2):
                near(way, rel, group).wait_send()
    for rel in range(2):
        for half in range(2):
            for way in range(2):
                far(way, rel, half).wait_send()


def dispatch(rows, meta, text_rows):
    width = rows.shape[-1]
    dma = pltpu.SemaphoreType.DMA
    capacity = rows.shape[2]
    return pl.pallas_call(
        dispatch_kernel,
        out_shape=(
            jax.ShapeDtypeStruct((EXP_DEV, N_COL, N_ROW, capacity, width), BF16),
            jax.ShapeDtypeStruct((N_ROW, N_COL) + meta.shape[1:], F32),
            jax.ShapeDtypeStruct((2, N_XZ, N_ROW * 8, width), BF16),
        ),
        in_specs=[VMEM] * 3,
        out_specs=(ANY, VMEM, VMEM),
        scratch_shapes=[
            pltpu.VMEM((N_ROW, 8, width), F32),
            dma((2,)), dma((N_COL - 1,)), dma((N_COL,)), dma((N_COL - 1,)), dma((N_COL - 1,)),
            dma((N_ROW - 1,)), dma((N_ROW - 1,)),
            dma((GROUPS,)), dma((GROUPS,)), dma((2, 2, GROUPS)), dma((2, 2, GROUPS)),
            dma((2, 2, 2)), dma((2, 2, 2)),
        ] + gather_sems(),
        compiler_params=pltpu.CompilerParams(
            collective_id=0, has_side_effects=True, vmem_limit_bytes=40 << 20
        ),
    )(rows, meta, text_rows)


def middle_kernel(
    scalars, part_ref, tok_ref, text_ref, norm_ref, everyone_ref, grad_ref, every_grad_ref, d_text_ref,
    half, sums, from_xz, sums_row, from_row, e_stage, e_whole, g_stage,
    s1, r1, s2, r2, s3, r3, *sems,
):
    row, col, xz, core = here()
    width = tok_ref.shape[-1]
    greet(False, True)
    swap = remote(part_ref.at[1 - core], half, s1, r1, row, xz * 2 + 1 - core)
    swap.start()
    swap.wait()

    def add(i):
        sums[i] = (part_ref[core, i].astype(F32) + half[i].astype(F32)).astype(BF16)

    loop(0, N_XZ, add)

    def to_chip(d):
        to = (xz + d) % N_XZ
        return remote(sums.at[to], from_xz.at[d - 1], s2.at[d - 1], r2.at[d - 1], row, to * 2 + core)

    loop(1, N_XZ, lambda d: to_chip(d).start())
    loop(1, N_XZ, lambda d: to_chip(d).wait_recv())
    total = sums[xz].astype(F32)
    for d in range(N_XZ - 1):
        total = total + from_xz[d].astype(F32)
    sums_row[...] = total.reshape(sums_row.shape)

    def to_row(d):
        to = (row + d) % N_ROW
        return remote(sums_row.at[to], from_row.at[d - 1], s3.at[d - 1], r3.at[d - 1], to, col)

    loop(1, N_ROW, lambda d: to_row(d).start())
    loop(1, N_ROW, lambda d: to_row(d).wait_recv())
    total = sums_row[row]
    for d in range(N_ROW - 1):
        total = total + from_row[d]
    pooled = tok_ref[...] + total * (1.0 / SEQ)
    pooled_norm = jnp.sqrt(jnp.sum(pooled * pooled, -1, keepdims=True) + 1e-06)
    embed = pooled / pooled_norm
    embed_b = embed.astype(BF16)
    embeds = Gather(e_stage, e_whole, sems[:6])
    grads = Gather(g_stage, every_grad_ref, sems[6:])
    embeds.start(embed_b.astype(F32))
    scale, shift, factor = scalars[0], scalars[1], scalars[2]
    records = 2 * N_XZ * N_ROW * 8
    first = ((core * N_XZ + xz) * N_ROW + row) * 8
    same = first + lax.broadcasted_iota(jnp.int32, (8, records), 0) == lax.broadcasted_iota(
        jnp.int32, (8, records), 1
    )
    labels = jnp.where(same, 1.0, -1.0).astype(F32)

    def weigh(mine, others):
        logits = scale * lax.dot_general(mine, others, (((1,), (1,)), ((), ())), preferred_element_type=F32) + shift
        weights = (-factor * labels * jax.nn.sigmoid(-labels * logits)).astype(BF16)
        return jnp.dot(weights, others, preferred_element_type=F32)

    embed_grad = weigh(embed_b, everyone_ref[...].reshape(records, width))
    pooled_grad = (embed_grad - embed * jnp.sum(embed * embed_grad, -1, keepdims=True)) / pooled_norm
    out_grad = pooled_grad * (1.0 / SEQ)
    grad_ref[...] = out_grad
    grads.start(out_grad)
    grads.spread()
    embeds.spread()
    grads.swap()
    embeds.swap()
    grads.finish()
    embeds.finish()
    text_unit = text_ref[...]
    text_grad = weigh(text_unit.astype(BF16), e_whole[...].reshape(records, width))
    d_text_ref[...] = (text_grad - text_unit * jnp.sum(text_unit * text_grad, -1, keepdims=True)) / norm_ref[...]
    swap_like = to_chip
    loop(1, N_XZ, lambda d: swap_like(d).wait_send())
    loop(1, N_ROW, lambda d: to_row(d).wait_send())


def middle(scalars, part, tok_mean, text_unit, text_norm, everyone):
    width = tok_mean.shape[-1]
    dma = pltpu.SemaphoreType.DMA
    whole = (2, N_XZ, N_ROW * 8, width)
    return pl.pallas_call(
        middle_kernel,
        out_shape=(
            jax.ShapeDtypeStruct((8, width), F32),
            jax.ShapeDtypeStruct(whole, BF16),
            jax.ShapeDtypeStruct((8, width), F32),
        ),
        in_specs=[SMEM] + [VMEM] * 5,
        out_specs=(VMEM,) * 3,
        scratch_shapes=[
            pltpu.VMEM(whole[1:], BF16), pltpu.VMEM(whole[1:], BF16),
            pltpu.VMEM((N_XZ - 1,) + whole[2:], BF16),
            pltpu.VMEM((N_ROW, 8, width), F32), pltpu.VMEM((N_ROW - 1, 8, width), F32),
            pltpu.VMEM((N_ROW, 8, width), F32), pltpu.VMEM(whole, BF16), pltpu.VMEM((N_ROW, 8, width), F32),
            dma, dma, dma((N_XZ - 1,)), dma((N_XZ - 1,)), dma((N_ROW - 1,)), dma((N_ROW - 1,)),
        ] + gather_sems() + gather_sems(),
        compiler_params=pltpu.CompilerParams(
            collective_id=1, has_side_effects=True, vmem_limit_bytes=40 << 20
        ),
    )(scalars, part, tok_mean, text_unit, text_norm, everyone)


def return_kernel(
    part_ref, q_ref, out_ref, q_out_ref,
    far_buf, near_buf, x_buf, sum_buf, q_buf, q_msg,
    own_sem, far_send, far_recv, near_send, near_recv, x_send, x_recv, a_send, a_recv,
    q1_send, q1_recv, q2_send, q2_recv,
):
    row, col, xz, core = here()
    place = core * N_XZ + xz
    y, high = row % 4, row // 4
    other_row = (1 - high) * 4 + y
    greet(True, True)

    def row_of(rel, step):
        return ((high + rel) % 2) * 4 + (y + step + 4) % 4

    def q_row(d):
        to = (row + d) % N_ROW
        return remote(q_ref.at[to], q_buf.at[d - 1], q1_send.at[d - 1], q1_recv.at[d - 1], to, col)

    loop(1, N_ROW, lambda d: q_row(d).start())

    def piece(group, at_row):
        return part_ref.at[:, pl.ds(group * PER_GROUP, PER_GROUP), at_row]

    def far(way, rel, half):
        return remote(
            piece(2 * way + half, row_of(rel, 2)), far_buf.at[way, rel, half],
            far_send.at[way, rel, half], far_recv.at[way, rel, half], row_of(0, 1 - 2 * way), col,
        )

    def near(way, rel, group):
        step = 1 - 2 * way
        src = far_buf.at[way, rel, group % 2] if group // 2 == way else piece(group, row_of(rel, step))
        return remote(
            src, near_buf.at[way, rel, group],
            near_send.at[way, rel, group], near_recv.at[way, rel, group], row_of(0, step), col,
        )

    def across(group):
        return remote(near_buf.at[0, 1, group], x_buf.at[group], x_send.at[group], x_recv.at[group], other_row, col)

    def add_into(target, *terms):
        for x in range(EXP_DEV):
            for i in range(PER_GROUP):
                total = terms[0][x, i].astype(F32)
                for term in terms[1:]:
                    total = total + term[x, i].astype(F32)
                target[x, i] = total.astype(BF16)

    for half in range(2):
        for rel in (1, 0):
            for way in range(2):
                far(way, rel, half).start()
    for rel in (1, 0):
        for half in range(2):
            for way in range(2):
                near(way, rel, 2 * (1 - way) + half).start()
    for half in range(2):
        for rel in (1, 0):
            for way in range(2):
                step = 1 - 2 * way
                far(way, rel, half).wait_recv()
                at = far_buf.at[way, rel, half]
                add_into(at, at, piece(2 * way + half, row_of(rel, step)))
                near(way, rel, 2 * way + half).start()
    loop(1, N_ROW, lambda d: q_row(d).wait_recv())
    total = q_ref[row]
    for d in range(N_ROW - 1):
        total = total + q_buf[d]
    q_msg[...] = jnp.broadcast_to(total[:, None, :], q_msg.shape)
    q_out_ref[place] = q_msg[place]

    def q_col(d):
        to = (place + d) % N_COL
        return remote(q_msg.at[to], q_out_ref.at[place], q2_send.at[d - 1], q2_recv.at[d - 1], row, column_of(to))

    def q_col_arrived(d):
        at = q_out_ref.at[(place + N_COL - d) % N_COL]
        remote(at, at, q2_send.at[d - 1], q2_recv.at[d - 1], row, col).wait_recv()

    loop(1, N_COL, lambda d: q_col(d).start())
    for group in (2, 0, 3, 1):
        near(0, 1, group).wait_recv()
        near(1, 1, group).wait_recv()
        at = near_buf.at[0, 1, group]
        add_into(at, at, near_buf.at[1, 1, group], piece(group, other_row))
        across(group).start()

    def back(group, i):
        to = group * PER_GROUP + i
        return remote(sum_buf.at[group, :, i], out_ref.at[place], a_send.at[to], a_recv.at[place], row, column_of(to))

    def own_back(group, i):
        return pltpu.make_async_copy(sum_buf.at[group, :, i], out_ref.at[place], own_sem)

    for group in (2, 0, 3, 1):
        near(0, 0, group).wait_recv()
        near(1, 0, group).wait_recv()
        across(group).wait_recv()
        add_into(
            sum_buf.at[group], near_buf.at[0, 0, group], near_buf.at[1, 0, group], x_buf.at[group], piece(group, row)
        )

        def send(i, group=group):
            @pl.when(group * PER_GROUP + i != place)
            def _():
                back(group, i).start()

            @pl.when(group * PER_GROUP + i == place)
            def _():
                own_back(group, i).start()
        loop(0, PER_GROUP, send)

    def back_arrived(d):
        at = out_ref.at[(place + N_COL - d) % N_COL]
        remote(at, at, a_send.at[0], a_recv.at[(place + N_COL - d) % N_COL], row, col).wait_recv()

    loop(1, N_COL, back_arrived)
    own_back(0, 0).wait()
    loop(1, N_COL, q_col_arrived)
    loop(1, N_ROW, lambda d: q_row(d).wait_send())
    loop(1, N_COL, lambda d: q_col(d).wait_send())
    for group in range(GROUPS):
        across(group).wait_send()

        def sent(i, group=group):
            @pl.when(group * PER_GROUP + i != place)
            def _():
                back(group, i).wait_send()
        loop(0, PER_GROUP, sent)
        for way in range(2):
            for rel in range(2):
                near(way, rel, group).wait_send()
    for rel in range(2):
        for half in range(2):
            for way in range(2):
                far(way, rel, half).wait_send()


def give_back(part, q):
    capacity, width = part.shape[-2:]
    dma = pltpu.SemaphoreType.DMA
    block = (EXP_DEV, PER_GROUP, capacity, width)
    return pl.pallas_call(
        return_kernel,
        out_shape=(
            jax.ShapeDtypeStruct((N_COL, EXP_DEV, capacity, width), BF16),
            jax.ShapeDtypeStruct((N_COL, 8, q.shape[-1]), F32),
        ),
        in_specs=[VMEM] * 2,
        out_specs=(VMEM,) * 2,
        scratch_shapes=[
            pltpu.VMEM((2, 2, 2) + block, BF16), pltpu.VMEM((2, 2, GROUPS) + block, BF16),
            pltpu.VMEM((GROUPS,) + block, BF16), pltpu.VMEM((GROUPS,) + block, BF16),
            pltpu.VMEM((N_ROW - 1,) + q.shape[1:], F32), pltpu.VMEM((N_COL, 8, q.shape[-1]), F32),
            dma, dma((2, 2, 2)), dma((2, 2, 2)), dma((2, 2, GROUPS)), dma((2, 2, GROUPS)),
            dma((GROUPS,)), dma((GROUPS,)), dma((N_COL,)), dma((N_COL,)),
            dma((N_ROW - 1,)), dma((N_ROW - 1,)), dma((N_COL - 1,)), dma((N_COL - 1,)),
        ],
        compiler_params=pltpu.CompilerParams(
            collective_id=2, has_side_effects=True, vmem_limit_bytes=50 << 20
        ),
    )(part, q)


def reduce_kernel(in_ref, out_ref, from_row, mine, s1, r1, s2, r2, s3, r3):
    row, col, xz, core = here()
    greet(True, True)

    def scatter(d):
        to = (row + d) % N_ROW
        return remote(in_ref.at[to], from_row.at[row], s1.at[d - 1], r1.at[d - 1], to, col)

    def scattered(d):
        at = from_row.at[(row + N_ROW - d) % N_ROW]
        remote(at, at, s1.at[d - 1], r1.at[d - 1], row, col).wait_recv()

    def share(d):
        return remote(mine.at[col], mine.at[col], s2.at[d - 1], r2.at[d - 1], row, (col + d) % N_COL)

    def shared(d):
        at = mine.at[(col + N_COL - d) % N_COL]
        remote(at, at, s2.at[d - 1], r2.at[d - 1], row, col).wait_recv()

    def tell(d):
        return remote(out_ref.at[row], out_ref.at[row], s3.at[d - 1], r3.at[d - 1], (row + d) % N_ROW, col)

    def told(d):
        at = out_ref.at[(row + N_ROW - d) % N_ROW]
        remote(at, at, s3.at[d - 1], r3.at[d - 1], row, col).wait_recv()

    loop(1, N_ROW, lambda d: scatter(d).start())
    from_row[row] = in_ref[row]
    loop(1, N_ROW, scattered)
    mine[col] = jnp.sum(from_row[...], 0)
    loop(1, N_COL, lambda d: share(d).start())
    loop(1, N_COL, shared)
    out_ref[row] = jnp.sum(mine[...], 0)
    loop(1, N_ROW, lambda d: tell(d).start())
    loop(1, N_ROW, told)
    loop(1, N_ROW, lambda d: scatter(d).wait_send())
    loop(1, N_COL, lambda d: share(d).wait_send())
    loop(1, N_ROW, lambda d: tell(d).wait_send())


def reduce_all(part):
    dma = pltpu.SemaphoreType.DMA
    cut = part.reshape(N_ROW, -1, 128)
    total = pl.pallas_call(
        reduce_kernel,
        out_shape=jax.ShapeDtypeStruct(cut.shape, F32),
        in_specs=[VMEM],
        out_specs=VMEM,
        scratch_shapes=[
            pltpu.VMEM(cut.shape, F32), pltpu.VMEM((N_COL,) + cut.shape[1:], F32),
            dma((N_ROW - 1,)), dma((N_ROW - 1,)), dma((N_COL - 1,)), dma((N_COL - 1,)),
            dma((N_ROW - 1,)), dma((N_ROW - 1,)),
        ],
        compiler_params=pltpu.CompilerParams(collective_id=3, has_side_effects=True),
    )(cut)
    return total.reshape(part.shape)


def body(tokens, expert_ids, text, w_gate, w_up, w_down, router, log_scale, bias, loss_scale):
    tok_count, width = tokens.shape
    samples = tok_count // SEQ
    experts = EXP_DEV * N_COL
    capacity = max(2, 4 * tok_count // experts)
    batch = samples * N_ROW * N_COL
    token_wide = tokens.astype(F32)
    inverse_rms = lax.rsqrt(jnp.mean(token_wide * token_wide, -1, keepdims=True) + 1e-06)
    normed = token_wide * inverse_rms
    norm_in = normed.astype(BF16)
    norm_wide = norm_in.astype(F32)
    scores = jnp.dot(norm_wide, router, precision=lax.Precision.HIGHEST)
    choose = (expert_ids[:, :, None] == jnp.arange(experts, dtype=jnp.int32)[None, None, :]).astype(F32)
    chosen = jnp.sum(choose * scores[:, None, :], -1)
    gates = jax.nn.sigmoid(chosen - chosen[:, ::-1])
    flat_expert = expert_ids.reshape(-1)
    member = (flat_expert[:, None] == jnp.arange(experts, dtype=jnp.int32)[None, :]).astype(jnp.int32)
    position = jnp.sum(jnp.cumsum(member, 0) * member, 1) - 1
    slot_index = place_of(flat_expert // EXP_DEV) * (EXP_DEV * capacity) + (flat_expert % EXP_DEV) * capacity + position
    hit = slot_index[None, :] == jnp.arange(experts * capacity, dtype=jnp.int32)[:, None]
    table = hit.astype(BF16)
    pair_rows = jnp.repeat(norm_in, 2, axis=0)
    outgoing = jnp.dot(table, pair_rows, preferred_element_type=F32).astype(BF16)
    slot_gate = jnp.sum(jnp.where(hit, gates.reshape(1, -1), 0.0), -1)
    pair_record = (jnp.arange(2 * tok_count, dtype=jnp.int32) // (2 * SEQ))[None, :]
    slot_record = jnp.sum(jnp.where(hit, pair_record, 0), -1)
    in_record = slot_record.reshape(N_COL, 1, -1) == jnp.arange(samples, dtype=jnp.int32)[None, :, None]
    meta = jnp.where(in_record, slot_gate.reshape(N_COL, 1, -1), 0.0)
    meta = jnp.pad(meta, ((0, 0), (0, 0), (0, 128 - meta.shape[-1])))

    text_wide = text.astype(F32)
    text_norm = jnp.sqrt(jnp.sum(text_wide * text_wide, -1, keepdims=True) + 1e-06)
    text_unit = text_wide / text_norm

    grid, gate_table, everyone = dispatch(outgoing.reshape(N_COL, EXP_DEV, capacity, width), meta, text_unit)

    picked = gate_table[..., : EXP_DEV * capacity].reshape(N_ROW, N_COL, samples, EXP_DEV, capacity)
    picked = picked.transpose(3, 1, 0, 2, 4).reshape(EXP_DEV, 8, 16, samples, 1, capacity)
    pool = (picked * jnp.eye(16, dtype=F32)[:, None, :, None]).astype(BF16)
    pool = pool.reshape(EXP_DEV, 8, 16 * samples, 16 * capacity)

    rows = grid.reshape(EXP_DEV, -1, width)
    gate_pre = jnp.einsum("xsd,xdf->xsf", rows, w_gate, preferred_element_type=F32)
    up_pre = jnp.einsum("xsd,xdf->xsf", rows, w_up, preferred_element_type=F32)
    sigma = jax.nn.sigmoid(gate_pre)
    silu_gate = gate_pre * sigma
    hidden = (silu_gate * up_pre).astype(BF16)
    units = hidden.shape[-1]
    pooled_hidden = jnp.einsum(
        "xgrs,xgsf->xgrf", pool, hidden.reshape(EXP_DEV, 8, -1, units), preferred_element_type=F32
    ).astype(BF16).reshape(EXP_DEV, batch, units)
    share = jnp.einsum("xrf,xfd->rd", pooled_hidden, w_down, preferred_element_type=F32).astype(BF16)

    scale = jnp.exp(log_scale[0])
    scalars = jnp.stack([scale, bias[0], loss_scale[0] * scale / batch])
    tok_mean = jnp.mean(token_wide.reshape(samples, SEQ, width), 1)
    own_grad, every_grad, d_text = middle(
        scalars, share.reshape(2, N_XZ, -1, width), tok_mean, text_unit, text_norm, everyone
    )
    every_grad = every_grad.reshape(batch, width)
    back = jnp.einsum("rd,xfd->xrf", every_grad, w_down, preferred_element_type=F32).astype(BF16)
    hidden_grad = jnp.einsum(
        "xgrs,xgrf->xgsf", pool, back.reshape(EXP_DEV, 8, -1, units), preferred_element_type=F32
    ).reshape(hidden.shape)
    q_part = jnp.sum(hidden.astype(F32) * hidden_grad, -1).reshape(EXP_DEV, N_COL, N_ROW, capacity)
    q_part = q_part.transpose(2, 1, 0, 3).reshape(N_ROW, N_COL, EXP_DEV * capacity)
    q_part = jnp.pad(q_part, ((0, 0), (0, 0), (0, 128 - q_part.shape[-1])))
    slope = sigma * (1.0 + gate_pre * (1.0 - sigma))
    gate_delta = (hidden_grad * up_pre * slope).astype(BF16)
    up_delta = (hidden_grad * silu_gate).astype(BF16)
    d_down = jnp.einsum("xrf,rd->xfd", pooled_hidden, every_grad, preferred_element_type=F32)
    d_gate = jnp.einsum("xsd,xsf->xdf", rows, gate_delta, preferred_element_type=F32)
    d_up = jnp.einsum("xsd,xsf->xdf", rows, up_delta, preferred_element_type=F32)
    input_part = jnp.einsum("xsf,xdf->xsd", gate_delta, w_gate, preferred_element_type=F32) + jnp.einsum(
        "xsf,xdf->xsd", up_delta, w_up, preferred_element_type=F32
    )
    input_slots, q_slots = give_back(input_part.astype(BF16).reshape(grid.shape), q_part)

    both = (hit[:, ::2] | hit[:, 1::2]).astype(BF16)
    input_sum = lax.dot_general(
        both, input_slots.reshape(-1, width), (((0,), (0,)), ((), ())), preferred_element_type=F32
    )
    q_flat = q_slots[:, 0, : EXP_DEV * capacity].reshape(-1, 1)
    q = jnp.sum(jnp.where(hit, q_flat, 0.0), 0).reshape(tok_count, 2)
    logit_grad = q - gates * jnp.sum(q, -1, keepdims=True)
    score_grad = jnp.sum(logit_grad[:, :, None] * choose, 1)
    d_router = reduce_all(jnp.dot(norm_wide.T, score_grad, precision=lax.Precision.HIGHEST))
    out_grad = jnp.repeat(own_grad, SEQ, axis=0)
    norm_grad = input_sum + jnp.dot(score_grad, router.T, precision=lax.Precision.HIGHEST)
    d_tokens = out_grad + inverse_rms * (norm_grad - normed * jnp.mean(norm_grad * normed, -1, keepdims=True))
    return (d_text, d_tokens, d_gate, d_up, d_down, d_router)


def solution(mesh):
    in_specs = (
        P(("row", "col"), None),
        P(("row", "col"), None),
        P(("row", "col"), None),
        P("col", None, "row"),
        P("col", None, "row"),
        P("col", "row", None),
        P(),
        P(),
        P(),
        P(),
    )
    out_specs = (
        P(("row", "col"), None),
        P(("row", "col"), None),
        P("col", None, "row"),
        P("col", None, "row"),
        P("col", "row", None),
        P(),
    )
    return jax.shard_map(body, mesh=mesh, in_specs=in_specs, out_specs=out_specs, check_vma=False)
```

```python
import functools
import types

import jax
import jax.numpy as jnp
from jax import lax
from jax.experimental import pallas as pl
from jax.experimental.pallas import tpu as pltpu
from jax.sharding import PartitionSpec as P

EXP_DEV = 2
SEQ = 16
F32 = jnp.float32
BF16 = jnp.bfloat16
MESH = pl.DeviceIdType.MESH
VMEM = pl.BlockSpec(memory_space=pltpu.VMEM)
SMEM = pl.BlockSpec(memory_space=pltpu.SMEM)
ANY = pl.BlockSpec(memory_space=pl.ANY)
N_ROW, N_COL, N_XZ = 8, 16, 8
GROUPS, PER_GROUP = 4, 4


def column_of(place):
    return (place % N_XZ) * 2 + place // N_XZ


def place_of(column):
    return (column % 2) * N_XZ + column // 2


def remote(src, dst, send_sem, recv_sem, row, col):
    return pltpu.make_async_remote_copy(
        src_ref=src, dst_ref=dst, send_sem=send_sem, recv_sem=recv_sem,
        device_id={"row": row, "col": col}, device_id_type=MESH,
    )


def here():
    row, col = lax.axis_index("row"), lax.axis_index("col")
    return row, col, col // 2, col % 2


def greet(all_columns, all_rows):
    row, col, xz, core = here()
    barrier = pltpu.get_barrier_semaphore()

    def signal(r, c):
        pl.semaphore_signal(barrier, inc=1, device_id={"row": r, "col": c}, device_id_type=MESH)

    count = 0
    if all_columns:
        def col_step(d, _):
            signal(row, (col + d) % N_COL)
            return 0
        lax.fori_loop(1, N_COL, col_step, 0)
        count += N_COL - 1
    else:
        def xz_step(d, _):
            signal(row, ((xz + d) % N_XZ) * 2 + core)
            return 0
        lax.fori_loop(1, N_XZ, xz_step, 0)
        signal(row, xz * 2 + 1 - core)
        count += N_XZ
    if all_rows:
        def row_step(d, _):
            signal((row + d) % N_ROW, col)
            return 0
        lax.fori_loop(1, N_ROW, row_step, 0)
        count += N_ROW - 1
    pl.semaphore_wait(barrier, count)


def loop(low, high, step):
    lax.fori_loop(low, high, lambda i, _: (step(i), 0)[1], 0)


class Gather:
    def __init__(self, stage, whole, sems):
        self.stage, self.whole = stage, whole
        self.s1, self.r1, self.s2, self.r2, self.s3, self.r3 = sems
        self.row, self.col, self.xz, self.core = here()

    def first(self, d):
        to = (self.row + d) % N_ROW
        mine = self.stage.at[self.row]
        return remote(mine, mine, self.s1.at[d - 1], self.r1.at[d - 1], to, self.col)

    def second(self, d):
        to = (self.xz + d) % N_XZ
        mine = self.whole.at[self.core, self.xz]
        return remote(mine, mine, self.s2.at[d - 1], self.r2.at[d - 1], self.row, to * 2 + self.core)

    def third(self):
        mine = self.whole.at[self.core]
        return remote(mine, mine, self.s3, self.r3, self.row, self.xz * 2 + 1 - self.core)

    def first_arrived(self, d):
        at = self.stage.at[(self.row + N_ROW - d) % N_ROW]
        remote(at, at, self.s1.at[d - 1], self.r1.at[d - 1], self.row, self.col).wait_recv()

    def second_arrived(self, d):
        at = self.whole.at[self.core, (self.xz + N_XZ - d) % N_XZ]
        remote(at, at, self.s2.at[d - 1], self.r2.at[d - 1], self.row, self.col).wait_recv()

    def start(self, rows):
        self.stage[self.row] = rows
        loop(1, N_ROW, lambda d: self.first(d).start())

    def spread(self):
        loop(1, N_ROW, self.first_arrived)
        block = self.stage[...]
        self.whole[self.core, self.xz] = block.reshape(-1, block.shape[-1]).astype(BF16)
        loop(1, N_XZ, lambda d: self.second(d).start())

    def swap(self):
        loop(1, N_XZ, self.second_arrived)
        self.third().start()

    def finish(self):
        at = self.whole.at[1 - self.core]
        remote(at, at, self.s3, self.r3, self.row, self.col).wait_recv()
        loop(1, N_ROW, lambda d: self.first(d).wait_send())
        loop(1, N_XZ, lambda d: self.second(d).wait_send())
        self.third().wait_send()


def gather_sems():
    dma = pltpu.SemaphoreType.DMA
    return [dma((N_ROW - 1,)), dma((N_ROW - 1,)), dma((N_XZ - 1,)), dma((N_XZ - 1,)), dma, dma]


def fused_kernel(names, *refs):
    n = types.SimpleNamespace(**dict(zip(names, refs)))
    row, col, xz, core = here()
    place = core * N_XZ + xz
    y, high = row % 4, row // 4
    other_row = (1 - high) * 4 + y
    width = n.tok_mean.shape[-1]
    units = n.w_gate.shape[-1]
    capacity = n.rows.shape[2]
    slots = N_COL * capacity
    records = N_COL * 8
    batch = N_ROW * records

    def row_of(rel, step):
        return ((high + rel) % 2) * 4 + (y + step + 4) % 4

    def arrived(at, sem):
        remote(at, at, n.a_send.at[0], sem, row, col).wait_recv()

    greet(True, True)

    def meta_part(d):
        to = (place + d) % N_COL
        return remote(n.meta.at[to], n.table.at[place], n.m_send.at[d - 1], n.m_recv.at[d - 1], row, column_of(to))

    def part(d):
        to = (place + d) % N_COL
        return remote(
            n.rows.at[to], n.grid.at[:, place, row], n.a_send.at[d - 1], n.a_recv.at[place], row, column_of(to)
        )

    loop(1, N_COL, lambda d: meta_part(d).start())
    own = pltpu.make_async_copy(n.rows.at[place], n.grid.at[:, place, row], n.own_sem)
    own.start()
    loop(1, N_COL, lambda d: part(d).start())
    texts = Gather(n.t_stage, n.everyone, [n.ts1, n.tr1, n.ts2, n.tr2, n.ts3, n.tr3])
    texts.start(n.text[...])
    n.table[place] = n.meta[place]
    loop(1, N_COL, lambda d: arrived(n.table.at[(place + N_COL - d) % N_COL], n.m_recv.at[d - 1]))
    n.compact[row] = jnp.sum(n.table[...].reshape(N_COL // 4, 4, 8, 128), 1)

    def table_copy(d):
        at = n.compact.at[row]
        return remote(at, at, n.c_send.at[d - 1], n.c_recv.at[d - 1], (row + d) % N_ROW, col)

    loop(1, N_ROW, lambda d: table_copy(d).start())

    def piece(ref, group, at_row):
        return ref.at[:, pl.ds(group * PER_GROUP, PER_GROUP), at_row]

    def across(group):
        at = piece(n.grid, group, row)
        return remote(at, at, n.x_send.at[group], n.x_recv.at[group], other_row, col)

    def near(way, rel, group):
        at = piece(n.grid, group, row_of(rel, 0))
        step = 1 - 2 * way
        return remote(at, at, n.n_send.at[way, rel, group], n.n_recv.at[way, rel, group], row_of(0, step), col)

    def far(way, rel, half):
        step = 1 - 2 * way
        at = piece(n.grid, 2 * way + half, row_of(rel, -step))
        return remote(at, at, n.f_send.at[way, rel, half], n.f_recv.at[way, rel, half], row_of(0, step), col)

    def iota(shape, dim):
        return lax.broadcasted_iota(jnp.int32, shape, dim)

    def forward(r):
        def one(x):
            tile = n.compact[r]
            spread = jnp.broadcast_to(tile[:, None], (4, 4, 8, 128)).reshape(records, 128)
            at = (records, 128)
            spread = jnp.where(iota(at, 1) // 32 == (iota(at, 0) // 8) % 4, spread, 0.0).astype(BF16)
            at = (128, slots)
            pick = (iota(at, 0) % 32 == x * capacity + iota(at, 1) % capacity).astype(F32).astype(BF16)
            at = (records, slots)
            pool = jnp.dot(spread, pick, preferred_element_type=F32)
            pool = jnp.where(iota(at, 0) // 8 == iota(at, 1) // capacity, pool, 0.0).astype(BF16)
            at = (slots, 128)
            pick = (iota(at, 1) % 32 == x * capacity + iota(at, 0) % capacity).astype(F32).astype(BF16)
            at = (slots, records)
            turned = lax.dot_general(pick, spread, (((1,), (1,)), ((), ())), preferred_element_type=F32)
            n.turned[r, x] = jnp.where(iota(at, 1) // 8 == iota(at, 0) // capacity, turned, 0.0).astype(BF16)
            rows = n.grid[x, :, r].reshape(slots, width)
            gate_pre = jnp.dot(rows, n.w_gate[x], preferred_element_type=F32)
            up_pre = jnp.dot(rows, n.w_up[x], preferred_element_type=F32)
            sigma = jax.nn.sigmoid(gate_pre)
            silu_gate = gate_pre * sigma
            hidden = (silu_gate * up_pre).astype(BF16)
            shape = (N_COL, capacity, units)
            n.hidden[x, :, r] = hidden.reshape(shape)
            n.for_gate[x, :, r] = (up_pre * (sigma * (1.0 + gate_pre * (1.0 - sigma)))).astype(BF16).reshape(shape)
            n.for_up[x, :, r] = silu_gate.astype(BF16).reshape(shape)
            n.acc[x, :, r] = jnp.dot(pool, hidden, preferred_element_type=F32).reshape(N_COL, 8, units)
        loop(0, EXP_DEV, one)

    own.wait()
    for group in range(GROUPS):
        def one(i, group=group):
            from_place = group * PER_GROUP + i

            @pl.when(from_place != place)
            def _():
                arrived(n.grid.at[:, from_place, row], n.a_recv.at[from_place])
        loop(0, PER_GROUP, one)
        across(group).start()
        near(0, 0, group).start()
        near(1, 0, group).start()

    def neighbour(way, rel, group):
        step = 1 - 2 * way
        arrived(piece(n.grid, group, row_of(rel, -step)), n.n_recv.at[way, rel, group])
        if group // 2 == way:
            far(way, rel, group % 2).start()

    texts.spread()
    forward(row)
    loop(1, N_ROW, lambda d: arrived(n.compact.at[(row + N_ROW - d) % N_ROW], n.c_recv.at[d - 1]))
    for group in range(GROUPS):
        arrived(piece(n.grid, group, other_row), n.x_recv.at[group])
        near(0, 1, group).start()
        near(1, 1, group).start()
        neighbour(0, 0, group)
        neighbour(1, 0, group)
    texts.swap()
    forward(other_row)
    loop(0, 2, lambda way: forward(row_of(0, 2 * way - 1)))
    for group in range(GROUPS):
        neighbour(0, 1, group)
        neighbour(1, 1, group)
    loop(0, 2, lambda way: forward(row_of(1, 2 * way - 1)))
    for rel in range(2):
        for half in range(2):
            for way in range(2):
                arrived(piece(n.grid, 2 * way + half, row_of(rel, 2)), n.f_recv.at[way, rel, half])
        forward(row_of(rel, 2))

    def quarter(q):
        return n.hb[0, q], n.hb[1, q]

    def round_pooled(q):
        for x in range(EXP_DEV):
            n.hb[x, q] = n.acc[x, pl.ds(q * 4, 4)].reshape(-1, units).astype(BF16)

    def share(q):
        first, second = quarter(q)
        total = jnp.dot(first, n.w_down[0], preferred_element_type=F32) + jnp.dot(
            second, n.w_down[1], preferred_element_type=F32
        )
        n.part[q // 2, pl.ds((q % 2) * 4, 4)] = total.astype(BF16).reshape(4, -1, width)

    loop(0, 4, round_pooled)
    loop(0, 2, lambda i: share((1 - core) * 2 + i))
    swap = remote(n.part.at[1 - core], n.half, n.s1, n.r1, row, xz * 2 + 1 - core)
    swap.start()
    loop(0, 2, lambda i: share(core * 2 + i))
    swap.wait()

    def add(i):
        n.sums[i] = (n.part[core, i].astype(F32) + n.half[i].astype(F32)).astype(BF16)

    loop(0, N_XZ, add)

    def to_chip(d):
        to = (xz + d) % N_XZ
        return remote(n.sums.at[to], n.from_xz.at[d - 1], n.s2.at[d - 1], n.r2.at[d - 1], row, to * 2 + core)

    loop(1, N_XZ, lambda d: to_chip(d).start())
    loop(1, N_XZ, lambda d: to_chip(d).wait_recv())
    total = n.sums[xz].astype(F32)
    for d in range(N_XZ - 1):
        total = total + n.from_xz[d].astype(F32)
    n.sums_row[...] = total.reshape(n.sums_row.shape)

    def to_row(d):
        to = (row + d) % N_ROW
        return remote(n.sums_row.at[to], n.from_row.at[d - 1], n.s3.at[d - 1], n.r3.at[d - 1], to, col)

    loop(1, N_ROW, lambda d: to_row(d).start())
    texts.finish()
    loop(1, N_ROW, lambda d: to_row(d).wait_recv())
    total = n.sums_row[row]
    for d in range(N_ROW - 1):
        total = total + n.from_row[d]
    pooled = n.tok_mean[...] + total * (1.0 / SEQ)
    pooled_norm = jnp.sqrt(jnp.sum(pooled * pooled, -1, keepdims=True) + 1e-06)
    embed = pooled / pooled_norm
    embed_b = embed.astype(BF16)
    embeds = Gather(n.e_stage, n.e_whole, [n.es1, n.er1, n.es2, n.er2, n.es3, n.er3])
    grads = Gather(n.g_stage, n.grads, [n.gs1, n.gr1, n.gs2, n.gr2, n.gs3, n.gr3])
    embeds.start(embed_b.astype(F32))
    scale, shift, factor = n.scalars[0], n.scalars[1], n.scalars[2]
    at = (8, batch)
    same = (place * N_ROW + row) * 8 + iota(at, 0) == iota(at, 1)
    labels = jnp.where(same, 1.0, -1.0).astype(F32)

    def weigh(mine, others):
        logits = scale * lax.dot_general(mine, others, (((1,), (1,)), ((), ())), preferred_element_type=F32) + shift
        weights = (-factor * labels * jax.nn.sigmoid(-labels * logits)).astype(BF16)
        return jnp.dot(weights, others, preferred_element_type=F32)

    embed_grad = weigh(embed_b, n.everyone[...].reshape(batch, width))
    pooled_grad = (embed_grad - embed * jnp.sum(embed * embed_grad, -1, keepdims=True)) / pooled_norm
    out_grad = pooled_grad * (1.0 / SEQ)
    n.own_grad[...] = out_grad
    grads.start(out_grad)
    grads.spread()
    grads.swap()
    grads.finish()

    def through_down(q):
        block = n.grads[q // 2, pl.ds((q % 2) * 4, 4)].reshape(-1, width)
        for x in range(EXP_DEV):
            back = lax.dot_general(block, n.w_down[x], (((1,), (1,)), ((), ())), preferred_element_type=F32)
            n.acc[x, pl.ds(q * 4, 4)] = back.reshape(4, N_ROW, 8, units)

    def backward(r):
        n.q[r] = jnp.zeros(n.q.shape[1:], F32)

        def one(x):
            back = n.acc[x, :, r].reshape(records, units).astype(BF16)
            hidden_grad = jnp.dot(n.turned[r, x], back, preferred_element_type=F32)
            shape = (N_COL, capacity, units)
            hidden = n.hidden[x, :, r].reshape(slots, units).astype(F32)
            q = jnp.sum(hidden * hidden_grad, -1, keepdims=True)
            at = (slots, 128)
            q = jnp.where(iota(at, 1) == x * capacity + iota(at, 0) % capacity, q, 0.0)
            n.q[r] += jnp.sum(q.reshape(N_COL, capacity, 128), 1)
            gate_delta = (hidden_grad * n.for_gate[x, :, r].reshape(slots, units).astype(F32)).astype(BF16)
            up_delta = (hidden_grad * n.for_up[x, :, r].reshape(slots, units).astype(F32)).astype(BF16)
            n.for_gate[x, :, r] = gate_delta.reshape(shape)
            n.for_up[x, :, r] = up_delta.reshape(shape)
            dims = (((1,), (1,)), ((), ()))
            total = lax.dot_general(gate_delta, n.w_gate[x], dims, preferred_element_type=F32)
            total = total + lax.dot_general(up_delta, n.w_up[x], dims, preferred_element_type=F32)
            n.back[x, :, r] = total.astype(BF16).reshape(N_COL, capacity, width)
        loop(0, EXP_DEV, one)

    def far_back(way, rel, half):
        return remote(
            piece(n.back, 2 * way + half, row_of(rel, 2)), n.far_buf.at[way, rel, half],
            n.bf_send.at[way, rel, half], n.bf_recv.at[way, rel, half], row_of(0, 1 - 2 * way), col,
        )

    def near_back(way, rel, group):
        step = 1 - 2 * way
        mine = group // 2 == way
        src = n.far_buf.at[way, rel, group % 2] if mine else piece(n.back, group, row_of(rel, step))
        return remote(
            src, n.near_buf.at[way, rel, group],
            n.bn_send.at[way, rel, group], n.bn_recv.at[way, rel, group], row_of(0, step), col,
        )

    def across_back(group):
        return remote(
            n.near_buf.at[0, 1, group], n.x_buf.at[group], n.bx_send.at[group], n.bx_recv.at[group], other_row, col
        )

    def add_into(target, *terms):
        def one(k):
            x, i = k // PER_GROUP, k % PER_GROUP
            total = terms[0][x, i].astype(F32)
            for term in terms[1:]:
                total = total + term[x, i].astype(F32)
            target[x, i] = total.astype(BF16)
        loop(0, EXP_DEV * PER_GROUP, one)

    def q_row(d):
        to = (row + d) % N_ROW
        return remote(n.q.at[to], n.q_buf.at[d - 1], n.q1_send.at[d - 1], n.q1_recv.at[d - 1], to, col)

    loop(0, 4, through_down)
    for rel in (1, 0):
        backward(row_of(rel, 2))
        for half in range(2):
            for way in range(2):
                far_back(way, rel, half).start()
    for rel in (1, 0):
        loop(0, 2, lambda way, rel=rel: backward(row_of(rel, 1 - 2 * way)))
        for half in range(2):
            for way in range(2):
                near_back(way, rel, 2 * (1 - way) + half).start()
    backward(other_row)
    backward(row)
    loop(1, N_ROW, lambda d: q_row(d).start())
    embeds.spread()
    for rel in (1, 0):
        for half in range(2):
            for way in range(2):
                far_back(way, rel, half).wait_recv()
                at = n.far_buf.at[way, rel, half]
                add_into(at, at, piece(n.back, 2 * way + half, row_of(rel, 1 - 2 * way)))
                near_back(way, rel, 2 * way + half).start()
    loop(1, N_ROW, lambda d: q_row(d).wait_recv())
    total = n.q[row]
    for d in range(N_ROW - 1):
        total = total + n.q_buf[d]
    n.q_msg[...] = jnp.broadcast_to(total[:, None, :], n.q_msg.shape)
    n.q_in[place] = n.q_msg[place]

    def q_col(d):
        to = (place + d) % N_COL
        return remote(n.q_msg.at[to], n.q_in.at[place], n.q2_send.at[d - 1], n.q2_recv.at[d - 1], row, column_of(to))

    loop(1, N_COL, lambda d: q_col(d).start())
    embeds.swap()

    def weight_grads(x):
        dims = (((0,), (0,)), ((), ()))

        def one(t):
            at = pl.ds(pl.multiple_of(t * 256, 256), 256)
            rows = n.grid[x, :, :, :, at].reshape(-1, 256)
            n.gate_out[x, at] = lax.dot_general(
                rows, n.for_gate[x].reshape(-1, units), dims, preferred_element_type=F32
            )
            n.up_out[x, at] = lax.dot_general(
                rows, n.for_up[x].reshape(-1, units), dims, preferred_element_type=F32
            )
        loop(0, width // 256, one)
        pltpu.make_async_copy(n.gate_out.at[x], n.d_gate.at[x], n.out_sem.at[0, x]).start()
        pltpu.make_async_copy(n.up_out.at[x], n.d_up.at[x], n.out_sem.at[1, x]).start()

    weight_grads(0)
    loop(1, N_COL, lambda d: arrived(n.q_in.at[(place + N_COL - d) % N_COL], n.q2_recv.at[d - 1]))
    ids = n.ids[...]
    gates = n.gates[...]
    found = []
    for k in range(2):
        at = (ids.shape[0], N_COL)
        by_place = (iota(at, 1) == ids[:, k : k + 1]).astype(F32)
        lines = jnp.dot(by_place, n.q_in[:, 0, :], precision=lax.Precision.HIGHEST, preferred_element_type=F32)
        at = (ids.shape[0], 128)
        found.append(jnp.sum(jnp.where(iota(at, 1) == ids[:, 2 + k : 3 + k], lines, 0.0), -1, keepdims=True))
    both = found[0] + found[1]
    score_grad = jnp.zeros((ids.shape[0], 128), F32)
    for k in range(2):
        logit_grad = found[k] - gates[:, k : k + 1] * both
        score_grad = score_grad + jnp.where(iota(score_grad.shape, 1) == ids[:, 4 + k : 5 + k], logit_grad, 0.0)
    n.score_grad[...] = score_grad
    router_part = jnp.dot(
        score_grad.T[: EXP_DEV * N_COL], n.norm[...], precision=lax.Precision.HIGHEST, preferred_element_type=F32
    )
    for i in range(4):
        for j in range(2):
            n.dr[j * 4 + i] = router_part[i * 8 : i * 8 + 8, j * (width // 2) : (j + 1) * (width // 2)]

    def scatter(d):
        to = (row + d) % N_ROW
        return remote(n.dr.at[to], n.dr_in.at[row], n.d1_send.at[d - 1], n.d1_recv.at[d - 1], to, col)

    def tell_col(d):
        at = n.dr_sum.at[col]
        return remote(at, at, n.d2_send.at[d - 1], n.d2_recv.at[d - 1], row, (col + d) % N_COL)

    def tell_row(d):
        at = n.d_router.at[row]
        return remote(at, at, n.d3_send.at[d - 1], n.d3_recv.at[d - 1], (row + d) % N_ROW, col)

    loop(1, N_ROW, lambda d: scatter(d).start())
    n.dr_in[row] = n.dr[row]
    for group in (2, 0, 3, 1):
        for way in range(2):
            near_back(way, 1, group).wait_recv()
        at = n.near_buf.at[0, 1, group]
        add_into(at, at, n.near_buf.at[1, 1, group], piece(n.back, group, other_row))
        across_back(group).start()
    loop(1, N_ROW, lambda d: arrived(n.dr_in.at[(row + N_ROW - d) % N_ROW], n.d1_recv.at[d - 1]))
    n.dr_sum[col] = jnp.sum(n.dr_in[...], 0)
    loop(1, N_COL, lambda d: tell_col(d).start())
    weight_grads(1)

    def down_grads(x):
        def one(t):
            at = pl.ds(pl.multiple_of(t * 128, 128), 128)
            n.down_out[x, at] = lax.dot_general(
                n.hb[x, :, :, at].reshape(-1, 128), n.grads[...].reshape(batch, width),
                (((0,), (0,)), ((), ())), preferred_element_type=F32,
            )
        loop(0, units // 128, one)
        pltpu.make_async_copy(n.down_out.at[x], n.d_down.at[x], n.out_sem.at[2, x]).start()

    down_grads(0)
    down_grads(1)
    loop(1, N_COL, lambda d: arrived(n.dr_sum.at[(col + N_COL - d) % N_COL], n.d2_recv.at[d - 1]))
    n.d_router[row] = jnp.sum(n.dr_sum[...], 0)
    loop(1, N_ROW, lambda d: tell_row(d).start())
    embeds.finish()
    text_unit = n.text[...]
    text_grad = weigh(text_unit.astype(BF16), n.e_whole[...].reshape(batch, width))
    n.d_text[...] = (text_grad - text_unit * jnp.sum(text_unit * text_grad, -1, keepdims=True)) / n.text_norm[...]

    def home(group, i):
        to = group * PER_GROUP + i
        return remote(
            n.sum_buf.at[group, :, i], n.slots.at[place], n.h_send.at[to], n.h_recv.at[place], row, column_of(to)
        )

    def own_home(group, i):
        return pltpu.make_async_copy(n.sum_buf.at[group, :, i], n.slots.at[place], n.own_sem)

    for group in (2, 0, 3, 1):
        for way in range(2):
            near_back(way, 0, group).wait_recv()
        across_back(group).wait_recv()
        add_into(
            n.sum_buf.at[group], n.near_buf.at[0, 0, group], n.near_buf.at[1, 0, group], n.x_buf.at[group],
            piece(n.back, group, row),
        )

        def send(i, group=group):
            @pl.when(group * PER_GROUP + i != place)
            def _():
                home(group, i).start()

            @pl.when(group * PER_GROUP + i == place)
            def _():
                own_home(group, i).start()
        loop(0, PER_GROUP, send)

    loop(1, N_ROW, lambda d: arrived(n.d_router.at[(row + N_ROW - d) % N_ROW], n.d3_recv.at[d - 1]))
    loop(1, N_COL, lambda d: meta_part(d).wait_send())
    loop(1, N_COL, lambda d: part(d).wait_send())
    loop(1, N_COL, lambda d: q_col(d).wait_send())
    loop(1, N_COL, lambda d: tell_col(d).wait_send())
    loop(1, N_ROW, lambda d: table_copy(d).wait_send())
    loop(1, N_ROW, lambda d: to_row(d).wait_send())
    loop(1, N_ROW, lambda d: q_row(d).wait_send())
    loop(1, N_ROW, lambda d: scatter(d).wait_send())
    loop(1, N_ROW, lambda d: tell_row(d).wait_send())
    loop(1, N_XZ, lambda d: to_chip(d).wait_send())
    for group in range(GROUPS):
        across(group).wait_send()
        across_back(group).wait_send()
        for way in range(2):
            for rel in range(2):
                near(way, rel, group).wait_send()
                near_back(way, rel, group).wait_send()
    for rel in range(2):
        for half in range(2):
            for way in range(2):
                far(way, rel, half).wait_send()
                far_back(way, rel, half).wait_send()
    for x in range(EXP_DEV):
        pltpu.make_async_copy(n.gate_out.at[x], n.d_gate.at[x], n.out_sem.at[0, x]).wait()
        pltpu.make_async_copy(n.up_out.at[x], n.d_up.at[x], n.out_sem.at[1, x]).wait()
        pltpu.make_async_copy(n.down_out.at[x], n.d_down.at[x], n.out_sem.at[2, x]).wait()
    loop(1, N_COL, lambda d: arrived(n.slots.at[(place + N_COL - d) % N_COL], n.h_recv.at[(place + N_COL - d) % N_COL]))
    own_home(0, 0).wait()
    for group in range(GROUPS):
        def sent(i, group=group):
            @pl.when(group * PER_GROUP + i != place)
            def _():
                home(group, i).wait_send()
        loop(0, PER_GROUP, sent)


def fused(ins):
    width = ins["tok_mean"].shape[-1]
    units = ins["w_gate"].shape[-1]
    tok_count = ins["ids"].shape[0]
    capacity = ins["rows"].shape[2]
    slots, records = N_COL * capacity, N_COL * 8
    whole = (2, N_XZ, N_ROW * 8, width)
    block = (EXP_DEV, PER_GROUP, capacity, width)
    grid = (EXP_DEV, N_COL, N_ROW, capacity)
    outs = {
        "own_grad": ((8, width), F32, VMEM),
        "d_text": ((8, width), F32, VMEM),
        "slots": ((N_COL, EXP_DEV, capacity, width), BF16, VMEM),
        "score_grad": ((tok_count, 128), F32, VMEM),
        "d_router": ((N_ROW, 8, width // 2), F32, VMEM),
        "d_gate": (ins["w_gate"].shape, F32, ANY),
        "d_up": (ins["w_up"].shape, F32, ANY),
        "d_down": (ins["w_down"].shape, F32, ANY),
    }
    scratch = {
        "grid": (grid + (width,), BF16),
        "table": ((N_COL, 8, 128), F32),
        "compact": ((N_ROW, N_COL // 4, 8, 128), F32),
        "t_stage": ((N_ROW, 8, width), F32),
        "everyone": (whole, BF16),
        "turned": ((N_ROW, EXP_DEV, slots, records), BF16),
        "hidden": (grid + (units,), BF16),
        "for_gate": (grid + (units,), BF16),
        "for_up": (grid + (units,), BF16),
        "acc": ((EXP_DEV, N_COL, N_ROW, 8, units), F32),
        "hb": ((EXP_DEV, 4, N_ROW * records // 4, units), BF16),
        "part": (whole, BF16),
        "half": (whole[1:], BF16),
        "sums": (whole[1:], BF16),
        "from_xz": ((N_XZ - 1,) + whole[2:], BF16),
        "sums_row": ((N_ROW, 8, width), F32),
        "from_row": ((N_ROW - 1, 8, width), F32),
        "e_stage": ((N_ROW, 8, width), F32),
        "e_whole": (whole, BF16),
        "g_stage": ((N_ROW, 8, width), F32),
        "grads": (whole, BF16),
        "back": (grid + (width,), BF16),
        "far_buf": ((2, 2, 2) + block, BF16),
        "near_buf": ((2, 2, GROUPS) + block, BF16),
        "x_buf": ((GROUPS,) + block, BF16),
        "sum_buf": ((GROUPS,) + block, BF16),
        "q": ((N_ROW, N_COL, 128), F32),
        "q_buf": ((N_ROW - 1, N_COL, 128), F32),
        "q_msg": ((N_COL, 8, 128), F32),
        "q_in": ((N_COL, 8, 128), F32),
        "dr": ((N_ROW, 8, width // 2), F32),
        "dr_in": ((N_ROW, 8, width // 2), F32),
        "dr_sum": ((N_COL, 8, width // 2), F32),
        "gate_out": (ins["w_gate"].shape, F32),
        "up_out": (ins["w_up"].shape, F32),
        "down_out": (ins["w_down"].shape, F32),
    }
    row, col, chips = (N_ROW - 1,), (N_COL - 1,), (N_XZ - 1,)
    sems = {
        "own_sem": (), "out_sem": (3, EXP_DEV),
        "m_send": col, "m_recv": col, "a_send": col, "a_recv": (N_COL,), "c_send": row, "c_recv": row,
        "x_send": (GROUPS,), "x_recv": (GROUPS,), "n_send": (2, 2, GROUPS), "n_recv": (2, 2, GROUPS),
        "f_send": (2, 2, 2), "f_recv": (2, 2, 2),
        "s1": (), "r1": (), "s2": chips, "r2": chips, "s3": row, "r3": row,
        "bf_send": (2, 2, 2), "bf_recv": (2, 2, 2), "bn_send": (2, 2, GROUPS), "bn_recv": (2, 2, GROUPS),
        "bx_send": (GROUPS,), "bx_recv": (GROUPS,), "h_send": (N_COL,), "h_recv": (N_COL,),
        "q1_send": row, "q1_recv": row, "q2_send": col, "q2_recv": col,
        "d1_send": row, "d1_recv": row, "d2_send": col, "d2_recv": col, "d3_send": row, "d3_recv": row,
    }
    for letter in "teg":
        for kind in "sr":
            sems.update({letter + kind + "1": row, letter + kind + "2": chips, letter + kind + "3": ()})
    names = list(ins) + list(outs) + list(scratch) + list(sems)
    result = pl.pallas_call(
        functools.partial(fused_kernel, names),
        out_shape=tuple(jax.ShapeDtypeStruct(shape, dtype) for shape, dtype, _ in outs.values()),
        in_specs=[SMEM if name == "scalars" else VMEM for name in ins],
        out_specs=tuple(spec for _, _, spec in outs.values()),
        scratch_shapes=[pltpu.VMEM(shape, dtype) for shape, dtype in scratch.values()]
        + [pltpu.SemaphoreType.DMA(shape) for shape in sems.values()],
        compiler_params=pltpu.CompilerParams(
            collective_id=0, has_side_effects=True, vmem_limit_bytes=61 << 20
        ),
    )(*ins.values())
    return dict(zip(outs, result))


def body(tokens, expert_ids, text, w_gate, w_up, w_down, router, log_scale, bias, loss_scale):
    tok_count, width = tokens.shape
    samples = tok_count // SEQ
    experts = EXP_DEV * N_COL
    capacity = max(2, 4 * tok_count // experts)
    line = EXP_DEV * capacity
    batch = samples * N_ROW * N_COL
    token_wide = tokens.astype(F32)
    inverse_rms = lax.rsqrt(jnp.mean(token_wide * token_wide, -1, keepdims=True) + 1e-06)
    normed = token_wide * inverse_rms
    norm_in = normed.astype(BF16)
    norm_wide = norm_in.astype(F32)
    scores = jnp.dot(norm_wide, router, precision=lax.Precision.HIGHEST)
    choose = (expert_ids[:, :, None] == jnp.arange(experts, dtype=jnp.int32)[None, None, :]).astype(F32)
    chosen = jnp.sum(choose * scores[:, None, :], -1)
    gates = jax.nn.sigmoid(chosen - chosen[:, ::-1])
    member = jnp.sum(choose, 1)
    before = jnp.cumsum(member, 0) - member
    position = jnp.sum(choose * before[:, None, :], -1).astype(jnp.int32)
    to_place = place_of(expert_ids // EXP_DEV)
    in_line = (expert_ids % EXP_DEV) * capacity + position
    slot_index = to_place * line + in_line
    slot = jnp.arange(experts * capacity, dtype=jnp.int32)[:, None]
    hit0 = slot_index[:, 0][None, :] == slot
    hit1 = slot_index[:, 1][None, :] == slot
    both = (hit0 | hit1).astype(BF16)
    outgoing = jnp.dot(both, norm_in, preferred_element_type=F32).astype(BF16)
    slot_gate = jnp.sum(
        jnp.where(hit0, gates[:, 0][None, :], 0.0) + jnp.where(hit1, gates[:, 1][None, :], 0.0), -1
    )
    record = (jnp.arange(tok_count, dtype=jnp.int32) // SEQ)[None, :]
    slot_record = jnp.sum(jnp.where(hit0 | hit1, record, 0), -1)
    in_record = slot_record.reshape(N_COL, 1, line) == jnp.arange(samples, dtype=jnp.int32)[None, :, None]
    meta = jnp.where(in_record, slot_gate.reshape(N_COL, 1, line), 0.0)
    own_place = place_of(lax.axis_index("col"))
    mine = (jnp.arange(128, dtype=jnp.int32) // line == own_place % 4)[None, None, :]
    meta = jnp.where(mine, jnp.tile(meta, (1, 1, 128 // line)), 0.0)
    text_wide = text.astype(F32)
    text_norm = jnp.sqrt(jnp.sum(text_wide * text_wide, -1, keepdims=True) + 1e-06)
    scale = jnp.exp(log_scale[0])
    got = fused({
        "scalars": jnp.stack([scale, bias[0], loss_scale[0] * scale / batch]),
        "rows": outgoing.reshape(N_COL, EXP_DEV, capacity, width),
        "meta": meta,
        "text": text_wide / text_norm,
        "text_norm": text_norm,
        "tok_mean": jnp.mean(token_wide.reshape(samples, SEQ, width), 1),
        "w_gate": w_gate,
        "w_up": w_up,
        "w_down": w_down,
        "ids": jnp.concatenate([to_place, in_line, expert_ids, expert_ids], -1),
        "gates": gates,
        "norm": norm_wide,
    })
    input_sum = lax.dot_general(
        both, got["slots"].reshape(-1, width), (((0,), (0,)), ((), ())), preferred_element_type=F32
    )
    score_grad = got["score_grad"][:, :experts]
    out_grad = jnp.repeat(got["own_grad"], SEQ, axis=0)
    norm_grad = input_sum + jnp.dot(score_grad, router.T, precision=lax.Precision.HIGHEST)
    d_tokens = out_grad + inverse_rms * (norm_grad - normed * jnp.mean(norm_grad * normed, -1, keepdims=True))
    d_router = got["d_router"].reshape(2, experts, width // 2).transpose(0, 2, 1).reshape(width, experts)
    return (got["d_text"], d_tokens, got["d_gate"], got["d_up"], got["d_down"], d_router)


def solution(mesh):
    in_specs = (
        P(("row", "col"), None),
        P(("row", "col"), None),
        P(("row", "col"), None),
        P("col", None, "row"),
        P("col", None, "row"),
        P("col", "row", None),
        P(),
        P(),
        P(),
        P(),
    )
    out_specs = (
        P(("row", "col"), None),
        P(("row", "col"), None),
        P("col", None, "row"),
        P("col", None, "row"),
        P("col", "row", None),
        P(),
    )
    return jax.shard_map(body, mesh=mesh, in_specs=in_specs, out_specs=out_specs, check_vma=False)
```

```python
import functools
import types

import jax
import jax.numpy as jnp
from jax import lax
from jax.experimental import pallas as pl
from jax.experimental.pallas import tpu as pltpu
from jax.sharding import PartitionSpec as P

EXP_DEV = 2
SEQ = 16
F32 = jnp.float32
BF16 = jnp.bfloat16
MESH = pl.DeviceIdType.MESH
VMEM = pl.BlockSpec(memory_space=pltpu.VMEM)
SMEM = pl.BlockSpec(memory_space=pltpu.SMEM)
ANY = pl.BlockSpec(memory_space=pl.ANY)
N_ROW, N_COL, N_XZ = 8, 16, 8
GROUPS, PER_GROUP = 4, 4


def column_of(place):
    return (place % N_XZ) * 2 + place // N_XZ


def place_of(column):
    return (column % 2) * N_XZ + column // 2


def remote(src, dst, send_sem, recv_sem, row, col):
    return pltpu.make_async_remote_copy(
        src_ref=src, dst_ref=dst, send_sem=send_sem, recv_sem=recv_sem,
        device_id={"row": row, "col": col}, device_id_type=MESH,
    )


def here():
    row, col = lax.axis_index("row"), lax.axis_index("col")
    return row, col, col // 2, col % 2


def greet(all_columns, all_rows):
    row, col, xz, core = here()
    barrier = pltpu.get_barrier_semaphore()

    def signal(r, c):
        pl.semaphore_signal(barrier, inc=1, device_id={"row": r, "col": c}, device_id_type=MESH)

    count = 0
    if all_columns:
        def col_step(d, _):
            signal(row, (col + d) % N_COL)
            return 0
        lax.fori_loop(1, N_COL, col_step, 0)
        count += N_COL - 1
    else:
        def xz_step(d, _):
            signal(row, ((xz + d) % N_XZ) * 2 + core)
            return 0
        lax.fori_loop(1, N_XZ, xz_step, 0)
        signal(row, xz * 2 + 1 - core)
        count += N_XZ
    if all_rows:
        def row_step(d, _):
            signal((row + d) % N_ROW, col)
            return 0
        lax.fori_loop(1, N_ROW, row_step, 0)
        count += N_ROW - 1
    return count


def all_here(count):
    pl.semaphore_wait(pltpu.get_barrier_semaphore(), count)


def loop(low, high, step):
    lax.fori_loop(low, high, lambda i, _: (step(i), 0)[1], 0)


class Gather:
    def __init__(self, begin, stage, whole, sems):
        self.begin, self.stage, self.whole = begin, stage, whole
        self.s1, self.r1, self.s2, self.r2, self.s3, self.r3 = sems
        self.row, self.col, self.xz, self.core = here()

    def first(self, d):
        to = (self.row + d) % N_ROW
        mine = self.stage.at[self.row]
        return remote(mine, mine, self.s1.at[d - 1], self.r1.at[d - 1], to, self.col)

    def second(self, d):
        to = (self.xz + d) % N_XZ
        mine = self.whole.at[self.core, self.xz]
        return remote(mine, mine, self.s2.at[d - 1], self.r2.at[d - 1], self.row, to * 2 + self.core)

    def third(self):
        mine = self.whole.at[self.core]
        return remote(mine, mine, self.s3, self.r3, self.row, self.xz * 2 + 1 - self.core)

    def first_arrived(self, d):
        at = self.stage.at[(self.row + N_ROW - d) % N_ROW]
        remote(at, at, self.s1.at[d - 1], self.r1.at[d - 1], self.row, self.col).wait_recv()

    def second_arrived(self, d):
        at = self.whole.at[self.core, (self.xz + N_XZ - d) % N_XZ]
        remote(at, at, self.s2.at[d - 1], self.r2.at[d - 1], self.row, self.col).wait_recv()

    def start(self, rows):
        self.stage[self.row] = rows
        self.begin(N_ROW, self.first)

    def spread(self):
        loop(1, N_ROW, self.first_arrived)
        block = self.stage[...]
        self.whole[self.core, self.xz] = block.reshape(-1, block.shape[-1]).astype(BF16)
        self.begin(N_XZ, self.second)

    def swap(self):
        loop(1, N_XZ, self.second_arrived)
        self.begin(2, lambda d: self.third())

    def finish(self):
        at = self.whole.at[1 - self.core]
        remote(at, at, self.s3, self.r3, self.row, self.col).wait_recv()


def gather_sems():
    dma = pltpu.SemaphoreType.DMA
    return [dma((N_ROW - 1,)), dma((N_ROW - 1,)), dma((N_XZ - 1,)), dma((N_XZ - 1,)), dma, dma]


def fused_kernel(names, *refs):
    n = types.SimpleNamespace(**dict(zip(names, refs)))
    row, col, xz, core = here()
    place = core * N_XZ + xz
    y, high = row % 4, row // 4
    other_row = (1 - high) * 4 + y
    width = n.tokens.shape[-1]
    units = n.w_gate.shape[-1]
    capacity = n.grid.shape[3]
    slots = N_COL * capacity
    records = N_COL * 8
    batch = N_ROW * records

    def row_of(rel, step):
        return ((high + rel) % 2) * 4 + (y + step + 4) % 4

    def arrived(at, sem):
        remote(at, at, n.a_send.at[0], sem, row, col).wait_recv()

    pending = []

    def begin(count, make):
        loop(1, count, lambda d: make(d).start())
        pending.append(lambda: loop(1, count, lambda d: make(d).wait_send()))

    def launch(make, *where):
        make(*where).start()
        pending.append(lambda: make(*where).wait_send())

    def iota(shape, dim):
        return lax.broadcasted_iota(jnp.int32, shape, dim)

    def exact(left, right, dims):
        return lax.dot_general(
            left, right, (dims, ((), ())), precision=lax.Precision.HIGHEST, preferred_element_type=F32
        )

    def fast(left, right, dims):
        return lax.dot_general(left, right, (dims, ((), ())), preferred_element_type=F32)

    def one_hot(at, lanes):
        return (iota((at.shape[0], lanes), 1) == at).astype(F32)

    greeted = greet(True, True)

    tokens = n.tokens[...].astype(F32)
    tok_count = tokens.shape[0]
    inverse_rms = lax.rsqrt(jnp.mean(tokens * tokens, -1, keepdims=True) + 1e-06)
    norm_in = (tokens * inverse_rms).astype(BF16)
    scores = exact(norm_in.astype(F32), n.router[...], ((1,), (0,)))
    experts = scores.shape[-1]
    ids = [n.ids[:, k : k + 1] for k in range(2)]
    choose = [one_hot(ids[k], experts) for k in range(2)]
    chosen = [jnp.sum(choose[k] * scores, -1, keepdims=True) for k in range(2)]
    gates = [jax.nn.sigmoid(chosen[k] - chosen[1 - k]) for k in range(2)]
    earlier = (iota((tok_count, tok_count), 0) > iota((tok_count, tok_count), 1)).astype(F32).astype(BF16)
    before = fast(earlier, (choose[0] + choose[1]).astype(BF16), ((1,), (0,)))
    to_place, in_line, hits = [], [], []
    meta = jnp.zeros((N_COL * 8, 128), F32)
    for k in range(2):
        position = jnp.sum(choose[k] * before, -1, keepdims=True).astype(jnp.int32)
        column = ids[k] >> 1
        to_place.append((column & 1) * N_XZ + (column >> 1))
        in_line.append((ids[k] & 1) * capacity + position)
        hits.append(one_hot(to_place[k] * (EXP_DEV * capacity) + in_line[k], N_COL * EXP_DEV * capacity))
        by_record = one_hot(to_place[k] * 8 + (iota((tok_count, 1), 0) >> 4), N_COL * 8) * gates[k]
        by_line = one_hot((place % 4) * (EXP_DEV * capacity) + in_line[k], 128)
        meta = meta + fast(by_record.astype(BF16), by_line.astype(BF16), ((0,), (0,)))
    hit = (hits[0] + hits[1]).astype(BF16)
    n.meta[...] = meta.reshape(N_COL, 8, 128)
    n.rows[...] = fast(hit, norm_in, ((0,), (0,))).astype(BF16).reshape(n.rows.shape)
    text = n.text[...].astype(F32)
    text_norm = jnp.sqrt(jnp.sum(text * text, -1, keepdims=True) + 1e-06)
    text_unit = text / text_norm
    scale = jnp.exp(jnp.full((8, 128), n.log_scale[0], F32))[:1, :1]
    shift = n.bias[0]
    factor = n.loss_scale[0] * scale * (1.0 / batch)
    all_here(greeted)

    def meta_part(d):
        to = (place + d) % N_COL
        return remote(n.meta.at[to], n.table.at[place], n.m_send.at[d - 1], n.m_recv.at[d - 1], row, column_of(to))

    def part(d):
        to = (place + d) % N_COL
        return remote(
            n.rows.at[to], n.grid.at[:, place, row], n.a_send.at[d - 1], n.a_recv.at[place], row, column_of(to)
        )

    begin(N_COL, meta_part)
    own = pltpu.make_async_copy(n.rows.at[place], n.grid.at[:, place, row], n.own_sem)
    own.start()
    begin(N_COL, part)
    texts = Gather(begin, n.t_stage, n.everyone, [n.ts1, n.tr1, n.ts2, n.tr2, n.ts3, n.tr3])
    texts.start(text_unit)
    n.table[place] = n.meta[place]
    loop(1, N_COL, lambda d: arrived(n.table.at[(place + N_COL - d) % N_COL], n.m_recv.at[d - 1]))
    n.compact[row] = jnp.sum(n.table[...].reshape(N_COL // 4, 4, 8, 128), 1)

    def table_copy(d):
        at = n.compact.at[row]
        return remote(at, at, n.c_send.at[d - 1], n.c_recv.at[d - 1], (row + d) % N_ROW, col)

    begin(N_ROW, table_copy)

    def piece(ref, group, at_row):
        return ref.at[:, pl.ds(group * PER_GROUP, PER_GROUP), at_row]

    def across(group):
        at = piece(n.grid, group, row)
        return remote(at, at, n.x_send.at[group], n.x_recv.at[group], other_row, col)

    def near(way, rel, group):
        at = piece(n.grid, group, row_of(rel, 0))
        step = 1 - 2 * way
        return remote(at, at, n.n_send.at[way, rel, group], n.n_recv.at[way, rel, group], row_of(0, step), col)

    def far(way, rel, half):
        step = 1 - 2 * way
        at = piece(n.grid, 2 * way + half, row_of(rel, -step))
        return remote(at, at, n.f_send.at[way, rel, half], n.f_recv.at[way, rel, half], row_of(0, step), col)

    def forward(r):
        def one(x):
            tile = n.compact[r]
            spread = jnp.broadcast_to(tile[:, None], (4, 4, 8, 128)).reshape(records, 128)
            at = (records, 128)
            spread = jnp.where(iota(at, 1) // 32 == (iota(at, 0) // 8) % 4, spread, 0.0).astype(BF16)
            at = (128, slots)
            pick = (iota(at, 0) % 32 == x * capacity + iota(at, 1) % capacity).astype(F32).astype(BF16)
            at = (records, slots)
            pool = jnp.dot(spread, pick, preferred_element_type=F32)
            pool = jnp.where(iota(at, 0) // 8 == iota(at, 1) // capacity, pool, 0.0).astype(BF16)
            at = (slots, 128)
            pick = (iota(at, 1) % 32 == x * capacity + iota(at, 0) % capacity).astype(F32).astype(BF16)
            at = (slots, records)
            turned = lax.dot_general(pick, spread, (((1,), (1,)), ((), ())), preferred_element_type=F32)
            n.turned[r, x] = jnp.where(iota(at, 1) // 8 == iota(at, 0) // capacity, turned, 0.0).astype(BF16)
            rows = n.grid[x, :, r].reshape(slots, width)
            gate_pre = jnp.dot(rows, n.w_gate[x], preferred_element_type=F32)
            up_pre = jnp.dot(rows, n.w_up[x], preferred_element_type=F32)
            sigma = jax.nn.sigmoid(gate_pre)
            silu_gate = gate_pre * sigma
            hidden = (silu_gate * up_pre).astype(BF16)
            shape = (N_COL, capacity, units)
            n.hidden[x, :, r] = hidden.reshape(shape)
            n.for_gate[x, :, r] = (up_pre * (sigma * (1.0 + gate_pre * (1.0 - sigma)))).astype(BF16).reshape(shape)
            n.for_up[x, :, r] = silu_gate.astype(BF16).reshape(shape)
            n.acc[x, :, r] = jnp.dot(pool, hidden, preferred_element_type=F32).reshape(N_COL, 8, units)
        loop(0, EXP_DEV, one)

    own.wait()
    for group in range(GROUPS):
        def one(i, group=group):
            from_place = group * PER_GROUP + i

            @pl.when(from_place != place)
            def _():
                arrived(n.grid.at[:, from_place, row], n.a_recv.at[from_place])
        loop(0, PER_GROUP, one)
        launch(across, group)
        launch(near, 0, 0, group)
        launch(near, 1, 0, group)

    def neighbour(way, rel, group):
        step = 1 - 2 * way
        arrived(piece(n.grid, group, row_of(rel, -step)), n.n_recv.at[way, rel, group])
        if group // 2 == way:
            launch(far, way, rel, group % 2)

    texts.spread()
    forward(row)
    loop(1, N_ROW, lambda d: arrived(n.compact.at[(row + N_ROW - d) % N_ROW], n.c_recv.at[d - 1]))
    for group in range(GROUPS):
        arrived(piece(n.grid, group, other_row), n.x_recv.at[group])
        launch(near, 0, 1, group)
        launch(near, 1, 1, group)
        neighbour(0, 0, group)
        neighbour(1, 0, group)
    texts.swap()
    forward(other_row)
    loop(0, 2, lambda way: forward(row_of(0, 2 * way - 1)))
    for group in range(GROUPS):
        neighbour(0, 1, group)
        neighbour(1, 1, group)
    loop(0, 2, lambda way: forward(row_of(1, 2 * way - 1)))
    for rel in range(2):
        for half in range(2):
            for way in range(2):
                arrived(piece(n.grid, 2 * way + half, row_of(rel, 2)), n.f_recv.at[way, rel, half])
        forward(row_of(rel, 2))

    def quarter(q):
        return n.hb[0, q], n.hb[1, q]

    def round_pooled(q):
        for x in range(EXP_DEV):
            n.hb[x, q] = n.acc[x, pl.ds(q * 4, 4)].reshape(-1, units).astype(BF16)

    def share(q):
        first, second = quarter(q)
        total = jnp.dot(first, n.w_down[0], preferred_element_type=F32) + jnp.dot(
            second, n.w_down[1], preferred_element_type=F32
        )
        n.part[q // 2, pl.ds((q % 2) * 4, 4)] = total.astype(BF16).reshape(4, -1, width)

    loop(0, 4, round_pooled)
    loop(0, 2, lambda i: share((1 - core) * 2 + i))
    swap = remote(n.part.at[1 - core], n.half, n.s1, n.r1, row, xz * 2 + 1 - core)
    swap.start()
    loop(0, 2, lambda i: share(core * 2 + i))
    swap.wait()

    def add(i):
        n.sums[i] = (n.part[core, i].astype(F32) + n.half[i].astype(F32)).astype(BF16)

    loop(0, N_XZ, add)

    def to_chip(d):
        to = (xz + d) % N_XZ
        return remote(n.sums.at[to], n.from_xz.at[d - 1], n.s2.at[d - 1], n.r2.at[d - 1], row, to * 2 + core)

    begin(N_XZ, to_chip)
    loop(1, N_XZ, lambda d: to_chip(d).wait_recv())
    total = n.sums[xz].astype(F32)
    for d in range(N_XZ - 1):
        total = total + n.from_xz[d].astype(F32)
    n.sums_row[...] = total.reshape(n.sums_row.shape)

    def to_row(d):
        to = (row + d) % N_ROW
        return remote(n.sums_row.at[to], n.from_row.at[d - 1], n.s3.at[d - 1], n.r3.at[d - 1], to, col)

    begin(N_ROW, to_row)
    texts.finish()
    loop(1, N_ROW, lambda d: to_row(d).wait_recv())
    total = n.sums_row[row]
    for d in range(N_ROW - 1):
        total = total + n.from_row[d]
    tok_mean = jnp.mean(n.tokens[...].astype(F32).reshape(-1, SEQ, width), 1)
    pooled = tok_mean + total * (1.0 / SEQ)
    pooled_norm = jnp.sqrt(jnp.sum(pooled * pooled, -1, keepdims=True) + 1e-06)
    embed = pooled / pooled_norm
    embed_b = embed.astype(BF16)
    embeds = Gather(begin, n.e_stage, n.e_whole, [n.es1, n.er1, n.es2, n.er2, n.es3, n.er3])
    grads = Gather(begin, n.g_stage, n.grads, [n.gs1, n.gr1, n.gs2, n.gr2, n.gs3, n.gr3])
    embeds.start(embed_b.astype(F32))
    at = (8, batch)
    same = (place * N_ROW + row) * 8 + iota(at, 0) == iota(at, 1)
    labels = jnp.where(same, 1.0, -1.0).astype(F32)

    def weigh(mine, others):
        logits = scale * lax.dot_general(mine, others, (((1,), (1,)), ((), ())), preferred_element_type=F32) + shift
        weights = (-factor * labels * jax.nn.sigmoid(-labels * logits)).astype(BF16)
        return jnp.dot(weights, others, preferred_element_type=F32)

    embed_grad = weigh(embed_b, n.everyone[...].reshape(batch, width))
    pooled_grad = (embed_grad - embed * jnp.sum(embed * embed_grad, -1, keepdims=True)) / pooled_norm
    out_grad = pooled_grad * (1.0 / SEQ)
    n.own_grad[...] = out_grad
    grads.start(out_grad)
    grads.spread()
    grads.swap()
    grads.finish()

    def through_down(q):
        block = n.grads[q // 2, pl.ds((q % 2) * 4, 4)].reshape(-1, width)
        for x in range(EXP_DEV):
            back = lax.dot_general(block, n.w_down[x], (((1,), (1,)), ((), ())), preferred_element_type=F32)
            n.acc[x, pl.ds(q * 4, 4)] = back.reshape(4, N_ROW, 8, units)

    def backward(r):
        n.q[r] = jnp.zeros(n.q.shape[1:], F32)

        def one(x):
            back = n.acc[x, :, r].reshape(records, units).astype(BF16)
            hidden_grad = jnp.dot(n.turned[r, x], back, preferred_element_type=F32)
            shape = (N_COL, capacity, units)
            hidden = n.hidden[x, :, r].reshape(slots, units).astype(F32)
            q = jnp.sum(hidden * hidden_grad, -1, keepdims=True)
            at = (slots, 128)
            q = jnp.where(iota(at, 1) == x * capacity + iota(at, 0) % capacity, q, 0.0)
            n.q[r] += jnp.sum(q.reshape(N_COL, capacity, 128), 1)
            gate_delta = (hidden_grad * n.for_gate[x, :, r].reshape(slots, units).astype(F32)).astype(BF16)
            up_delta = (hidden_grad * n.for_up[x, :, r].reshape(slots, units).astype(F32)).astype(BF16)
            n.for_gate[x, :, r] = gate_delta.reshape(shape)
            n.for_up[x, :, r] = up_delta.reshape(shape)
            dims = (((1,), (1,)), ((), ()))
            total = lax.dot_general(gate_delta, n.w_gate[x], dims, preferred_element_type=F32)
            total = total + lax.dot_general(up_delta, n.w_up[x], dims, preferred_element_type=F32)
            n.back[x, :, r] = total.astype(BF16).reshape(N_COL, capacity, width)
        loop(0, EXP_DEV, one)

    def far_back(way, rel, half):
        return remote(
            piece(n.back, 2 * way + half, row_of(rel, 2)), n.far_buf.at[way, rel, half],
            n.bf_send.at[way, rel, half], n.bf_recv.at[way, rel, half], row_of(0, 1 - 2 * way), col,
        )

    def near_back(way, rel, group):
        step = 1 - 2 * way
        mine = group // 2 == way
        src = n.far_buf.at[way, rel, group % 2] if mine else piece(n.back, group, row_of(rel, step))
        return remote(
            src, n.near_buf.at[way, rel, group],
            n.bn_send.at[way, rel, group], n.bn_recv.at[way, rel, group], row_of(0, step), col,
        )

    def across_back(group):
        return remote(
            n.near_buf.at[0, 1, group], n.x_buf.at[group], n.bx_send.at[group], n.bx_recv.at[group], other_row, col
        )

    def add_into(target, *terms):
        def one(k):
            x, i = k // PER_GROUP, k % PER_GROUP
            total = terms[0][x, i].astype(F32)
            for term in terms[1:]:
                total = total + term[x, i].astype(F32)
            target[x, i] = total.astype(BF16)
        loop(0, EXP_DEV * PER_GROUP, one)

    def q_row(d):
        to = (row + d) % N_ROW
        return remote(n.q.at[to], n.q_buf.at[d - 1], n.q1_send.at[d - 1], n.q1_recv.at[d - 1], to, col)

    loop(0, 4, through_down)
    for rel in (1, 0):
        backward(row_of(rel, 2))
        for half in range(2):
            for way in range(2):
                launch(far_back, way, rel, half)
    for rel in (1, 0):
        loop(0, 2, lambda way, rel=rel: backward(row_of(rel, 1 - 2 * way)))
        for half in range(2):
            for way in range(2):
                launch(near_back, way, rel, 2 * (1 - way) + half)
    backward(other_row)
    backward(row)
    begin(N_ROW, q_row)
    embeds.spread()
    for rel in (1, 0):
        for half in range(2):
            for way in range(2):
                far_back(way, rel, half).wait_recv()
                at = n.far_buf.at[way, rel, half]
                add_into(at, at, piece(n.back, 2 * way + half, row_of(rel, 1 - 2 * way)))
                launch(near_back, way, rel, 2 * way + half)
    loop(1, N_ROW, lambda d: q_row(d).wait_recv())
    total = n.q[row]
    for d in range(N_ROW - 1):
        total = total + n.q_buf[d]
    n.q_msg[...] = jnp.broadcast_to(total[:, None, :], n.q_msg.shape)
    n.q_in[place] = n.q_msg[place]

    def q_col(d):
        to = (place + d) % N_COL
        return remote(n.q_msg.at[to], n.q_in.at[place], n.q2_send.at[d - 1], n.q2_recv.at[d - 1], row, column_of(to))

    begin(N_COL, q_col)
    embeds.swap()

    def weight_grads(x):
        dims = (((0,), (0,)), ((), ()))

        def one(t):
            at = pl.ds(pl.multiple_of(t * 256, 256), 256)
            rows = n.grid[x, :, :, :, at].reshape(-1, 256)
            n.gate_out[x, at] = lax.dot_general(
                rows, n.for_gate[x].reshape(-1, units), dims, preferred_element_type=F32
            )
            n.up_out[x, at] = lax.dot_general(
                rows, n.for_up[x].reshape(-1, units), dims, preferred_element_type=F32
            )
        loop(0, width // 256, one)
        pltpu.make_async_copy(n.gate_out.at[x], n.d_gate.at[x], n.out_sem.at[0, x]).start()
        pltpu.make_async_copy(n.up_out.at[x], n.d_up.at[x], n.out_sem.at[1, x]).start()

    weight_grads(0)
    loop(1, N_COL, lambda d: arrived(n.q_in.at[(place + N_COL - d) % N_COL], n.q2_recv.at[d - 1]))
    found = []
    for k in range(2):
        lines = exact(one_hot(to_place[k], N_COL), n.q_in[:, 0, :], ((1,), (0,)))
        found.append(jnp.sum(one_hot(in_line[k], 128) * lines, -1, keepdims=True))
    both = found[0] + found[1]
    score_grad = jnp.zeros((tok_count, 128), F32)
    for k in range(2):
        score_grad = score_grad + one_hot(ids[k], 128) * (found[k] - gates[k] * both)
    router_part = exact(score_grad.T[:experts], norm_in.astype(F32), ((1,), (0,)))
    for i in range(4):
        for j in range(2):
            n.dr[j * 4 + i] = router_part[i * 8 : i * 8 + 8, j * (width // 2) : (j + 1) * (width // 2)]

    def scatter(d):
        to = (row + d) % N_ROW
        return remote(n.dr.at[to], n.dr_in.at[row], n.d1_send.at[d - 1], n.d1_recv.at[d - 1], to, col)

    def tell_col(d):
        at = n.dr_sum.at[col]
        return remote(at, at, n.d2_send.at[d - 1], n.d2_recv.at[d - 1], row, (col + d) % N_COL)

    def tell_row(d):
        at = n.dr_out.at[row]
        return remote(at, at, n.d3_send.at[d - 1], n.d3_recv.at[d - 1], (row + d) % N_ROW, col)

    begin(N_ROW, scatter)
    n.dr_in[row] = n.dr[row]
    for group in (2, 0, 3, 1):
        for way in range(2):
            near_back(way, 1, group).wait_recv()
        at = n.near_buf.at[0, 1, group]
        add_into(at, at, n.near_buf.at[1, 1, group], piece(n.back, group, other_row))
        launch(across_back, group)
    loop(1, N_ROW, lambda d: arrived(n.dr_in.at[(row + N_ROW - d) % N_ROW], n.d1_recv.at[d - 1]))
    n.dr_sum[col] = jnp.sum(n.dr_in[...], 0)
    begin(N_COL, tell_col)
    weight_grads(1)

    def down_grads(x):
        def one(t):
            at = pl.ds(pl.multiple_of(t * 128, 128), 128)
            n.down_out[x, at] = lax.dot_general(
                n.hb[x, :, :, at].reshape(-1, 128), n.grads[...].reshape(batch, width),
                (((0,), (0,)), ((), ())), preferred_element_type=F32,
            )
        loop(0, units // 128, one)
        pltpu.make_async_copy(n.down_out.at[x], n.d_down.at[x], n.out_sem.at[2, x]).start()

    down_grads(0)
    down_grads(1)
    loop(1, N_COL, lambda d: arrived(n.dr_sum.at[(col + N_COL - d) % N_COL], n.d2_recv.at[d - 1]))
    n.dr_out[row] = jnp.sum(n.dr_sum[...], 0)
    begin(N_ROW, tell_row)
    embeds.finish()
    text_grad = weigh(text_unit.astype(BF16), n.e_whole[...].reshape(batch, width))
    n.d_text[...] = (text_grad - text_unit * jnp.sum(text_unit * text_grad, -1, keepdims=True)) / text_norm

    def home(group, i):
        to = group * PER_GROUP + i
        return remote(
            n.sum_buf.at[group, :, i], n.slots.at[place], n.h_send.at[to], n.h_recv.at[place], row, column_of(to)
        )

    def own_home(group, i):
        return pltpu.make_async_copy(n.sum_buf.at[group, :, i], n.slots.at[place], n.own_sem)

    for group in (2, 0, 3, 1):
        for way in range(2):
            near_back(way, 0, group).wait_recv()
        across_back(group).wait_recv()
        add_into(
            n.sum_buf.at[group], n.near_buf.at[0, 0, group], n.near_buf.at[1, 0, group], n.x_buf.at[group],
            piece(n.back, group, row),
        )

        def send(i, group=group):
            @pl.when(group * PER_GROUP + i != place)
            def _():
                home(group, i).start()

            @pl.when(group * PER_GROUP + i == place)
            def _():
                own_home(group, i).start()
        loop(0, PER_GROUP, send)

    loop(1, N_ROW, lambda d: arrived(n.dr_out.at[(row + N_ROW - d) % N_ROW], n.d3_recv.at[d - 1]))
    for wait in pending:
        wait()
    for x in range(EXP_DEV):
        pltpu.make_async_copy(n.gate_out.at[x], n.d_gate.at[x], n.out_sem.at[0, x]).wait()
        pltpu.make_async_copy(n.up_out.at[x], n.d_up.at[x], n.out_sem.at[1, x]).wait()
        pltpu.make_async_copy(n.down_out.at[x], n.d_down.at[x], n.out_sem.at[2, x]).wait()
    loop(1, N_COL, lambda d: arrived(n.slots.at[(place + N_COL - d) % N_COL], n.h_recv.at[(place + N_COL - d) % N_COL]))
    own_home(0, 0).wait()
    for group in range(GROUPS):
        def sent(i, group=group):
            @pl.when(group * PER_GROUP + i != place)
            def _():
                home(group, i).wait_send()
        loop(0, PER_GROUP, sent)
    for j in range(2):
        block = n.dr_out[pl.ds(j * 4, 4)].reshape(experts, width // 2)
        block = jnp.concatenate([block, jnp.zeros((128 - experts, width // 2), F32)], 0)
        n.d_router[pl.ds(j * (width // 2), width // 2), :] = block.T[:, :experts]
    input_sum = fast(hit, n.slots[...].reshape(-1, width), ((1,), (0,)))
    norm_grad = input_sum + exact(score_grad[:, :experts], n.router[...], ((1,), (1,)))
    normed = n.tokens[...].astype(F32) * inverse_rms
    out_grad = jnp.broadcast_to(n.own_grad[...][:, None, :], (8, SEQ, width)).reshape(tok_count, width)
    n.d_tokens[...] = out_grad + inverse_rms * (
        norm_grad - normed * jnp.mean(norm_grad * normed, -1, keepdims=True)
    )


def fused(ins):
    tok_count, width = ins["tokens"].shape
    units = ins["w_gate"].shape[-1]
    experts = EXP_DEV * N_COL
    capacity = max(2, 4 * tok_count // experts)
    slots, records = N_COL * capacity, N_COL * 8
    whole = (2, N_XZ, N_ROW * 8, width)
    block = (EXP_DEV, PER_GROUP, capacity, width)
    grid = (EXP_DEV, N_COL, N_ROW, capacity)
    outs = {
        "d_text": ((8, width), F32, VMEM),
        "d_tokens": ((tok_count, width), F32, VMEM),
        "d_gate": (ins["w_gate"].shape, F32, ANY),
        "d_up": (ins["w_up"].shape, F32, ANY),
        "d_down": (ins["w_down"].shape, F32, ANY),
        "d_router": (ins["router"].shape, F32, VMEM),
    }
    scratch = {
        "rows": ((N_COL, EXP_DEV, capacity, width), BF16),
        "meta": ((N_COL, 8, 128), F32),
        "own_grad": ((8, width), F32),
        "slots": ((N_COL, EXP_DEV, capacity, width), BF16),
        "dr_out": ((N_ROW, 8, width // 2), F32),
        "grid": (grid + (width,), BF16),
        "table": ((N_COL, 8, 128), F32),
        "compact": ((N_ROW, N_COL // 4, 8, 128), F32),
        "t_stage": ((N_ROW, 8, width), F32),
        "everyone": (whole, BF16),
        "turned": ((N_ROW, EXP_DEV, slots, records), BF16),
        "hidden": (grid + (units,), BF16),
        "for_gate": (grid + (units,), BF16),
        "for_up": (grid + (units,), BF16),
        "acc": ((EXP_DEV, N_COL, N_ROW, 8, units), F32),
        "hb": ((EXP_DEV, 4, N_ROW * records // 4, units), BF16),
        "part": (whole, BF16),
        "half": (whole[1:], BF16),
        "sums": (whole[1:], BF16),
        "from_xz": ((N_XZ - 1,) + whole[2:], BF16),
        "sums_row": ((N_ROW, 8, width), F32),
        "from_row": ((N_ROW - 1, 8, width), F32),
        "e_stage": ((N_ROW, 8, width), F32),
        "e_whole": (whole, BF16),
        "g_stage": ((N_ROW, 8, width), F32),
        "grads": (whole, BF16),
        "back": (grid + (width,), BF16),
        "far_buf": ((2, 2, 2) + block, BF16),
        "near_buf": ((2, 2, GROUPS) + block, BF16),
        "x_buf": ((GROUPS,) + block, BF16),
        "sum_buf": ((GROUPS,) + block, BF16),
        "q": ((N_ROW, N_COL, 128), F32),
        "q_buf": ((N_ROW - 1, N_COL, 128), F32),
        "q_msg": ((N_COL, 8, 128), F32),
        "q_in": ((N_COL, 8, 128), F32),
        "dr": ((N_ROW, 8, width // 2), F32),
        "dr_in": ((N_ROW, 8, width // 2), F32),
        "dr_sum": ((N_COL, 8, width // 2), F32),
        "gate_out": (ins["w_gate"].shape, F32),
        "up_out": (ins["w_up"].shape, F32),
        "down_out": (ins["w_down"].shape, F32),
    }
    row, col, chips = (N_ROW - 1,), (N_COL - 1,), (N_XZ - 1,)
    sems = {
        "own_sem": (), "out_sem": (3, EXP_DEV),
        "m_send": col, "m_recv": col, "a_send": col, "a_recv": (N_COL,), "c_send": row, "c_recv": row,
        "x_send": (GROUPS,), "x_recv": (GROUPS,), "n_send": (2, 2, GROUPS), "n_recv": (2, 2, GROUPS),
        "f_send": (2, 2, 2), "f_recv": (2, 2, 2),
        "s1": (), "r1": (), "s2": chips, "r2": chips, "s3": row, "r3": row,
        "bf_send": (2, 2, 2), "bf_recv": (2, 2, 2), "bn_send": (2, 2, GROUPS), "bn_recv": (2, 2, GROUPS),
        "bx_send": (GROUPS,), "bx_recv": (GROUPS,), "h_send": (N_COL,), "h_recv": (N_COL,),
        "q1_send": row, "q1_recv": row, "q2_send": col, "q2_recv": col,
        "d1_send": row, "d1_recv": row, "d2_send": col, "d2_recv": col, "d3_send": row, "d3_recv": row,
    }
    for letter in "teg":
        for kind in "sr":
            sems.update({letter + kind + "1": row, letter + kind + "2": chips, letter + kind + "3": ()})
    names = list(ins) + list(outs) + list(scratch) + list(sems)
    result = pl.pallas_call(
        functools.partial(fused_kernel, names),
        out_shape=tuple(jax.ShapeDtypeStruct(shape, dtype) for shape, dtype, _ in outs.values()),
        in_specs=[SMEM if name in ("log_scale", "bias", "loss_scale") else VMEM for name in ins],
        out_specs=tuple(spec for _, _, spec in outs.values()),
        scratch_shapes=[pltpu.VMEM(shape, dtype) for shape, dtype in scratch.values()]
        + [pltpu.SemaphoreType.DMA(shape) for shape in sems.values()],
        compiler_params=pltpu.CompilerParams(
            collective_id=0, has_side_effects=True, vmem_limit_bytes=61 << 20
        ),
    )(*ins.values())
    return result


def body(tokens, expert_ids, text, w_gate, w_up, w_down, router, log_scale, bias, loss_scale):
    return fused({
        "tokens": tokens, "ids": expert_ids, "text": text, "w_gate": w_gate, "w_up": w_up, "w_down": w_down,
        "router": router, "log_scale": log_scale, "bias": bias, "loss_scale": loss_scale,
    })


def solution(mesh):
    in_specs = (
        P(("row", "col"), None),
        P(("row", "col"), None),
        P(("row", "col"), None),
        P("col", None, "row"),
        P("col", None, "row"),
        P("col", "row", None),
        P(),
        P(),
        P(),
        P(),
    )
    out_specs = (
        P(("row", "col"), None),
        P(("row", "col"), None),
        P("col", None, "row"),
        P("col", None, "row"),
        P("col", "row", None),
        P(),
    )
    return jax.shard_map(body, mesh=mesh, in_specs=in_specs, out_specs=out_specs, check_vma=False)
```

```python
import functools
import types

import jax
import jax.numpy as jnp
from jax import lax
from jax.experimental import pallas as pl
from jax.experimental.pallas import tpu as pltpu
from jax.sharding import PartitionSpec as P

EXP_DEV = 2
SEQ = 16
F32 = jnp.float32
BF16 = jnp.bfloat16
MESH = pl.DeviceIdType.MESH
VMEM = pl.BlockSpec(memory_space=pltpu.VMEM)
SMEM = pl.BlockSpec(memory_space=pltpu.SMEM)
ANY = pl.BlockSpec(memory_space=pl.ANY)
N_ROW, N_COL, N_XZ = 8, 16, 8
X_OUT, X_BACK = 9, 8
KEPT = ("d_gate", "d_up", "d_down", "d_text", "d_tokens", "d_router")


def column_of(place):
    return (place % N_XZ) * 2 + place // N_XZ


def place_of(column):
    return (column % 2) * N_XZ + column // 2


def remote(src, dst, send_sem, recv_sem, row, col):
    return pltpu.make_async_remote_copy(
        src_ref=src, dst_ref=dst, send_sem=send_sem, recv_sem=recv_sem,
        device_id={"row": row, "col": col}, device_id_type=MESH,
    )


def here():
    row, col = lax.axis_index("row"), lax.axis_index("col")
    return row, col, col // 2, col % 2


def greet(all_columns, all_rows):
    row, col, xz, core = here()
    barrier = pltpu.get_barrier_semaphore()

    def signal(r, c):
        pl.semaphore_signal(barrier, inc=1, device_id={"row": r, "col": c}, device_id_type=MESH)

    count = 0
    if all_columns:
        def col_step(d, _):
            signal(row, (col + d) % N_COL)
            return 0
        lax.fori_loop(1, N_COL, col_step, 0)
        count += N_COL - 1
    else:
        def xz_step(d, _):
            signal(row, ((xz + d) % N_XZ) * 2 + core)
            return 0
        lax.fori_loop(1, N_XZ, xz_step, 0)
        signal(row, xz * 2 + 1 - core)
        count += N_XZ
    if all_rows:
        def row_step(d, _):
            signal((row + d) % N_ROW, col)
            return 0
        lax.fori_loop(1, N_ROW, row_step, 0)
        count += N_ROW - 1
    return count


def all_here(count):
    pl.semaphore_wait(pltpu.get_barrier_semaphore(), count)


def loop(low, high, step):
    lax.fori_loop(low, high, lambda i, _: (step(i), 0)[1], 0)


class Gather:
    def __init__(self, begin, stage, whole, sems):
        self.begin, self.stage, self.whole = begin, stage, whole
        self.s1, self.r1, self.s2, self.r2, self.s3, self.r3 = sems
        self.row, self.col, self.xz, self.core = here()

    def first(self, d):
        to = (self.row + d) % N_ROW
        mine = self.stage.at[self.row]
        return remote(mine, mine, self.s1.at[d - 1], self.r1.at[d - 1], to, self.col)

    def second(self, d):
        to = (self.xz + d) % N_XZ
        mine = self.whole.at[self.core, self.xz]
        return remote(mine, mine, self.s2.at[d - 1], self.r2.at[d - 1], self.row, to * 2 + self.core)

    def third(self, d):
        at = self.whole.at[self.core, (self.xz + N_XZ - d) % N_XZ]
        return remote(at, at, self.s3.at[d], self.r3.at[d], self.row, self.xz * 2 + 1 - self.core)

    def first_arrived(self, d):
        at = self.stage.at[(self.row + N_ROW - d) % N_ROW]
        remote(at, at, self.s1.at[d - 1], self.r1.at[d - 1], self.row, self.col).wait_recv()

    def second_arrived(self, d):
        at = self.whole.at[self.core, (self.xz + N_XZ - d) % N_XZ]
        remote(at, at, self.s2.at[d - 1], self.r2.at[d - 1], self.row, self.col).wait_recv()

    def start(self, rows):
        self.stage[self.row] = rows
        self.begin(N_ROW, self.first)

    def spread(self):
        loop(1, N_ROW, self.first_arrived)
        block = self.stage[...]
        self.whole[self.core, self.xz] = block.reshape(-1, block.shape[-1]).astype(BF16)
        self.begin(N_XZ, self.second)
        self.third(0).start()

    def swap(self):
        def one(d):
            self.second_arrived(d)
            self.third(d).start()
        loop(1, N_XZ, one)

    def finish(self):
        def one(d):
            at = self.whole.at[1 - self.core, (self.xz + N_XZ - d) % N_XZ]
            remote(at, at, self.s3.at[d], self.r3.at[d], self.row, self.col).wait_recv()
        loop(0, N_XZ, one)
        loop(0, N_XZ, lambda d: self.third(d).wait_send())


class QuietGather(Gather):
    def __init__(self, begin, stage, whole, sems):
        super().__init__(begin, stage, whole, sems[:6])
        self.s4, self.r4 = sems[6:]
        self.x, self.z = self.xz // 4, self.xz % 4

    def column(self, x, z, core):
        return (x * 4 + z) * 2 + core

    def pair(self):
        at = self.whole.at[self.core, self.x, self.z]
        return remote(at, at, self.s4, self.r4, self.row, self.column(1 - self.x, self.z, self.core))

    def second(self, d):
        at = self.whole.at[self.core, :, self.z]
        to = self.column(self.x, (self.z + d) % 4, self.core)
        return remote(at, at, self.s2.at[d - 1], self.r2.at[d - 1], self.row, to)

    def third(self, d):
        at = self.whole.at[self.core, :, (self.z + 4 - d) % 4]
        return remote(at, at, self.s3.at[d], self.r3.at[d], self.row, self.xz * 2 + 1 - self.core)

    def spread(self):
        loop(1, N_ROW, self.first_arrived)
        block = self.stage[...]
        self.whole[self.core, self.x, self.z] = block.reshape(-1, block.shape[-1]).astype(BF16)
        self.begin(2, lambda d: self.pair())

    def relay(self):
        at = self.whole.at[self.core, 1 - self.x, self.z]
        remote(at, at, self.s4, self.r4, self.row, self.col).wait_recv()
        self.begin(4, self.second)
        self.third(0).start()

    def swap(self):
        def one(d):
            at = self.whole.at[self.core, :, (self.z + 4 - d) % 4]
            remote(at, at, self.s2.at[d - 1], self.r2.at[d - 1], self.row, self.col).wait_recv()
            self.third(d).start()
        loop(1, 4, one)

    def finish(self):
        def one(d):
            at = self.whole.at[1 - self.core, :, (self.z + 4 - d) % 4]
            remote(at, at, self.s3.at[d], self.r3.at[d], self.row, self.col).wait_recv()
        loop(0, 4, one)
        loop(0, 4, lambda d: self.third(d).wait_send())


def fused_kernel(names, *refs):
    n = types.SimpleNamespace(**dict(zip(names, refs)))
    row, col, xz, core = here()
    place = core * N_XZ + xz
    y, high = row % 4, row // 4
    other_row = (1 - high) * 4 + y
    width = n.tokens.shape[-1]
    units = n.w_gate.shape[-1]
    capacity = n.grid.shape[3]
    slots = N_COL * capacity
    records = N_COL * 8
    batch = N_ROW * records

    def row_of(rel, step):
        return ((high + rel) % 2) * 4 + (y + step + 4) % 4

    def arrived(at, sem):
        remote(at, at, n.a_send.at[0], sem, row, col).wait_recv()

    pending = []

    def begin(count, make):
        loop(1, count, lambda d: make(d).start())
        pending.append(lambda: loop(1, count, lambda d: make(d).wait_send()))

    def iota(shape, dim):
        return lax.broadcasted_iota(jnp.int32, shape, dim)

    def exact(left, right, dims):
        return lax.dot_general(
            left, right, (dims, ((), ())), precision=lax.Precision.HIGHEST, preferred_element_type=F32
        )

    def fast(left, right, dims):
        return lax.dot_general(left, right, (dims, ((), ())), preferred_element_type=F32)

    def one_hot(at, lanes):
        return (iota((at.shape[0], lanes), 1) == at).astype(F32)

    greeted = greet(True, True)

    tokens = n.tokens[...].astype(F32)
    tok_count = tokens.shape[0]
    inverse_rms = lax.rsqrt(jnp.mean(tokens * tokens, -1, keepdims=True) + 1e-06)
    norm_in = (tokens * inverse_rms).astype(BF16)
    scores = exact(norm_in.astype(F32), n.router[...], ((1,), (1,)))
    experts = scores.shape[-1]
    diagonal = iota((tok_count, tok_count), 0) == iota((tok_count, tok_count), 1)
    ids = [jnp.sum(jnp.where(diagonal, n.ids[k : k + 1], 0), -1, keepdims=True) for k in range(2)]
    choose = [one_hot(ids[k], experts) for k in range(2)]
    chosen = [jnp.sum(choose[k] * scores, -1, keepdims=True) for k in range(2)]
    gates = [jax.nn.sigmoid(chosen[k] - chosen[1 - k]) for k in range(2)]
    earlier = (iota((tok_count, tok_count), 0) > iota((tok_count, tok_count), 1)).astype(F32).astype(BF16)
    before = fast(earlier, (choose[0] + choose[1]).astype(BF16), ((1,), (0,)))
    to_place, in_line, hits = [], [], []
    meta = jnp.zeros((N_COL * 8, 128), F32)
    for k in range(2):
        position = jnp.sum(choose[k] * before, -1, keepdims=True).astype(jnp.int32)
        column = ids[k] >> 1
        to_place.append((column & 1) * N_XZ + (column >> 1))
        in_line.append((ids[k] & 1) * capacity + position)
        hits.append(one_hot(to_place[k] * (EXP_DEV * capacity) + in_line[k], N_COL * EXP_DEV * capacity))
        by_record = one_hot(to_place[k] * 8 + (iota((tok_count, 1), 0) >> 4), N_COL * 8) * gates[k]
        by_line = one_hot((place % 4) * (EXP_DEV * capacity) + in_line[k], 128)
        meta = meta + fast(by_record.astype(BF16), by_line.astype(BF16), ((0,), (0,)))
    hit = (hits[0] + hits[1]).astype(BF16)
    n.meta[...] = meta.reshape(N_COL, 8, 128)
    n.rows[...] = fast(hit, norm_in, ((0,), (0,))).astype(BF16).reshape(n.rows.shape)
    text = n.text[...].astype(F32)
    text_norm = jnp.sqrt(jnp.sum(text * text, -1, keepdims=True) + 1e-06)
    text_unit = text / text_norm
    scale = jnp.exp(jnp.full((8, 128), n.log_scale[0], F32))[:1, :1]
    shift = n.bias[0]
    factor = n.loss_scale[0] * scale * (1.0 / batch)
    all_here(greeted)

    def meta_part(d):
        to = (place + d) % N_COL
        return remote(n.meta.at[to], n.table.at[place], n.m_send.at[d - 1], n.m_recv.at[d - 1], row, column_of(to))

    def part(d):
        to = (place + d) % N_COL
        return remote(
            n.rows.at[to], n.grid.at[:, place, row], n.a_send.at[d - 1], n.a_recv.at[place], row, column_of(to)
        )

    begin(N_COL, meta_part)
    own = pltpu.make_async_copy(n.rows.at[place], n.grid.at[:, place, row], n.own_sem)
    own.start()
    begin(N_COL, part)
    texts = QuietGather(
        begin, n.t_stage, n.everyone, [n.ts1, n.tr1, n.ts2, n.tr2, n.ts3, n.tr3, n.ts4, n.tr4]
    )
    texts.start(text_unit)
    n.table[place] = n.meta[place]
    loop(1, N_COL, lambda d: arrived(n.table.at[(place + N_COL - d) % N_COL], n.m_recv.at[d - 1]))
    n.compact[row] = jnp.sum(n.table[...].reshape(N_COL // 4, 4, 8, 128), 1)

    def table_copy(d):
        at = n.compact.at[row]
        return remote(at, at, n.c_send.at[d - 1], n.c_recv.at[d - 1], (row + d) % N_ROW, col)

    begin(N_ROW, table_copy)

    def near_of(way):
        return 1 - 2 * way

    def source(d):
        return (place + N_COL - d) % N_COL

    def block(d, at_row):
        return n.grid.at[:, source(d), at_row]

    def across(step, d):
        at = block(d, row_of(0, step))
        return remote(at, at, n.x_send.at[step % 4, d], n.x_recv.at[step % 4, d], other_row, col)

    def near(way, rel, d):
        at = block(d, row_of(rel, 0))
        return remote(at, at, n.n_send.at[way, rel, d], n.n_recv.at[way, rel, d], row_of(0, near_of(way)), col)

    def far(rel, d):
        step = near_of(d % 2)
        at = block(d, row_of(rel, -step))
        return remote(at, at, n.f_send.at[rel, d], n.f_recv.at[rel, d], row_of(0, step), col)

    def got_across(step, d):
        arrived(block(d, row_of(1, step)), n.x_recv.at[step % 4, d])

    def got_near(way, rel, d):
        arrived(block(d, row_of(rel, -near_of(way))), n.n_recv.at[way, rel, d])

    def got_far(rel, d):
        arrived(block(d, row_of(rel, 2)), n.f_recv.at[rel, d])

    def forward(r):
        def one(x):
            tile = n.compact[r]
            spread = jnp.broadcast_to(tile[:, None], (4, 4, 8, 128)).reshape(records, 128)
            at = (records, 128)
            spread = jnp.where(iota(at, 1) // 32 == (iota(at, 0) // 8) % 4, spread, 0.0).astype(BF16)
            at = (128, slots)
            pick = (iota(at, 0) % 32 == x * capacity + iota(at, 1) % capacity).astype(F32).astype(BF16)
            at = (records, slots)
            pool = jnp.dot(spread, pick, preferred_element_type=F32)
            pool = jnp.where(iota(at, 0) // 8 == iota(at, 1) // capacity, pool, 0.0).astype(BF16)
            at = (slots, 128)
            pick = (iota(at, 1) % 32 == x * capacity + iota(at, 0) % capacity).astype(F32).astype(BF16)
            at = (slots, records)
            turned = lax.dot_general(pick, spread, (((1,), (1,)), ((), ())), preferred_element_type=F32)
            n.turned[r, x] = jnp.where(iota(at, 1) // 8 == iota(at, 0) // capacity, turned, 0.0).astype(BF16)
            rows = n.grid[x, :, r].reshape(slots, width)
            gate_pre = jnp.dot(rows, n.w_gate[x], preferred_element_type=F32)
            up_pre = jnp.dot(rows, n.w_up[x], preferred_element_type=F32)
            sigma = jax.nn.sigmoid(gate_pre)
            silu_gate = gate_pre * sigma
            hidden = (silu_gate * up_pre).astype(BF16)
            shape = (N_COL, capacity, units)
            n.hidden[x, :, r] = hidden.reshape(shape)
            n.for_gate[x, :, r] = (up_pre * (sigma * (1.0 + gate_pre * (1.0 - sigma)))).astype(BF16).reshape(shape)
            n.for_up[x, :, r] = silu_gate.astype(BF16).reshape(shape)
            n.acc[x, :, r] = jnp.dot(pool, hidden, preferred_element_type=F32).reshape(N_COL, 8, units)
        loop(0, EXP_DEV, one)

    def from_column(d):
        @pl.when(d != 0)
        def _():
            arrived(block(d, row), n.a_recv.at[source(d)])

        near(0, 0, d).start()
        near(1, 0, d).start()
        across(0, d).start()

    own.wait()
    loop(0, N_COL, from_column)
    texts.spread()
    forward(row)
    loop(1, N_ROW, lambda d: arrived(n.compact.at[(row + N_ROW - d) % N_ROW], n.c_recv.at[d - 1]))

    def x_first(d):
        got_across(0, d)
        near(0, 1, d).start()
        near(1, 1, d).start()
        got_near(0, 0, d)
        got_near(1, 0, d)
        far(0, d).start()

    def y_first(d):
        got_near(0, 0, d)
        got_near(1, 0, d)
        far(0, d).start()
        across(-1, d).start()
        across(1, d).start()

    def y_first_far(d):
        got_far(0, d)
        across(2, d).start()
        got_across(0, d)

    def x_first_other(d):
        got_near(0, 1, d)
        got_near(1, 1, d)
        far(1, d).start()

    def y_first_other(d):
        got_across(-1, d)
        got_across(1, d)

    loop(0, X_OUT, x_first)
    texts.relay()
    loop(X_OUT, N_COL, y_first)
    loop(0, 2, lambda way: forward(row_of(0, near_of(way))))
    loop(X_OUT, N_COL, y_first_far)
    forward(other_row)
    texts.swap()
    loop(0, X_OUT, x_first_other)
    loop(X_OUT, N_COL, y_first_other)
    loop(0, 2, lambda way: forward(row_of(1, near_of(way))))
    loop(0, X_OUT, lambda d: got_far(0, d))
    forward(row_of(0, 2))
    loop(0, X_OUT, lambda d: got_far(1, d))
    loop(X_OUT, N_COL, lambda d: got_across(2, d))
    forward(row_of(1, 2))

    def sent_first(d):
        far(1, d).wait_send()
        for way in range(2):
            near(way, 1, d).wait_send()

    def sent_all(d):
        far(0, d).wait_send()
        across(0, d).wait_send()
        for way in range(2):
            near(way, 0, d).wait_send()

    def sent_last(d):
        for step in (-1, 1, 2):
            across(step, d).wait_send()

    pending.append(lambda: loop(0, X_OUT, sent_first))
    pending.append(lambda: loop(0, N_COL, sent_all))
    pending.append(lambda: loop(X_OUT, N_COL, sent_last))

    def quarter(q):
        return n.hb[0, q], n.hb[1, q]

    def round_pooled(q):
        for x in range(EXP_DEV):
            n.hb[x, q] = n.acc[x, pl.ds(q * 4, 4)].reshape(-1, units).astype(BF16)

    def shares(k):
        return n.back.at[0, pl.ds(k * 4, 4)]

    def of_chip(first, i):
        return n.back.at[0, first + i // 2, pl.ds((i % 2) * 4, 4)]

    def came(d):
        return n.back.at[1, (d - 1) // 2, pl.ds(((d - 1) % 2) * 4, 4)]

    def share(q):
        first, second = quarter(q)
        total = fast(first, n.w_down[0], ((1,), (0,))) + fast(second, n.w_down[1], ((1,), (0,)))
        n.back[0, pl.ds(q * 2, 2)] = total.astype(BF16).reshape(2, N_ROW, capacity, width)

    loop(0, 4, round_pooled)
    loop(0, 2, lambda i: share((1 - core) * 2 + i))
    swap = remote(shares(1 - core), shares(2), n.s1, n.r1, row, xz * 2 + 1 - core)
    swap.start()
    loop(0, 2, lambda i: share(core * 2 + i))
    swap.wait()

    def add(i):
        of_chip(12, i)[...] = (of_chip(core * 4, i)[...].astype(F32) + of_chip(8, i)[...].astype(F32)).astype(BF16)

    loop(0, N_XZ, add)

    def to_chip(d):
        to = (xz + d) % N_XZ
        return remote(of_chip(12, to), came(d), n.s2.at[d - 1], n.r2.at[d - 1], row, to * 2 + core)

    loop(1, N_XZ, lambda d: to_chip(d).start())
    loop(1, N_XZ, lambda d: to_chip(d).wait_recv())
    total = of_chip(12, xz)[...].astype(F32)
    for d in range(1, N_XZ):
        total = total + came(d)[...].astype(F32)
    n.sums_row[...] = total.reshape(n.sums_row.shape)
    loop(1, N_XZ, lambda d: to_chip(d).wait_send())

    def to_row(d):
        to = (row + d) % N_ROW
        return remote(n.sums_row.at[to], n.from_row.at[d - 1], n.s3.at[d - 1], n.r3.at[d - 1], to, col)

    begin(N_ROW, to_row)
    texts.finish()
    loop(1, N_ROW, lambda d: to_row(d).wait_recv())
    total = n.sums_row[row]
    for d in range(N_ROW - 1):
        total = total + n.from_row[d]
    tok_mean = jnp.mean(n.tokens[...].astype(F32).reshape(-1, SEQ, width), 1)
    pooled = tok_mean + total * (1.0 / SEQ)
    pooled_norm = jnp.sqrt(jnp.sum(pooled * pooled, -1, keepdims=True) + 1e-06)
    embed = pooled / pooled_norm
    embed_b = embed.astype(BF16)
    embeds = QuietGather(
        begin, n.e_stage, n.e_whole, [n.es1, n.er1, n.es2, n.er2, n.es3, n.er3, n.es4, n.er4]
    )
    grads = Gather(begin, n.g_stage, n.grads, [n.gs1, n.gr1, n.gs2, n.gr2, n.gs3, n.gr3])
    embeds.start(embed_b.astype(F32))
    at = (8, batch)
    same = (place * N_ROW + row) * 8 + iota(at, 0) == iota(at, 1)
    labels = jnp.where(same, 1.0, -1.0).astype(F32)

    def weigh(mine, others):
        logits = scale * lax.dot_general(mine, others, (((1,), (1,)), ((), ())), preferred_element_type=F32) + shift
        weights = (-factor * labels * jax.nn.sigmoid(-labels * logits)).astype(BF16)
        return jnp.dot(weights, others, preferred_element_type=F32)

    embed_grad = weigh(embed_b, n.everyone[...].reshape(batch, width))
    pooled_grad = (embed_grad - embed * jnp.sum(embed * embed_grad, -1, keepdims=True)) / pooled_norm
    out_grad = pooled_grad * (1.0 / SEQ)
    n.own_grad[...] = out_grad
    grads.start(out_grad)
    grads.spread()
    grads.swap()
    grads.finish()

    def through_down(q):
        block = n.grads[q // 2, pl.ds((q % 2) * 4, 4)].reshape(-1, width)
        for x in range(EXP_DEV):
            back = lax.dot_general(block, n.w_down[x], (((1,), (1,)), ((), ())), preferred_element_type=F32)
            n.acc[x, pl.ds(q * 4, 4)] = back.reshape(4, N_ROW, 8, units)

    def deltas(r):
        n.q[r] = jnp.zeros(n.q.shape[1:], F32)

        def one(x):
            back = n.acc[x, :, r].reshape(records, units).astype(BF16)
            hidden_grad = jnp.dot(n.turned[r, x], back, preferred_element_type=F32)
            shape = (N_COL, capacity, units)
            hidden = n.hidden[x, :, r].reshape(slots, units).astype(F32)
            q = jnp.sum(hidden * hidden_grad, -1, keepdims=True)
            at = (slots, 128)
            q = jnp.where(iota(at, 1) == x * capacity + iota(at, 0) % capacity, q, 0.0)
            n.q[r] += jnp.sum(q.reshape(N_COL, capacity, 128), 1)
            gate_delta = hidden_grad * n.for_gate[x, :, r].reshape(slots, units).astype(F32)
            up_delta = hidden_grad * n.for_up[x, :, r].reshape(slots, units).astype(F32)
            n.for_gate[x, :, r] = gate_delta.astype(BF16).reshape(shape)
            n.for_up[x, :, r] = up_delta.astype(BF16).reshape(shape)
        loop(0, EXP_DEV, one)

    def backward(r):
        def one(x):
            total = fast(n.for_gate[x, :, r].reshape(slots, units), n.w_gate[x], ((1,), (1,)))
            total = total + fast(n.for_up[x, :, r].reshape(slots, units), n.w_up[x], ((1,), (1,)))
            n.back[x, :, r] = total.astype(BF16).reshape(N_COL, capacity, width)
        loop(0, EXP_DEV, one)

    def target(d, at_row):
        return n.back.at[:, (place + d) % N_COL, at_row]

    def far_back(rel, d):
        src = target(d, row_of(rel, 2))
        return remote(src, n.far_buf.at[rel, d], n.bf_send.at[rel, d], n.bf_recv.at[rel, d], row_of(0, near_of(d % 2)), col)

    def near_back(way, rel, d):
        src = target(d, row_of(rel, near_of(way)))
        return remote(
            src, n.near_buf.at[way, rel, d], n.bn_send.at[way, rel, d], n.bn_recv.at[way, rel, d],
            row_of(0, near_of(way)), col,
        )

    def from_across(step, d):
        if step == 0:
            return n.x_buf.at[d]
        return n.x_last.at[step % 4 - 1, d - X_BACK]

    def across_back(step, d):
        return remote(
            target(d, row_of(1, step)), from_across(step, d), n.bx_send.at[step % 4, d], n.bx_recv.at[step % 4, d],
            other_row, col,
        )

    def add_into(place_of_sum, *terms):
        for x in range(EXP_DEV):
            total = place_of_sum[x].astype(F32)
            for term in terms:
                total = total + term[x].astype(F32)
            place_of_sum[x] = total.astype(BF16)

    def q_row(d):
        to = (row + d) % N_ROW
        return remote(n.q.at[to], n.q_buf.at[d - 1], n.q1_send.at[d - 1], n.q1_recv.at[d - 1], to, col)

    embeds.spread()
    loop(0, 4, through_down)
    deltas(row_of(1, 2))
    backward(row_of(1, 2))
    loop(0, X_BACK, lambda d: far_back(1, d).start())
    loop(X_BACK, N_COL, lambda d: across_back(2, d).start())

    def other_deltas(i):
        r = row_of(1, 2)
        deltas((r + i) % N_ROW)

    loop(1, N_ROW, other_deltas)
    begin(N_ROW, q_row)
    loop(0, 2, lambda way: backward(row_of(1, near_of(way))))
    loop(0, X_BACK, lambda d: near_back(1 - d % 2, 1, d).start())
    loop(X_BACK, N_COL, lambda d: (across_back(1, d).start(), across_back(-1, d).start()))
    backward(row_of(0, 2))
    loop(0, X_BACK, lambda d: far_back(0, d).start())

    def far_first(d):
        across_back(2, d).wait_recv()
        add_into(target(d, row_of(0, 2)), from_across(2, d))
        far_back(0, d).start()

    loop(X_BACK, N_COL, far_first)
    loop(1, N_ROW, lambda d: q_row(d).wait_recv())
    total = n.q[row]
    for d in range(N_ROW - 1):
        total = total + n.q_buf[d]
    n.q_msg[...] = jnp.broadcast_to(total[:, None, :], n.q_msg.shape)
    n.q_in[place] = n.q_msg[place]

    def q_col(d):
        to = (place + d) % N_COL
        return remote(n.q_msg.at[to], n.q_in.at[place], n.q2_send.at[d - 1], n.q2_recv.at[d - 1], row, column_of(to))

    begin(N_COL, q_col)
    embeds.relay()
    loop(0, 2, lambda way: backward(row_of(0, near_of(way))))
    loop(0, X_BACK, lambda d: near_back(1 - d % 2, 0, d).start())
    backward(other_row)
    loop(X_BACK, N_COL, lambda d: across_back(0, d).start())
    backward(row)

    def far_added(rel, d):
        way = d % 2
        far_back(rel, d).wait_recv()
        add_into(target(d, row_of(rel, near_of(way))), n.far_buf.at[rel, d])
        near_back(way, rel, d).start()

    def near_first(d):
        for step in (1, -1):
            across_back(step, d).wait_recv()
            add_into(target(d, row_of(0, step)), from_across(step, d))
        near_back(1 - d % 2, 0, d).start()

    loop(0, X_BACK, lambda d: far_added(1, d))
    loop(X_BACK, N_COL, near_first)
    loop(X_BACK, N_COL, lambda d: far_added(0, d))
    loop(0, X_BACK, lambda d: far_added(0, d))
    embeds.swap()

    def weight_grads(x):
        dims = (((0,), (0,)), ((), ()))

        def one(t):
            at = pl.ds(pl.multiple_of(t * 256, 256), 256)
            rows = n.grid[x, :, :, :, at].reshape(-1, 256)
            n.d_gate[x, at] = lax.dot_general(
                rows, n.for_gate[x].reshape(-1, units), dims, preferred_element_type=F32
            )
            n.d_up[x, at] = lax.dot_general(
                rows, n.for_up[x].reshape(-1, units), dims, preferred_element_type=F32
            )
        loop(0, width // 256, one)

    loop(1, N_COL, lambda d: arrived(n.q_in.at[(place + N_COL - d) % N_COL], n.q2_recv.at[d - 1]))
    found = []
    for k in range(2):
        lines = exact(one_hot(to_place[k], N_COL), n.q_in[:, 0, :], ((1,), (0,)))
        found.append(jnp.sum(one_hot(in_line[k], 128) * lines, -1, keepdims=True))
    both = found[0] + found[1]
    score_grad = jnp.zeros((tok_count, 128), F32)
    for k in range(2):
        score_grad = score_grad + one_hot(ids[k], 128) * (found[k] - gates[k] * both)
    router_part = exact(score_grad.T[:experts], norm_in.astype(F32), ((1,), (0,)))
    n.dr[...] = jnp.zeros(n.dr.shape, F32)
    tiles = width // 128
    n.router_term[...] = exact(score_grad[:, :experts], n.router[...], ((1,), (0,)))
    for k in range(experts // 8 * tiles):
        i, j = k // tiles, k % tiles
        n.dr[k // 2, k % 2] = router_part[i * 8 : i * 8 + 8, j * 128 : (j + 1) * 128]

    def scatter(d):
        to = (col + d) % N_COL
        return remote(n.dr.at[to], n.dr_in.at[col], n.d1_send.at[d - 1], n.d1_recv.at[d - 1], row, to)

    def tell_row(d):
        at = n.dr_sum.at[row]
        return remote(at, at, n.d2_send.at[d - 1], n.d2_recv.at[d - 1], (row + d) % N_ROW, col)

    def tell_col(d):
        at = n.dr_out.at[col]
        return remote(at, at, n.d3_send.at[d - 1], n.d3_recv.at[d - 1], row, (col + d) % N_COL)

    begin(N_COL, scatter)
    n.dr_in[col] = n.dr[col]
    weight_grads(0)

    def crossed(d):
        near_back(0, 1, d).wait_recv()
        near_back(1, 1, d).wait_recv()
        add_into(target(d, other_row), n.near_buf.at[0, 1, d], n.near_buf.at[1, 1, d])
        across_back(0, d).start()

    loop(0, X_BACK, crossed)
    loop(1, N_COL, lambda d: arrived(n.dr_in.at[(col + N_COL - d) % N_COL], n.d1_recv.at[d - 1]))
    n.dr_sum[row] = jnp.sum(n.dr_in[...], 0)
    begin(N_ROW, tell_row)
    weight_grads(1)

    def down_grads(x):
        def one(t):
            at = pl.ds(pl.multiple_of(t * 128, 128), 128)
            n.d_down[x, at] = fast(
                n.hb[x, :, :, at].reshape(-1, 128), n.grads[...].reshape(batch, width), ((0,), (0,))
            )
        loop(0, units // 128, one)

    def home(d):
        return remote(
            target(d, row), n.slots.at[place], n.h_send.at[d], n.h_recv.at[d], row, column_of((place + d) % N_COL)
        )

    own_home = pltpu.make_async_copy(target(0, row), n.slots.at[place], n.own_sem)

    def complete(d):
        near_back(0, 0, d).wait_recv()
        near_back(1, 0, d).wait_recv()
        across_back(0, d).wait_recv()
        add_into(target(d, row), n.near_buf.at[0, 0, d], n.near_buf.at[1, 0, d], from_across(0, d))

        @pl.when(d != 0)
        def _():
            home(d).start()

        @pl.when(d == 0)
        def _():
            own_home.start()

    loop(X_BACK, N_COL, complete)
    loop(1, N_ROW, lambda d: arrived(n.dr_sum.at[(row + N_ROW - d) % N_ROW], n.d2_recv.at[d - 1]))
    n.dr_out[col] = jnp.sum(n.dr_sum[...], 0)
    begin(N_COL, tell_col)
    down_grads(0)
    down_grads(1)
    embeds.finish()
    text_grad = weigh(text_unit.astype(BF16), n.e_whole[...].reshape(batch, width))
    n.d_text[...] = (text_grad - text_unit * jnp.sum(text_unit * text_grad, -1, keepdims=True)) / text_norm
    loop(0, X_BACK, complete)

    def back_first(d):
        far_back(1, d).wait_send()
        for way in range(2):
            near_back(way, 1, d).wait_send()

    def back_all(d):
        far_back(0, d).wait_send()
        across_back(0, d).wait_send()
        for way in range(2):
            near_back(way, 0, d).wait_send()

    def back_last(d):
        for step in (-1, 1, 2):
            across_back(step, d).wait_send()

    pending.append(lambda: loop(0, X_BACK, back_first))
    pending.append(lambda: loop(0, N_COL, back_all))
    pending.append(lambda: loop(X_BACK, N_COL, back_last))
    pending.append(lambda: loop(1, N_COL, lambda d: home(d).wait_send()))

    loop(1, N_COL, lambda d: arrived(n.dr_out.at[(col + N_COL - d) % N_COL], n.d3_recv.at[d - 1]))
    for wait in pending:
        wait()
    loop(1, N_COL, lambda d: arrived(n.slots.at[source(d)], n.h_recv.at[d]))
    own_home.wait()
    for k in range(experts // 8 * tiles):
        i, j = k // tiles, k % tiles
        n.d_router[i * 8 : i * 8 + 8, j * 128 : (j + 1) * 128] = n.dr_out[k // 2, k % 2]
    input_sum = fast(hit, n.slots[...].reshape(-1, width), ((1,), (0,)))
    norm_grad = input_sum + n.router_term[...]
    normed = n.tokens[...].astype(F32) * inverse_rms
    out_grad = jnp.broadcast_to(n.own_grad[...][:, None, :], (8, SEQ, width)).reshape(tok_count, width)
    n.d_tokens[...] = out_grad + inverse_rms * (
        norm_grad - normed * jnp.mean(norm_grad * normed, -1, keepdims=True)
    )


def fused(ins):
    tok_count, width = ins["tokens"].shape
    units = ins["w_gate"].shape[-1]
    experts = EXP_DEV * N_COL
    capacity = max(2, 4 * tok_count // experts)
    slots, records = N_COL * capacity, N_COL * 8
    whole = (2, N_XZ, N_ROW * 8, width)
    block = (EXP_DEV, capacity, width)
    grid = (EXP_DEV, N_COL, N_ROW, capacity)
    outs = {
        "d_text": ((8, width), F32, VMEM),
        "d_tokens": ((tok_count, width), F32, VMEM),
        "d_gate": (ins["w_gate"].shape, F32, VMEM),
        "d_up": (ins["w_up"].shape, F32, VMEM),
        "d_down": (ins["w_down"].shape, F32, VMEM),
        "d_router": (ins["router"].shape, F32, VMEM),
    }
    scratch = {
        "rows": ((N_COL, EXP_DEV, capacity, width), BF16),
        "meta": ((N_COL, 8, 128), F32),
        "own_grad": ((8, width), F32),
        "router_term": ((tok_count, width), F32),
        "slots": ((N_COL, EXP_DEV, capacity, width), BF16),
        "dr_out": ((N_COL, 2, 8, 128), F32),
        "grid": (grid + (width,), BF16),
        "table": ((N_COL, 8, 128), F32),
        "compact": ((N_ROW, N_COL // 4, 8, 128), F32),
        "t_stage": ((N_ROW, 8, width), F32),
        "everyone": ((2, 2, 4) + whole[2:], BF16),
        "turned": ((N_ROW, EXP_DEV, slots, records), BF16),
        "hidden": (grid + (units,), BF16),
        "for_gate": (grid + (units,), BF16),
        "for_up": (grid + (units,), BF16),
        "acc": ((EXP_DEV, N_COL, N_ROW, 8, units), F32),
        "hb": ((EXP_DEV, 4, N_ROW * records // 4, units), BF16),
        "sums_row": ((N_ROW, 8, width), F32),
        "from_row": ((N_ROW - 1, 8, width), F32),
        "e_stage": ((N_ROW, 8, width), F32),
        "e_whole": ((2, 2, 4) + whole[2:], BF16),
        "g_stage": ((N_ROW, 8, width), F32),
        "grads": (whole, BF16),
        "back": (grid + (width,), BF16),
        "far_buf": ((2, N_COL) + block, BF16),
        "near_buf": ((2, 2, N_COL) + block, BF16),
        "x_buf": ((N_COL,) + block, BF16),
        "x_last": ((3, N_COL - X_BACK) + block, BF16),
        "q": ((N_ROW, N_COL, 128), F32),
        "q_buf": ((N_ROW - 1, N_COL, 128), F32),
        "q_msg": ((N_COL, 8, 128), F32),
        "q_in": ((N_COL, 8, 128), F32),
        "dr": ((N_COL, 2, 8, 128), F32),
        "dr_in": ((N_COL, 2, 8, 128), F32),
        "dr_sum": ((N_ROW, 2, 8, 128), F32),
    }
    row, col, chips = (N_ROW - 1,), (N_COL - 1,), (N_XZ - 1,)
    sems = {
        "own_sem": (),
        "m_send": col, "m_recv": col, "a_send": col, "a_recv": (N_COL,), "c_send": row, "c_recv": row,
        "x_send": (4, N_COL), "x_recv": (4, N_COL), "n_send": (2, 2, N_COL), "n_recv": (2, 2, N_COL),
        "f_send": (2, N_COL), "f_recv": (2, N_COL),
        "s1": (), "r1": (), "s2": chips, "r2": chips, "s3": row, "r3": row,
        "bf_send": (2, N_COL), "bf_recv": (2, N_COL), "bn_send": (2, 2, N_COL), "bn_recv": (2, 2, N_COL),
        "bx_send": (4, N_COL), "bx_recv": (4, N_COL), "h_send": (N_COL,), "h_recv": (N_COL,),
        "q1_send": row, "q1_recv": row, "q2_send": col, "q2_recv": col,
        "d1_send": col, "d1_recv": col, "d2_send": row, "d2_recv": row, "d3_send": col, "d3_recv": col,
    }
    for letter in "teg":
        for kind in "sr":
            sems.update({letter + kind + "1": row, letter + kind + "2": chips, letter + kind + "3": (N_XZ,), letter + kind + "4": ()})
    names = list(ins) + list(outs) + list(scratch) + list(sems)
    result = pl.pallas_call(
        functools.partial(fused_kernel, names),
        out_shape=tuple(
            pltpu.VMEM(shape, dtype) if name in KEPT else jax.ShapeDtypeStruct(shape, dtype)
            for name, (shape, dtype, _) in outs.items()
        ),
        in_specs=[SMEM if name in ("log_scale", "bias", "loss_scale") else VMEM for name in ins],
        out_specs=tuple(spec for _, _, spec in outs.values()),
        scratch_shapes=[pltpu.VMEM(shape, dtype) for shape, dtype in scratch.values()]
        + [pltpu.SemaphoreType.DMA(shape) for shape in sems.values()],
        compiler_params=pltpu.CompilerParams(
            collective_id=0, has_side_effects=True, vmem_limit_bytes=50 << 20
        ),
    )(*ins.values())
    return result


def body(tokens, expert_ids, text, w_gate, w_up, w_down, router, log_scale, bias, loss_scale):
    *grads, d_router = fused({
        "tokens": tokens, "ids": expert_ids.T, "text": text, "w_gate": w_gate, "w_up": w_up, "w_down": w_down,
        "router": router.T, "log_scale": log_scale, "bias": bias, "loss_scale": loss_scale,
    })
    return (*grads, d_router.T)


def solution(mesh):
    in_specs = (
        P(("row", "col"), None),
        P(("row", "col"), None),
        P(("row", "col"), None),
        P("col", None, "row"),
        P("col", None, "row"),
        P("col", "row", None),
        P(),
        P(),
        P(),
        P(),
    )
    out_specs = (
        P(("row", "col"), None),
        P(("row", "col"), None),
        P("col", None, "row"),
        P("col", None, "row"),
        P("col", "row", None),
        P(),
    )
    return jax.shard_map(body, mesh=mesh, in_specs=in_specs, out_specs=out_specs, check_vma=False)
```

```python
import functools
import types

import jax
import jax.numpy as jnp
from jax import lax
from jax.experimental import pallas as pl
from jax.experimental.pallas import tpu as pltpu
from jax.sharding import PartitionSpec as P

EXP_DEV = 2
SEQ = 16
F32 = jnp.float32
BF16 = jnp.bfloat16
MESH = pl.DeviceIdType.MESH
VMEM = pl.BlockSpec(memory_space=pltpu.VMEM)
SMEM = pl.BlockSpec(memory_space=pltpu.SMEM)
ANY = pl.BlockSpec(memory_space=pl.ANY)
N_ROW, N_COL, N_XZ = 8, 16, 8
X_OUT, X_BACK = 10, 9
KEPT = ("d_gate", "d_up", "d_down", "d_text", "d_tokens", "d_router")


def column_of(place):
    return (place % N_XZ) * 2 + place // N_XZ


def place_of(column):
    return (column % 2) * N_XZ + column // 2


def remote(src, dst, send_sem, recv_sem, row, col):
    return pltpu.make_async_remote_copy(
        src_ref=src, dst_ref=dst, send_sem=send_sem, recv_sem=recv_sem,
        device_id={"row": row, "col": col}, device_id_type=MESH,
    )


def here():
    row, col = lax.axis_index("row"), lax.axis_index("col")
    return row, col, col // 2, col % 2


def greet(all_columns, all_rows):
    row, col, xz, core = here()
    barrier = pltpu.get_barrier_semaphore()

    def signal(r, c):
        pl.semaphore_signal(barrier, inc=1, device_id={"row": r, "col": c}, device_id_type=MESH)

    count = 0
    if all_columns:
        def col_step(d, _):
            signal(row, (col + d) % N_COL)
            return 0
        lax.fori_loop(1, N_COL, col_step, 0)
        count += N_COL - 1
    else:
        def xz_step(d, _):
            signal(row, ((xz + d) % N_XZ) * 2 + core)
            return 0
        lax.fori_loop(1, N_XZ, xz_step, 0)
        signal(row, xz * 2 + 1 - core)
        count += N_XZ
    if all_rows:
        def row_step(d, _):
            signal((row + d) % N_ROW, col)
            return 0
        lax.fori_loop(1, N_ROW, row_step, 0)
        count += N_ROW - 1
    return count


def all_here(count):
    pl.semaphore_wait(pltpu.get_barrier_semaphore(), count)


def loop(low, high, step):
    lax.fori_loop(low, high, lambda i, _: (step(i), 0)[1], 0)


class Gather:
    def __init__(self, begin, stage, whole, sems):
        self.begin, self.stage, self.whole = begin, stage, whole
        self.s1, self.r1, self.s2, self.r2, self.s3, self.r3 = sems
        self.row, self.col, self.xz, self.core = here()

    def first(self, d):
        to = (self.row + d) % N_ROW
        mine = self.stage.at[self.row]
        return remote(mine, mine, self.s1.at[d - 1], self.r1.at[d - 1], to, self.col)

    def second(self, d):
        to = (self.xz + d) % N_XZ
        mine = self.whole.at[self.core, self.xz]
        return remote(mine, mine, self.s2.at[d - 1], self.r2.at[d - 1], self.row, to * 2 + self.core)

    def third(self, d):
        at = self.whole.at[self.core, (self.xz + N_XZ - d) % N_XZ]
        return remote(at, at, self.s3.at[d], self.r3.at[d], self.row, self.xz * 2 + 1 - self.core)

    def first_arrived(self, d):
        at = self.stage.at[(self.row + N_ROW - d) % N_ROW]
        remote(at, at, self.s1.at[d - 1], self.r1.at[d - 1], self.row, self.col).wait_recv()

    def second_arrived(self, d):
        at = self.whole.at[self.core, (self.xz + N_XZ - d) % N_XZ]
        remote(at, at, self.s2.at[d - 1], self.r2.at[d - 1], self.row, self.col).wait_recv()

    def start(self, rows):
        self.stage[self.row] = rows
        self.begin(N_ROW, self.first)

    def spread(self):
        loop(1, N_ROW, self.first_arrived)
        block = self.stage[...]
        self.whole[self.core, self.xz] = block.reshape(-1, block.shape[-1]).astype(BF16)
        self.begin(N_XZ, self.second)
        self.third(0).start()

    def swap(self):
        def one(d):
            self.second_arrived(d)
            self.third(d).start()
        loop(1, N_XZ, one)

    def finish(self):
        def one(d):
            at = self.whole.at[1 - self.core, (self.xz + N_XZ - d) % N_XZ]
            remote(at, at, self.s3.at[d], self.r3.at[d], self.row, self.col).wait_recv()
        loop(0, N_XZ, one)
        loop(0, N_XZ, lambda d: self.third(d).wait_send())


class QuietGather(Gather):
    def __init__(self, begin, stage, whole, sems):
        super().__init__(begin, stage, whole, sems[:6])
        self.s4, self.r4 = sems[6:]
        self.x, self.z = self.xz // 4, self.xz % 4

    def column(self, x, z, core):
        return (x * 4 + z) * 2 + core

    def pair(self):
        at = self.whole.at[self.core, self.x, self.z]
        return remote(at, at, self.s4, self.r4, self.row, self.column(1 - self.x, self.z, self.core))

    def second(self, d):
        at = self.whole.at[self.core, :, self.z]
        to = self.column(self.x, (self.z + d) % 4, self.core)
        return remote(at, at, self.s2.at[d - 1], self.r2.at[d - 1], self.row, to)

    def third(self, d):
        at = self.whole.at[self.core, :, (self.z + 4 - d) % 4]
        return remote(at, at, self.s3.at[d], self.r3.at[d], self.row, self.xz * 2 + 1 - self.core)

    def spread(self):
        loop(1, N_ROW, self.first_arrived)
        block = self.stage[...]
        self.whole[self.core, self.x, self.z] = block.reshape(-1, block.shape[-1]).astype(BF16)
        self.begin(2, lambda d: self.pair())

    def relay(self):
        at = self.whole.at[self.core, 1 - self.x, self.z]
        remote(at, at, self.s4, self.r4, self.row, self.col).wait_recv()
        self.begin(4, self.second)
        self.third(0).start()

    def swap(self):
        def one(d):
            at = self.whole.at[self.core, :, (self.z + 4 - d) % 4]
            remote(at, at, self.s2.at[d - 1], self.r2.at[d - 1], self.row, self.col).wait_recv()
            self.third(d).start()
        loop(1, 4, one)

    def finish(self):
        def one(d):
            at = self.whole.at[1 - self.core, :, (self.z + 4 - d) % 4]
            remote(at, at, self.s3.at[d], self.r3.at[d], self.row, self.col).wait_recv()
        loop(0, 4, one)
        loop(0, 4, lambda d: self.third(d).wait_send())


def fused_kernel(names, *refs):
    n = types.SimpleNamespace(**dict(zip(names, refs)))
    row, col, xz, core = here()
    place = core * N_XZ + xz
    y, high = row % 4, row // 4
    other_row = (1 - high) * 4 + y
    width = n.tokens.shape[-1]
    units = n.w_gate.shape[-1]
    capacity = n.grid.shape[3]
    slots = N_COL * capacity
    records = N_COL * 8
    batch = N_ROW * records

    def row_of(rel, step):
        return ((high + rel) % 2) * 4 + (y + step + 4) % 4

    def arrived(at, sem):
        remote(at, at, n.a_send.at[0], sem, row, col).wait_recv()

    pending = []

    def begin(count, make):
        loop(1, count, lambda d: make(d).start())
        pending.append(lambda: loop(1, count, lambda d: make(d).wait_send()))

    def iota(shape, dim):
        return lax.broadcasted_iota(jnp.int32, shape, dim)

    def exact(left, right, dims):
        return lax.dot_general(
            left, right, (dims, ((), ())), precision=lax.Precision.HIGHEST, preferred_element_type=F32
        )

    def fast(left, right, dims):
        return lax.dot_general(left, right, (dims, ((), ())), preferred_element_type=F32)

    def one_hot(at, lanes):
        return (iota((at.shape[0], lanes), 1) == at).astype(F32)

    def fetch(k):
        source, target = ((n.in_gate, n.w_gate), (n.in_up, n.w_up), (n.in_down, n.w_down))[k]
        return pltpu.make_async_copy(source, target, n.w_sem.at[k])

    for k in range(3):
        fetch(k).start()
    greeted = greet(True, True)

    tokens = n.tokens[...].astype(F32)
    tok_count = tokens.shape[0]
    inverse_rms = lax.rsqrt(jnp.mean(tokens * tokens, -1, keepdims=True) + 1e-06)
    norm_in = (tokens * inverse_rms).astype(BF16)
    scores = exact(norm_in.astype(F32), n.router[...], ((1,), (1,)))
    experts = scores.shape[-1]
    diagonal = iota((tok_count, tok_count), 0) == iota((tok_count, tok_count), 1)
    ids = [jnp.sum(jnp.where(diagonal, n.ids[k : k + 1], 0), -1, keepdims=True) for k in range(2)]
    choose = [one_hot(ids[k], experts) for k in range(2)]
    chosen = [jnp.sum(choose[k] * scores, -1, keepdims=True) for k in range(2)]
    gates = [jax.nn.sigmoid(chosen[k] - chosen[1 - k]) for k in range(2)]
    earlier = (iota((tok_count, tok_count), 0) > iota((tok_count, tok_count), 1)).astype(F32).astype(BF16)
    before = fast(earlier, (choose[0] + choose[1]).astype(BF16), ((1,), (0,)))
    to_place, in_line, hits = [], [], []
    meta = jnp.zeros((N_COL * 8, 128), F32)
    for k in range(2):
        position = jnp.sum(choose[k] * before, -1, keepdims=True).astype(jnp.int32)
        column = ids[k] >> 1
        to_place.append((column & 1) * N_XZ + (column >> 1))
        in_line.append((ids[k] & 1) * capacity + position)
        hits.append(one_hot(to_place[k] * (EXP_DEV * capacity) + in_line[k], N_COL * EXP_DEV * capacity))
        by_record = one_hot(to_place[k] * 8 + (iota((tok_count, 1), 0) >> 4), N_COL * 8) * gates[k]
        by_line = one_hot((place % 4) * (EXP_DEV * capacity) + in_line[k], 128)
        meta = meta + fast(by_record.astype(BF16), by_line.astype(BF16), ((0,), (0,)))
    hit = (hits[0] + hits[1]).astype(BF16)
    n.meta[...] = meta.reshape(N_COL, 8, 128)
    n.rows[...] = fast(hit, norm_in, ((0,), (0,))).astype(BF16).reshape(n.rows.shape)
    text = n.text[...].astype(F32)
    text_norm = jnp.sqrt(jnp.sum(text * text, -1, keepdims=True) + 1e-06)
    text_unit = text / text_norm
    scale = jnp.exp(jnp.full((8, 128), n.log_scale[0], F32))[:1, :1]
    shift = n.bias[0]
    factor = n.loss_scale[0] * scale * (1.0 / batch)
    all_here(greeted)

    def meta_part(d):
        to = (place + d) % N_COL
        return remote(n.meta.at[to], n.table.at[place], n.m_send.at[d - 1], n.m_recv.at[d - 1], row, column_of(to))

    def part(d):
        to = (place + d) % N_COL
        return remote(
            n.rows.at[to], n.grid.at[:, place, row], n.a_send.at[d - 1], n.a_recv.at[place], row, column_of(to)
        )

    begin(N_COL, meta_part)
    own = pltpu.make_async_copy(n.rows.at[place], n.grid.at[:, place, row], n.own_sem)
    own.start()
    begin(N_COL, part)
    texts = QuietGather(
        begin, n.t_stage, n.everyone, [n.ts1, n.tr1, n.ts2, n.tr2, n.ts3, n.tr3, n.ts4, n.tr4]
    )
    texts.start(text_unit)
    n.table[place] = n.meta[place]
    loop(1, N_COL, lambda d: arrived(n.table.at[(place + N_COL - d) % N_COL], n.m_recv.at[d - 1]))
    n.compact[row] = jnp.sum(n.table[...].reshape(N_COL // 4, 4, 8, 128), 1)

    def table_copy(d):
        at = n.compact.at[row]
        return remote(at, at, n.c_send.at[d - 1], n.c_recv.at[d - 1], (row + d) % N_ROW, col)

    begin(N_ROW, table_copy)

    def near_of(way):
        return 1 - 2 * way

    def source(d):
        return (place + N_COL - d) % N_COL

    def block(d, at_row):
        return n.grid.at[:, source(d), at_row]

    def across(step, d):
        at = block(d, row_of(0, step))
        return remote(at, at, n.x_send.at[step % 4, d], n.x_recv.at[step % 4, d], other_row, col)

    def near(way, rel, d):
        at = block(d, row_of(rel, 0))
        return remote(at, at, n.n_send.at[way, rel, d], n.n_recv.at[way, rel, d], row_of(0, near_of(way)), col)

    def far(rel, d):
        step = near_of(d % 2)
        at = block(d, row_of(rel, -step))
        return remote(at, at, n.f_send.at[rel, d], n.f_recv.at[rel, d], row_of(0, step), col)

    def got_across(step, d):
        arrived(block(d, row_of(1, step)), n.x_recv.at[step % 4, d])

    def got_near(way, rel, d):
        arrived(block(d, row_of(rel, -near_of(way))), n.n_recv.at[way, rel, d])

    def got_far(rel, d):
        arrived(block(d, row_of(rel, 2)), n.f_recv.at[rel, d])

    def forward(r):
        def one(x):
            tile = n.compact[r]
            spread = jnp.broadcast_to(tile[:, None], (4, 4, 8, 128)).reshape(records, 128)
            at = (records, 128)
            spread = jnp.where(iota(at, 1) // 32 == (iota(at, 0) // 8) % 4, spread, 0.0).astype(BF16)
            at = (128, slots)
            pick = (iota(at, 0) % 32 == x * capacity + iota(at, 1) % capacity).astype(F32).astype(BF16)
            at = (records, slots)
            pool = jnp.dot(spread, pick, preferred_element_type=F32)
            pool = jnp.where(iota(at, 0) // 8 == iota(at, 1) // capacity, pool, 0.0).astype(BF16)
            at = (slots, 128)
            pick = (iota(at, 1) % 32 == x * capacity + iota(at, 0) % capacity).astype(F32).astype(BF16)
            at = (slots, records)
            turned = lax.dot_general(pick, spread, (((1,), (1,)), ((), ())), preferred_element_type=F32)
            n.turned[r, x] = jnp.where(iota(at, 1) // 8 == iota(at, 0) // capacity, turned, 0.0).astype(BF16)
            rows = n.grid[x, :, r].reshape(slots, width)
            gate_pre = jnp.dot(rows, n.w_gate[x], preferred_element_type=F32)
            up_pre = jnp.dot(rows, n.w_up[x], preferred_element_type=F32)
            sigma = jax.nn.sigmoid(gate_pre)
            silu_gate = gate_pre * sigma
            hidden = (silu_gate * up_pre).astype(BF16)
            shape = (N_COL, capacity, units)
            n.hidden[x, :, r] = hidden.reshape(shape)
            n.for_gate[x, :, r] = (up_pre * (sigma * (1.0 + gate_pre * (1.0 - sigma)))).astype(BF16).reshape(shape)
            n.for_up[x, :, r] = silu_gate.astype(BF16).reshape(shape)
            n.acc[x, :, r] = jnp.dot(pool, hidden, preferred_element_type=F32).reshape(N_COL, 8, units)
        loop(0, EXP_DEV, one)

    def from_column(d):
        @pl.when(d != 0)
        def _():
            arrived(block(d, row), n.a_recv.at[source(d)])

        near(0, 0, d).start()
        near(1, 0, d).start()
        across(0, d).start()

    own.wait()
    loop(0, N_COL, from_column)
    for k in range(3):
        fetch(k).wait()
    texts.spread()
    forward(row)
    loop(1, N_ROW, lambda d: arrived(n.compact.at[(row + N_ROW - d) % N_ROW], n.c_recv.at[d - 1]))

    def x_first(d):
        got_across(0, d)
        near(0, 1, d).start()
        near(1, 1, d).start()
        got_near(0, 0, d)
        got_near(1, 0, d)
        far(0, d).start()

    def y_first(d):
        got_near(0, 0, d)
        got_near(1, 0, d)
        far(0, d).start()
        across(-1, d).start()
        across(1, d).start()

    def y_first_far(d):
        got_far(0, d)
        across(2, d).start()
        got_across(0, d)

    def x_first_other(d):
        got_near(0, 1, d)
        got_near(1, 1, d)
        far(1, d).start()

    def y_first_other(d):
        got_across(-1, d)
        got_across(1, d)

    loop(0, N_COL - X_OUT, y_first)
    loop(N_COL - X_OUT, N_COL, x_first)
    texts.relay()
    loop(0, 2, lambda way: forward(row_of(0, near_of(way))))
    loop(0, N_COL - X_OUT, y_first_far)
    forward(other_row)
    texts.swap()
    loop(N_COL - X_OUT, N_COL, x_first_other)
    loop(0, N_COL - X_OUT, y_first_other)
    loop(0, 2, lambda way: forward(row_of(1, near_of(way))))
    loop(N_COL - X_OUT, N_COL, lambda d: got_far(0, d))
    forward(row_of(0, 2))
    loop(N_COL - X_OUT, N_COL, lambda d: got_far(1, d))
    loop(0, N_COL - X_OUT, lambda d: got_across(2, d))
    forward(row_of(1, 2))

    def sent_first(d):
        far(1, d).wait_send()
        for way in range(2):
            near(way, 1, d).wait_send()

    def sent_all(d):
        far(0, d).wait_send()
        across(0, d).wait_send()
        for way in range(2):
            near(way, 0, d).wait_send()

    def sent_last(d):
        for step in (-1, 1, 2):
            across(step, d).wait_send()

    pending.append(lambda: loop(N_COL - X_OUT, N_COL, sent_first))
    pending.append(lambda: loop(0, N_COL, sent_all))
    pending.append(lambda: loop(0, N_COL - X_OUT, sent_last))

    def quarter(q):
        return n.hb[0, q], n.hb[1, q]

    def round_pooled(q):
        for x in range(EXP_DEV):
            n.hb[x, q] = n.acc[x, pl.ds(q * 4, 4)].reshape(-1, units).astype(BF16)

    def shares(k):
        return n.back.at[0, pl.ds(k * 4, 4)]

    def of_chip(first, i):
        return n.back.at[0, first + i // 2, pl.ds((i % 2) * 4, 4)]

    def came(d):
        return n.back.at[1, (d - 1) // 2, pl.ds(((d - 1) % 2) * 4, 4)]

    def share(q):
        first, second = quarter(q)
        total = fast(first, n.w_down[0], ((1,), (0,))) + fast(second, n.w_down[1], ((1,), (0,)))
        n.back[0, pl.ds(q * 2, 2)] = total.astype(BF16).reshape(2, N_ROW, capacity, width)

    loop(0, 4, round_pooled)
    loop(0, 2, lambda i: share((1 - core) * 2 + i))
    swap = remote(shares(1 - core), shares(2), n.s1, n.r1, row, xz * 2 + 1 - core)
    swap.start()
    loop(0, 2, lambda i: share(core * 2 + i))
    swap.wait()

    def add(i):
        of_chip(12, i)[...] = (of_chip(core * 4, i)[...].astype(F32) + of_chip(8, i)[...].astype(F32)).astype(BF16)

    loop(0, N_XZ, add)

    def to_chip(d):
        to = (xz + d) % N_XZ
        return remote(of_chip(12, to), came(d), n.s2.at[d - 1], n.r2.at[d - 1], row, to * 2 + core)

    loop(1, N_XZ, lambda d: to_chip(d).start())
    loop(1, N_XZ, lambda d: to_chip(d).wait_recv())
    total = of_chip(12, xz)[...].astype(F32)
    for d in range(1, N_XZ):
        total = total + came(d)[...].astype(F32)
    n.sums_row[...] = total.reshape(n.sums_row.shape)
    loop(1, N_XZ, lambda d: to_chip(d).wait_send())

    def to_row(d):
        to = (row + d) % N_ROW
        return remote(n.sums_row.at[to], n.from_row.at[d - 1], n.s3.at[d - 1], n.r3.at[d - 1], to, col)

    begin(N_ROW, to_row)
    texts.finish()
    loop(1, N_ROW, lambda d: to_row(d).wait_recv())
    total = n.sums_row[row]
    for d in range(N_ROW - 1):
        total = total + n.from_row[d]
    tok_mean = jnp.mean(n.tokens[...].astype(F32).reshape(-1, SEQ, width), 1)
    pooled = tok_mean + total * (1.0 / SEQ)
    pooled_norm = jnp.sqrt(jnp.sum(pooled * pooled, -1, keepdims=True) + 1e-06)
    embed = pooled / pooled_norm
    embed_b = embed.astype(BF16)
    embeds = QuietGather(
        begin, n.e_stage, n.e_whole, [n.es1, n.er1, n.es2, n.er2, n.es3, n.er3, n.es4, n.er4]
    )
    grads = Gather(begin, n.g_stage, n.grads, [n.gs1, n.gr1, n.gs2, n.gr2, n.gs3, n.gr3])
    embeds.start(embed_b.astype(F32))
    at = (8, batch)
    same = (place * N_ROW + row) * 8 + iota(at, 0) == iota(at, 1)
    labels = jnp.where(same, 1.0, -1.0).astype(F32)

    def weigh(mine, others):
        logits = scale * lax.dot_general(mine, others, (((1,), (1,)), ((), ())), preferred_element_type=F32) + shift
        weights = (-factor * labels * jax.nn.sigmoid(-labels * logits)).astype(BF16)
        return jnp.dot(weights, others, preferred_element_type=F32)

    embed_grad = weigh(embed_b, n.everyone[...].reshape(batch, width))
    pooled_grad = (embed_grad - embed * jnp.sum(embed * embed_grad, -1, keepdims=True)) / pooled_norm
    out_grad = pooled_grad * (1.0 / SEQ)
    n.own_grad[...] = out_grad
    grads.start(out_grad)
    grads.spread()
    grads.swap()
    grads.finish()

    def through_down(q):
        block = n.grads[q // 2, pl.ds((q % 2) * 4, 4)].reshape(-1, width)
        for x in range(EXP_DEV):
            back = lax.dot_general(block, n.w_down[x], (((1,), (1,)), ((), ())), preferred_element_type=F32)
            n.acc[x, pl.ds(q * 4, 4)] = back.reshape(4, N_ROW, 8, units)

    def deltas(r):
        n.q[r] = jnp.zeros(n.q.shape[1:], F32)

        def one(x):
            back = n.acc[x, :, r].reshape(records, units).astype(BF16)
            hidden_grad = jnp.dot(n.turned[r, x], back, preferred_element_type=F32)
            shape = (N_COL, capacity, units)
            hidden = n.hidden[x, :, r].reshape(slots, units).astype(F32)
            q = jnp.sum(hidden * hidden_grad, -1, keepdims=True)
            at = (slots, 128)
            q = jnp.where(iota(at, 1) == x * capacity + iota(at, 0) % capacity, q, 0.0)
            n.q[r] += jnp.sum(q.reshape(N_COL, capacity, 128), 1)
            gate_delta = hidden_grad * n.for_gate[x, :, r].reshape(slots, units).astype(F32)
            up_delta = hidden_grad * n.for_up[x, :, r].reshape(slots, units).astype(F32)
            n.for_gate[x, :, r] = gate_delta.astype(BF16).reshape(shape)
            n.for_up[x, :, r] = up_delta.astype(BF16).reshape(shape)
        loop(0, EXP_DEV, one)

    def backward(r):
        def one(x):
            total = fast(n.for_gate[x, :, r].reshape(slots, units), n.w_gate[x], ((1,), (1,)))
            total = total + fast(n.for_up[x, :, r].reshape(slots, units), n.w_up[x], ((1,), (1,)))
            n.back[x, :, r] = total.astype(BF16).reshape(N_COL, capacity, width)
        loop(0, EXP_DEV, one)

    def target(d, at_row):
        return n.back.at[:, (place + d) % N_COL, at_row]

    def far_back(rel, d):
        src = target(d, row_of(rel, 2))
        return remote(src, n.far_buf.at[rel, d], n.bf_send.at[rel, d], n.bf_recv.at[rel, d], row_of(0, near_of(d % 2)), col)

    def near_back(way, rel, d):
        src = target(d, row_of(rel, near_of(way)))
        return remote(
            src, n.near_buf.at[way, rel, d], n.bn_send.at[way, rel, d], n.bn_recv.at[way, rel, d],
            row_of(0, near_of(way)), col,
        )

    def from_across(step, d):
        if step == 0:
            return n.x_buf.at[d]
        return n.x_last.at[step % 4 - 1, d]

    def across_back(step, d):
        return remote(
            target(d, row_of(1, step)), from_across(step, d), n.bx_send.at[step % 4, d], n.bx_recv.at[step % 4, d],
            other_row, col,
        )

    def add_into(place_of_sum, *terms):
        for x in range(EXP_DEV):
            total = place_of_sum[x].astype(F32)
            for term in terms:
                total = total + term[x].astype(F32)
            place_of_sum[x] = total.astype(BF16)

    def q_row(d):
        to = (row + d) % N_ROW
        return remote(n.q.at[to], n.q_buf.at[d - 1], n.q1_send.at[d - 1], n.q1_recv.at[d - 1], to, col)

    embeds.spread()
    loop(0, 4, through_down)
    deltas(row_of(1, 2))
    backward(row_of(1, 2))
    loop(N_COL - X_BACK, N_COL, lambda d: far_back(1, d).start())
    loop(0, N_COL - X_BACK, lambda d: across_back(2, d).start())

    def other_deltas(i):
        r = row_of(1, 2)
        deltas((r + i) % N_ROW)

    loop(1, N_ROW, other_deltas)
    begin(N_ROW, q_row)
    loop(0, 2, lambda way: backward(row_of(1, near_of(way))))
    loop(N_COL - X_BACK, N_COL, lambda d: near_back(1 - d % 2, 1, d).start())
    loop(0, N_COL - X_BACK, lambda d: (across_back(1, d).start(), across_back(-1, d).start()))
    backward(row_of(0, 2))
    loop(N_COL - X_BACK, N_COL, lambda d: far_back(0, d).start())

    def far_first(d):
        across_back(2, d).wait_recv()
        add_into(target(d, row_of(0, 2)), from_across(2, d))
        far_back(0, d).start()

    loop(0, N_COL - X_BACK, far_first)
    loop(1, N_ROW, lambda d: q_row(d).wait_recv())
    total = n.q[row]
    for d in range(N_ROW - 1):
        total = total + n.q_buf[d]
    n.q_msg[...] = jnp.broadcast_to(total[:, None, :], n.q_msg.shape)
    n.q_in[place] = n.q_msg[place]

    def q_col(d):
        to = (place + d) % N_COL
        return remote(n.q_msg.at[to], n.q_in.at[place], n.q2_send.at[d - 1], n.q2_recv.at[d - 1], row, column_of(to))

    begin(N_COL, q_col)
    embeds.relay()
    loop(0, 2, lambda way: backward(row_of(0, near_of(way))))
    loop(N_COL - X_BACK, N_COL, lambda d: near_back(1 - d % 2, 0, d).start())
    backward(other_row)
    loop(0, N_COL - X_BACK, lambda d: across_back(0, d).start())
    backward(row)

    def far_added(rel, d):
        way = d % 2
        far_back(rel, d).wait_recv()
        add_into(target(d, row_of(rel, near_of(way))), n.far_buf.at[rel, d])
        near_back(way, rel, d).start()

    def near_first(d):
        for step in (1, -1):
            across_back(step, d).wait_recv()
            add_into(target(d, row_of(0, step)), from_across(step, d))
        near_back(1 - d % 2, 0, d).start()

    loop(N_COL - X_BACK, N_COL, lambda d: far_added(1, d))
    loop(0, N_COL - X_BACK, near_first)
    loop(0, N_COL - X_BACK, lambda d: far_added(0, d))
    loop(N_COL - X_BACK, N_COL, lambda d: far_added(0, d))
    embeds.swap()

    def weight_grads(x):
        dims = (((0,), (0,)), ((), ()))

        def one(t):
            at = pl.ds(pl.multiple_of(t * 256, 256), 256)
            rows = n.grid[x, :, :, :, at].reshape(-1, 256)
            n.d_gate[x, at] = lax.dot_general(
                rows, n.for_gate[x].reshape(-1, units), dims, preferred_element_type=F32
            )
            n.d_up[x, at] = lax.dot_general(
                rows, n.for_up[x].reshape(-1, units), dims, preferred_element_type=F32
            )
        loop(0, width // 256, one)

    loop(1, N_COL, lambda d: arrived(n.q_in.at[(place + N_COL - d) % N_COL], n.q2_recv.at[d - 1]))
    found = []
    for k in range(2):
        lines = exact(one_hot(to_place[k], N_COL), n.q_in[:, 0, :], ((1,), (0,)))
        found.append(jnp.sum(one_hot(in_line[k], 128) * lines, -1, keepdims=True))
    both = found[0] + found[1]
    score_grad = jnp.zeros((tok_count, 128), F32)
    for k in range(2):
        score_grad = score_grad + one_hot(ids[k], 128) * (found[k] - gates[k] * both)
    router_part = exact(score_grad.T[:experts], norm_in.astype(F32), ((1,), (0,)))
    n.dr[...] = jnp.zeros(n.dr.shape, F32)
    tiles = width // 128
    n.router_term[...] = exact(score_grad[:, :experts], n.router[...], ((1,), (0,)))
    for k in range(experts // 8 * tiles):
        i, j = k // tiles, k % tiles
        n.dr[k // 2, k % 2] = router_part[i * 8 : i * 8 + 8, j * 128 : (j + 1) * 128]

    def scatter(d):
        to = (col + d) % N_COL
        return remote(n.dr.at[to], n.dr_in.at[col], n.d1_send.at[d - 1], n.d1_recv.at[d - 1], row, to)

    def tell_row(d):
        at = n.dr_sum.at[row]
        return remote(at, at, n.d2_send.at[d - 1], n.d2_recv.at[d - 1], (row + d) % N_ROW, col)

    def tell_col(d):
        at = n.dr_out.at[col]
        return remote(at, at, n.d3_send.at[d - 1], n.d3_recv.at[d - 1], row, (col + d) % N_COL)

    begin(N_COL, scatter)
    n.dr_in[col] = n.dr[col]
    weight_grads(0)

    def crossed(d):
        near_back(0, 1, d).wait_recv()
        near_back(1, 1, d).wait_recv()
        add_into(target(d, other_row), n.near_buf.at[0, 1, d], n.near_buf.at[1, 1, d])
        across_back(0, d).start()

    loop(N_COL - X_BACK, N_COL, crossed)
    loop(1, N_COL, lambda d: arrived(n.dr_in.at[(col + N_COL - d) % N_COL], n.d1_recv.at[d - 1]))
    n.dr_sum[row] = jnp.sum(n.dr_in[...], 0)
    begin(N_ROW, tell_row)
    weight_grads(1)

    def down_grads(x):
        def one(t):
            at = pl.ds(pl.multiple_of(t * 128, 128), 128)
            n.d_down[x, at] = fast(
                n.hb[x, :, :, at].reshape(-1, 128), n.grads[...].reshape(batch, width), ((0,), (0,))
            )
        loop(0, units // 128, one)

    def home(d):
        return remote(
            target(d, row), n.slots.at[place], n.h_send.at[d], n.h_recv.at[d], row, column_of((place + d) % N_COL)
        )

    own_home = pltpu.make_async_copy(target(0, row), n.slots.at[place], n.own_sem)

    def complete(d):
        near_back(0, 0, d).wait_recv()
        near_back(1, 0, d).wait_recv()
        across_back(0, d).wait_recv()
        add_into(target(d, row), n.near_buf.at[0, 0, d], n.near_buf.at[1, 0, d], from_across(0, d))

        @pl.when(d != 0)
        def _():
            home(d).start()

        @pl.when(d == 0)
        def _():
            own_home.start()

    loop(0, N_COL - X_BACK, complete)
    loop(1, N_ROW, lambda d: arrived(n.dr_sum.at[(row + N_ROW - d) % N_ROW], n.d2_recv.at[d - 1]))
    n.dr_out[col] = jnp.sum(n.dr_sum[...], 0)
    begin(N_COL, tell_col)
    down_grads(0)
    down_grads(1)
    embeds.finish()
    text_grad = weigh(text_unit.astype(BF16), n.e_whole[...].reshape(batch, width))
    n.d_text[...] = (text_grad - text_unit * jnp.sum(text_unit * text_grad, -1, keepdims=True)) / text_norm
    loop(N_COL - X_BACK, N_COL, complete)

    def back_first(d):
        far_back(1, d).wait_send()
        for way in range(2):
            near_back(way, 1, d).wait_send()

    def back_all(d):
        far_back(0, d).wait_send()
        across_back(0, d).wait_send()
        for way in range(2):
            near_back(way, 0, d).wait_send()

    def back_last(d):
        for step in (-1, 1, 2):
            across_back(step, d).wait_send()

    pending.append(lambda: loop(N_COL - X_BACK, N_COL, back_first))
    pending.append(lambda: loop(0, N_COL, back_all))
    pending.append(lambda: loop(0, N_COL - X_BACK, back_last))
    pending.append(lambda: loop(1, N_COL, lambda d: home(d).wait_send()))

    loop(1, N_COL, lambda d: arrived(n.dr_out.at[(col + N_COL - d) % N_COL], n.d3_recv.at[d - 1]))
    for wait in pending:
        wait()
    loop(1, N_COL, lambda d: arrived(n.slots.at[source(d)], n.h_recv.at[d]))
    own_home.wait()
    for k in range(experts // 8 * tiles):
        i, j = k // tiles, k % tiles
        n.d_router[i * 8 : i * 8 + 8, j * 128 : (j + 1) * 128] = n.dr_out[k // 2, k % 2]
    input_sum = fast(hit, n.slots[...].reshape(-1, width), ((1,), (0,)))
    norm_grad = input_sum + n.router_term[...]
    normed = n.tokens[...].astype(F32) * inverse_rms
    out_grad = jnp.broadcast_to(n.own_grad[...][:, None, :], (8, SEQ, width)).reshape(tok_count, width)
    n.d_tokens[...] = out_grad + inverse_rms * (
        norm_grad - normed * jnp.mean(norm_grad * normed, -1, keepdims=True)
    )


def fused(ins):
    tok_count, width = ins["tokens"].shape
    units = ins["in_gate"].shape[-1]
    experts = EXP_DEV * N_COL
    capacity = max(2, 4 * tok_count // experts)
    slots, records = N_COL * capacity, N_COL * 8
    whole = (2, N_XZ, N_ROW * 8, width)
    block = (EXP_DEV, capacity, width)
    grid = (EXP_DEV, N_COL, N_ROW, capacity)
    outs = {
        "d_text": ((8, width), F32, VMEM),
        "d_tokens": ((tok_count, width), F32, VMEM),
        "d_gate": (ins["in_gate"].shape, F32, VMEM),
        "d_up": (ins["in_up"].shape, F32, VMEM),
        "d_down": (ins["in_down"].shape, F32, VMEM),
        "d_router": (ins["router"].shape, F32, VMEM),
    }
    scratch = {
        "w_gate": (ins["in_gate"].shape, BF16),
        "w_up": (ins["in_up"].shape, BF16),
        "w_down": (ins["in_down"].shape, BF16),
        "rows": ((N_COL, EXP_DEV, capacity, width), BF16),
        "meta": ((N_COL, 8, 128), F32),
        "own_grad": ((8, width), F32),
        "router_term": ((tok_count, width), F32),
        "slots": ((N_COL, EXP_DEV, capacity, width), BF16),
        "dr_out": ((N_COL, 2, 8, 128), F32),
        "grid": (grid + (width,), BF16),
        "table": ((N_COL, 8, 128), F32),
        "compact": ((N_ROW, N_COL // 4, 8, 128), F32),
        "t_stage": ((N_ROW, 8, width), F32),
        "everyone": ((2, 2, 4) + whole[2:], BF16),
        "turned": ((N_ROW, EXP_DEV, slots, records), BF16),
        "hidden": (grid + (units,), BF16),
        "for_gate": (grid + (units,), BF16),
        "for_up": (grid + (units,), BF16),
        "acc": ((EXP_DEV, N_COL, N_ROW, 8, units), F32),
        "hb": ((EXP_DEV, 4, N_ROW * records // 4, units), BF16),
        "sums_row": ((N_ROW, 8, width), F32),
        "from_row": ((N_ROW - 1, 8, width), F32),
        "e_stage": ((N_ROW, 8, width), F32),
        "e_whole": ((2, 2, 4) + whole[2:], BF16),
        "g_stage": ((N_ROW, 8, width), F32),
        "grads": (whole, BF16),
        "back": (grid + (width,), BF16),
        "far_buf": ((2, N_COL) + block, BF16),
        "near_buf": ((2, 2, N_COL) + block, BF16),
        "x_buf": ((N_COL,) + block, BF16),
        "x_last": ((3, N_COL - X_BACK) + block, BF16),
        "q": ((N_ROW, N_COL, 128), F32),
        "q_buf": ((N_ROW - 1, N_COL, 128), F32),
        "q_msg": ((N_COL, 8, 128), F32),
        "q_in": ((N_COL, 8, 128), F32),
        "dr": ((N_COL, 2, 8, 128), F32),
        "dr_in": ((N_COL, 2, 8, 128), F32),
        "dr_sum": ((N_ROW, 2, 8, 128), F32),
    }
    row, col, chips = (N_ROW - 1,), (N_COL - 1,), (N_XZ - 1,)
    sems = {
        "own_sem": (), "w_sem": (3,),
        "m_send": col, "m_recv": col, "a_send": col, "a_recv": (N_COL,), "c_send": row, "c_recv": row,
        "x_send": (4, N_COL), "x_recv": (4, N_COL), "n_send": (2, 2, N_COL), "n_recv": (2, 2, N_COL),
        "f_send": (2, N_COL), "f_recv": (2, N_COL),
        "s1": (), "r1": (), "s2": chips, "r2": chips, "s3": row, "r3": row,
        "bf_send": (2, N_COL), "bf_recv": (2, N_COL), "bn_send": (2, 2, N_COL), "bn_recv": (2, 2, N_COL),
        "bx_send": (4, N_COL), "bx_recv": (4, N_COL), "h_send": (N_COL,), "h_recv": (N_COL,),
        "q1_send": row, "q1_recv": row, "q2_send": col, "q2_recv": col,
        "d1_send": col, "d1_recv": col, "d2_send": row, "d2_recv": row, "d3_send": col, "d3_recv": col,
    }
    for letter in "teg":
        for kind in "sr":
            sems.update({letter + kind + "1": row, letter + kind + "2": chips, letter + kind + "3": (N_XZ,), letter + kind + "4": ()})
    names = list(ins) + list(outs) + list(scratch) + list(sems)
    result = pl.pallas_call(
        functools.partial(fused_kernel, names),
        out_shape=tuple(
            pltpu.VMEM(shape, dtype) if name in KEPT else jax.ShapeDtypeStruct(shape, dtype)
            for name, (shape, dtype, _) in outs.items()
        ),
        in_specs=[
            SMEM if name in ("log_scale", "bias", "loss_scale") else ANY if name.startswith("in_") else VMEM
            for name in ins
        ],
        out_specs=tuple(spec for _, _, spec in outs.values()),
        scratch_shapes=[pltpu.VMEM(shape, dtype) for shape, dtype in scratch.values()]
        + [pltpu.SemaphoreType.DMA(shape) for shape in sems.values()],
        compiler_params=pltpu.CompilerParams(
            collective_id=0, has_side_effects=True, vmem_limit_bytes=50 << 20
        ),
    )(*ins.values())
    return result


def body(tokens, expert_ids, text, w_gate, w_up, w_down, router, log_scale, bias, loss_scale):
    *grads, d_router = fused({
        "tokens": tokens, "ids": expert_ids.T, "text": text, "in_gate": w_gate, "in_up": w_up, "in_down": w_down,
        "router": router.T, "log_scale": log_scale, "bias": bias, "loss_scale": loss_scale,
    })
    return (*grads, d_router.T)


def solution(mesh):
    in_specs = (
        P(("row", "col"), None),
        P(("row", "col"), None),
        P(("row", "col"), None),
        P("col", None, "row"),
        P("col", None, "row"),
        P("col", "row", None),
        P(),
        P(),
        P(),
        P(),
    )
    out_specs = (
        P(("row", "col"), None),
        P(("row", "col"), None),
        P("col", None, "row"),
        P("col", None, "row"),
        P("col", "row", None),
        P(),
    )
    return jax.shard_map(body, mesh=mesh, in_specs=in_specs, out_specs=out_specs, check_vma=False)
```

```python
import functools
import types

import jax
import jax.numpy as jnp
from jax import lax
from jax.experimental import pallas as pl
from jax.experimental.pallas import tpu as pltpu
from jax.sharding import PartitionSpec as P

EXP_DEV = 2
SEQ = 16
F32 = jnp.float32
BF16 = jnp.bfloat16
MESH = pl.DeviceIdType.MESH
VMEM = pl.BlockSpec(memory_space=pltpu.VMEM)
SMEM = pl.BlockSpec(memory_space=pltpu.SMEM)
ANY = pl.BlockSpec(memory_space=pl.ANY)
N_ROW, N_COL, N_XZ = 8, 16, 8
X_OUT, X_BACK = 10, 9
KEPT = ("d_gate", "d_up", "d_down", "d_text", "d_tokens", "d_router")


def column_of(place):
    return (place % N_XZ) * 2 + place // N_XZ


def place_of(column):
    return (column % 2) * N_XZ + column // 2


def remote(src, dst, send_sem, recv_sem, row, col):
    return pltpu.make_async_remote_copy(
        src_ref=src, dst_ref=dst, send_sem=send_sem, recv_sem=recv_sem,
        device_id={"row": row, "col": col}, device_id_type=MESH,
    )


def here():
    row, col = lax.axis_index("row"), lax.axis_index("col")
    return row, col, col // 2, col % 2


def greet(all_columns, all_rows):
    row, col, xz, core = here()
    barrier = pltpu.get_barrier_semaphore()

    def signal(r, c):
        pl.semaphore_signal(barrier, inc=1, device_id={"row": r, "col": c}, device_id_type=MESH)

    count = 0
    if all_columns:
        def col_step(d, _):
            signal(row, (col + d) % N_COL)
            return 0
        lax.fori_loop(1, N_COL, col_step, 0)
        count += N_COL - 1
    else:
        def xz_step(d, _):
            signal(row, ((xz + d) % N_XZ) * 2 + core)
            return 0
        lax.fori_loop(1, N_XZ, xz_step, 0)
        signal(row, xz * 2 + 1 - core)
        count += N_XZ
    if all_rows:
        def row_step(d, _):
            signal((row + d) % N_ROW, col)
            return 0
        lax.fori_loop(1, N_ROW, row_step, 0)
        count += N_ROW - 1
    return count


def all_here(count):
    pl.semaphore_wait(pltpu.get_barrier_semaphore(), count)


def loop(low, high, step):
    lax.fori_loop(low, high, lambda i, _: (step(i), 0)[1], 0)


class Gather:
    def __init__(self, begin, stage, whole, sems):
        self.begin, self.stage, self.whole = begin, stage, whole
        self.s1, self.r1, self.s2, self.r2, self.s3, self.r3 = sems
        self.row, self.col, self.xz, self.core = here()

    def first(self, d):
        to = (self.row + d) % N_ROW
        mine = self.stage.at[self.row]
        return remote(mine, mine, self.s1.at[d - 1], self.r1.at[d - 1], to, self.col)

    def second(self, d):
        to = (self.xz + d) % N_XZ
        mine = self.whole.at[self.core, self.xz]
        return remote(mine, mine, self.s2.at[d - 1], self.r2.at[d - 1], self.row, to * 2 + self.core)

    def third(self, d):
        at = self.whole.at[self.core, (self.xz + N_XZ - d) % N_XZ]
        return remote(at, at, self.s3.at[d], self.r3.at[d], self.row, self.xz * 2 + 1 - self.core)

    def first_arrived(self, d):
        at = self.stage.at[(self.row + N_ROW - d) % N_ROW]
        remote(at, at, self.s1.at[d - 1], self.r1.at[d - 1], self.row, self.col).wait_recv()

    def second_arrived(self, d):
        at = self.whole.at[self.core, (self.xz + N_XZ - d) % N_XZ]
        remote(at, at, self.s2.at[d - 1], self.r2.at[d - 1], self.row, self.col).wait_recv()

    def start(self, rows):
        self.stage[self.row] = rows
        self.begin(N_ROW, self.first)

    def spread(self):
        loop(1, N_ROW, self.first_arrived)
        block = self.stage[...]
        self.whole[self.core, self.xz] = block.reshape(-1, block.shape[-1]).astype(BF16)
        self.begin(N_XZ, self.second)
        self.third(0).start()

    def swap(self):
        def one(d):
            self.second_arrived(d)
            self.third(d).start()
        loop(1, N_XZ, one)

    def finish(self):
        def one(d):
            at = self.whole.at[1 - self.core, (self.xz + N_XZ - d) % N_XZ]
            remote(at, at, self.s3.at[d], self.r3.at[d], self.row, self.col).wait_recv()
        loop(0, N_XZ, one)
        loop(0, N_XZ, lambda d: self.third(d).wait_send())


class QuietGather(Gather):
    def __init__(self, begin, stage, whole, sems):
        super().__init__(begin, stage, whole, sems[:6])
        self.s4, self.r4 = sems[6:]
        self.x, self.z = self.xz // 4, self.xz % 4

    def column(self, x, z, core):
        return (x * 4 + z) * 2 + core

    def pair(self):
        at = self.whole.at[self.core, self.x, self.z]
        return remote(at, at, self.s4, self.r4, self.row, self.column(1 - self.x, self.z, self.core))

    def second(self, d):
        at = self.whole.at[self.core, :, self.z]
        to = self.column(self.x, (self.z + d) % 4, self.core)
        return remote(at, at, self.s2.at[d - 1], self.r2.at[d - 1], self.row, to)

    def third(self, d):
        at = self.whole.at[self.core, :, (self.z + 4 - d) % 4]
        return remote(at, at, self.s3.at[d], self.r3.at[d], self.row, self.xz * 2 + 1 - self.core)

    def spread(self):
        loop(1, N_ROW, self.first_arrived)
        block = self.stage[...]
        self.whole[self.core, self.x, self.z] = block.reshape(-1, block.shape[-1]).astype(BF16)
        self.begin(2, lambda d: self.pair())

    def relay(self):
        at = self.whole.at[self.core, 1 - self.x, self.z]
        remote(at, at, self.s4, self.r4, self.row, self.col).wait_recv()
        self.begin(4, self.second)
        self.third(0).start()

    def swap(self):
        def one(d):
            at = self.whole.at[self.core, :, (self.z + 4 - d) % 4]
            remote(at, at, self.s2.at[d - 1], self.r2.at[d - 1], self.row, self.col).wait_recv()
            self.third(d).start()
        loop(1, 4, one)

    def finish(self):
        def one(d):
            at = self.whole.at[1 - self.core, :, (self.z + 4 - d) % 4]
            remote(at, at, self.s3.at[d], self.r3.at[d], self.row, self.col).wait_recv()
        loop(0, 4, one)
        loop(0, 4, lambda d: self.third(d).wait_send())


def fused_kernel(names, *refs):
    n = types.SimpleNamespace(**dict(zip(names, refs)))
    row, col, xz, core = here()
    place = core * N_XZ + xz
    y, high = row % 4, row // 4
    other_row = (1 - high) * 4 + y
    width = n.tokens.shape[-1]
    units = n.w_gate.shape[-1]
    capacity = n.grid.shape[3]
    slots = N_COL * capacity
    records = N_COL * 8
    batch = N_ROW * records

    def row_of(rel, step):
        return ((high + rel) % 2) * 4 + (y + step + 4) % 4

    def arrived(at, sem):
        remote(at, at, n.a_send.at[0], sem, row, col).wait_recv()

    pending = []

    def begin(count, make):
        loop(1, count, lambda d: make(d).start())
        pending.append(lambda: loop(1, count, lambda d: make(d).wait_send()))

    def iota(shape, dim):
        return lax.broadcasted_iota(jnp.int32, shape, dim)

    def exact(left, right, dims):
        return lax.dot_general(
            left, right, (dims, ((), ())), precision=lax.Precision.HIGHEST, preferred_element_type=F32
        )

    def fast(left, right, dims):
        return lax.dot_general(left, right, (dims, ((), ())), preferred_element_type=F32)

    def one_hot(at, lanes):
        return (iota((at.shape[0], lanes), 1) == at).astype(F32)

    def fetch(k):
        source, target = ((n.in_gate, n.w_gate), (n.in_up, n.w_up), (n.in_down, n.w_down))[k]
        return pltpu.make_async_copy(source, target, n.w_sem.at[k])

    for k in range(3):
        fetch(k).start()
    greeted = greet(True, True)

    tokens = n.tokens[...].astype(F32)
    tok_count = tokens.shape[0]
    inverse_rms = lax.rsqrt(jnp.mean(tokens * tokens, -1, keepdims=True) + 1e-06)
    norm_in = (tokens * inverse_rms).astype(BF16)
    scores = exact(norm_in.astype(F32), n.router[...], ((1,), (1,)))
    experts = scores.shape[-1]
    diagonal = iota((tok_count, tok_count), 0) == iota((tok_count, tok_count), 1)
    ids = [jnp.sum(jnp.where(diagonal, n.ids[k : k + 1], 0), -1, keepdims=True) for k in range(2)]
    choose = [one_hot(ids[k], experts) for k in range(2)]
    chosen = [jnp.sum(choose[k] * scores, -1, keepdims=True) for k in range(2)]
    gates = [jax.nn.sigmoid(chosen[k] - chosen[1 - k]) for k in range(2)]
    earlier = (iota((tok_count, tok_count), 0) > iota((tok_count, tok_count), 1)).astype(F32).astype(BF16)
    before = fast(earlier, (choose[0] + choose[1]).astype(BF16), ((1,), (0,)))
    to_place, in_line, hits = [], [], []
    meta = jnp.zeros((N_COL * 8, 128), F32)
    for k in range(2):
        position = jnp.sum(choose[k] * before, -1, keepdims=True).astype(jnp.int32)
        column = ids[k] >> 1
        to_place.append((column & 1) * N_XZ + (column >> 1))
        in_line.append((ids[k] & 1) * capacity + position)
        hits.append(one_hot(to_place[k] * (EXP_DEV * capacity) + in_line[k], N_COL * EXP_DEV * capacity))
        by_record = one_hot(to_place[k] * 8 + (iota((tok_count, 1), 0) >> 4), N_COL * 8) * gates[k]
        by_line = one_hot((place % 4) * (EXP_DEV * capacity) + in_line[k], 128)
        meta = meta + fast(by_record.astype(BF16), by_line.astype(BF16), ((0,), (0,)))
    hit = (hits[0] + hits[1]).astype(BF16)
    n.meta[...] = meta.reshape(N_COL, 8, 128)
    n.rows[...] = fast(hit, norm_in, ((0,), (0,))).astype(BF16).reshape(n.rows.shape)
    text = n.text[...].astype(F32)
    text_norm = jnp.sqrt(jnp.sum(text * text, -1, keepdims=True) + 1e-06)
    text_unit = text / text_norm
    scale = jnp.exp(jnp.full((8, 128), n.log_scale[0], F32))[:1, :1]
    shift = n.bias[0]
    factor = n.loss_scale[0] * scale * (1.0 / batch)
    all_here(greeted)

    def meta_part(d):
        to = (place + d) % N_COL
        return remote(n.meta.at[to], n.table.at[place], n.m_send.at[d - 1], n.m_recv.at[d - 1], row, column_of(to))

    def part(d):
        to = (place + d) % N_COL
        return remote(
            n.rows.at[to], n.grid.at[:, place, row], n.a_send.at[d - 1], n.a_recv.at[place], row, column_of(to)
        )

    begin(N_COL, meta_part)
    own = pltpu.make_async_copy(n.rows.at[place], n.grid.at[:, place, row], n.own_sem)
    own.start()
    begin(N_COL, part)
    texts = QuietGather(
        begin, n.t_stage, n.everyone, [n.ts1, n.tr1, n.ts2, n.tr2, n.ts3, n.tr3, n.ts4, n.tr4]
    )
    texts.start(text_unit)
    n.table[place] = n.meta[place]
    loop(1, N_COL, lambda d: arrived(n.table.at[(place + N_COL - d) % N_COL], n.m_recv.at[d - 1]))
    n.compact[row] = jnp.sum(n.table[...].reshape(N_COL // 4, 4, 8, 128), 1)

    def table_copy(d):
        at = n.compact.at[row]
        return remote(at, at, n.c_send.at[d - 1], n.c_recv.at[d - 1], (row + d) % N_ROW, col)

    begin(N_ROW, table_copy)

    def near_of(way):
        return 1 - 2 * way

    def source(d):
        return (place + N_COL - d) % N_COL

    def block(d, at_row):
        return n.grid.at[:, source(d), at_row]

    def across(step, d):
        at = block(d, row_of(0, step))
        return remote(at, at, n.x_send.at[step % 4, d], n.x_recv.at[step % 4, d], other_row, col)

    def near(way, rel, d):
        at = block(d, row_of(rel, 0))
        return remote(at, at, n.n_send.at[way, rel, d], n.n_recv.at[way, rel, d], row_of(0, near_of(way)), col)

    def far(rel, d):
        step = near_of(d % 2)
        at = block(d, row_of(rel, -step))
        return remote(at, at, n.f_send.at[rel, d], n.f_recv.at[rel, d], row_of(0, step), col)

    def got_across(step, d):
        arrived(block(d, row_of(1, step)), n.x_recv.at[step % 4, d])

    def got_near(way, rel, d):
        arrived(block(d, row_of(rel, -near_of(way))), n.n_recv.at[way, rel, d])

    def got_far(rel, d):
        arrived(block(d, row_of(rel, 2)), n.f_recv.at[rel, d])

    def forward(r):
        def one(x):
            tile = n.compact[r]
            spread = jnp.broadcast_to(tile[:, None], (4, 4, 8, 128)).reshape(records, 128)
            at = (records, 128)
            spread = jnp.where(iota(at, 1) // 32 == (iota(at, 0) // 8) % 4, spread, 0.0).astype(BF16)
            at = (128, slots)
            pick = (iota(at, 0) % 32 == x * capacity + iota(at, 1) % capacity).astype(F32).astype(BF16)
            at = (records, slots)
            pool = jnp.dot(spread, pick, preferred_element_type=F32)
            pool = jnp.where(iota(at, 0) // 8 == iota(at, 1) // capacity, pool, 0.0).astype(BF16)
            at = (slots, 128)
            pick = (iota(at, 1) % 32 == x * capacity + iota(at, 0) % capacity).astype(F32).astype(BF16)
            at = (slots, records)
            turned = lax.dot_general(pick, spread, (((1,), (1,)), ((), ())), preferred_element_type=F32)
            n.turned[r, x] = jnp.where(iota(at, 1) // 8 == iota(at, 0) // capacity, turned, 0.0).astype(BF16)
            rows = n.grid[x, :, r].reshape(slots, width)
            gate_pre = jnp.dot(rows, n.w_gate[x], preferred_element_type=F32)
            up_pre = jnp.dot(rows, n.w_up[x], preferred_element_type=F32)
            sigma = jax.nn.sigmoid(gate_pre)
            silu_gate = gate_pre * sigma
            hidden = (silu_gate * up_pre).astype(BF16)
            shape = (N_COL, capacity, units)
            n.hidden[x, :, r] = hidden.reshape(shape)
            n.for_gate[x, :, r] = (up_pre * (sigma * (1.0 + gate_pre * (1.0 - sigma)))).astype(BF16).reshape(shape)
            n.for_up[x, :, r] = silu_gate.astype(BF16).reshape(shape)
            n.acc[x, :, r] = jnp.dot(pool, hidden, preferred_element_type=F32).reshape(N_COL, 8, units)
        loop(0, EXP_DEV, one)

    def from_column(d):
        @pl.when(d != 0)
        def _():
            arrived(block(d, row), n.a_recv.at[source(d)])

        near(0, 0, d).start()
        near(1, 0, d).start()
        across(0, d).start()

    own.wait()
    loop(0, N_COL, from_column)
    for k in range(3):
        fetch(k).wait()
    texts.spread()
    forward(row)
    loop(1, N_ROW, lambda d: arrived(n.compact.at[(row + N_ROW - d) % N_ROW], n.c_recv.at[d - 1]))

    def x_first(d):
        got_across(0, d)
        near(0, 1, d).start()
        near(1, 1, d).start()
        got_near(0, 0, d)
        got_near(1, 0, d)
        far(0, d).start()

    def y_first(d):
        got_near(0, 0, d)
        got_near(1, 0, d)
        far(0, d).start()
        across(-1, d).start()
        across(1, d).start()

    def y_first_far(d):
        got_far(0, d)
        across(2, d).start()
        got_across(0, d)

    def x_first_other(d):
        got_near(0, 1, d)
        got_near(1, 1, d)
        far(1, d).start()

    def y_first_other(d):
        got_across(-1, d)
        got_across(1, d)

    loop(0, N_COL - X_OUT, y_first)
    loop(N_COL - X_OUT, N_COL, x_first)
    texts.relay()
    loop(0, 2, lambda way: forward(row_of(0, near_of(way))))
    loop(0, N_COL - X_OUT, y_first_far)
    forward(other_row)
    texts.swap()
    loop(N_COL - X_OUT, N_COL, x_first_other)
    loop(0, N_COL - X_OUT, y_first_other)
    loop(0, 2, lambda way: forward(row_of(1, near_of(way))))
    loop(N_COL - X_OUT, N_COL, lambda d: got_far(0, d))
    forward(row_of(0, 2))
    loop(N_COL - X_OUT, N_COL, lambda d: got_far(1, d))
    loop(0, N_COL - X_OUT, lambda d: got_across(2, d))
    forward(row_of(1, 2))

    def sent_first(d):
        far(1, d).wait_send()
        for way in range(2):
            near(way, 1, d).wait_send()

    def sent_all(d):
        far(0, d).wait_send()
        across(0, d).wait_send()
        for way in range(2):
            near(way, 0, d).wait_send()

    def sent_last(d):
        for step in (-1, 1, 2):
            across(step, d).wait_send()

    pending.append(lambda: loop(N_COL - X_OUT, N_COL, sent_first))
    pending.append(lambda: loop(0, N_COL, sent_all))
    pending.append(lambda: loop(0, N_COL - X_OUT, sent_last))

    def quarter(q):
        return n.hb[0, q], n.hb[1, q]

    def round_pooled(q):
        for x in range(EXP_DEV):
            n.hb[x, q] = n.acc[x, pl.ds(q * 4, 4)].reshape(-1, units).astype(BF16)

    def shares(k):
        return n.back.at[0, pl.ds(k * 4, 4)]

    def of_chip(first, i):
        return n.back.at[0, first + i // 2, pl.ds((i % 2) * 4, 4)]

    def came(d):
        return n.back.at[1, (d - 1) // 2, pl.ds(((d - 1) % 2) * 4, 4)]

    def share(q):
        first, second = quarter(q)
        total = fast(first, n.w_down[0], ((1,), (0,))) + fast(second, n.w_down[1], ((1,), (0,)))
        n.back[0, pl.ds(q * 2, 2)] = total.astype(BF16).reshape(2, N_ROW, capacity, width)

    loop(0, 4, round_pooled)
    loop(0, 2, lambda i: share((1 - core) * 2 + i))
    swap = remote(shares(1 - core), shares(2), n.s1, n.r1, row, xz * 2 + 1 - core)
    swap.start()
    loop(0, 2, lambda i: share(core * 2 + i))
    swap.wait()

    def add(i):
        of_chip(12, i)[...] = (of_chip(core * 4, i)[...].astype(F32) + of_chip(8, i)[...].astype(F32)).astype(BF16)

    loop(0, N_XZ, add)

    def to_chip(d):
        to = (xz + d) % N_XZ
        return remote(of_chip(12, to), came(d), n.s2.at[d - 1], n.r2.at[d - 1], row, to * 2 + core)

    loop(1, N_XZ, lambda d: to_chip(d).start())
    loop(1, N_XZ, lambda d: to_chip(d).wait_recv())
    total = of_chip(12, xz)[...].astype(F32)
    for d in range(1, N_XZ):
        total = total + came(d)[...].astype(F32)
    n.sums_row[...] = total.reshape(n.sums_row.shape)
    loop(1, N_XZ, lambda d: to_chip(d).wait_send())

    def to_row(d):
        to = (row + d) % N_ROW
        return remote(n.sums_row.at[to], n.from_row.at[d - 1], n.s3.at[d - 1], n.r3.at[d - 1], to, col)

    begin(N_ROW, to_row)
    texts.finish()
    loop(1, N_ROW, lambda d: to_row(d).wait_recv())
    total = n.sums_row[row]
    for d in range(N_ROW - 1):
        total = total + n.from_row[d]
    tok_mean = jnp.mean(n.tokens[...].astype(F32).reshape(-1, SEQ, width), 1)
    pooled = tok_mean + total * (1.0 / SEQ)
    pooled_norm = jnp.sqrt(jnp.sum(pooled * pooled, -1, keepdims=True) + 1e-06)
    embed = pooled / pooled_norm
    embed_b = embed.astype(BF16)
    embeds = QuietGather(
        begin, n.e_stage, n.e_whole, [n.es1, n.er1, n.es2, n.er2, n.es3, n.er3, n.es4, n.er4]
    )
    grads = Gather(begin, n.g_stage, n.grads, [n.gs1, n.gr1, n.gs2, n.gr2, n.gs3, n.gr3])
    embeds.start(embed_b.astype(F32))
    at = (8, batch)
    same = (place * N_ROW + row) * 8 + iota(at, 0) == iota(at, 1)
    labels = jnp.where(same, 1.0, -1.0).astype(F32)

    def weigh(mine, others):
        logits = scale * lax.dot_general(mine, others, (((1,), (1,)), ((), ())), preferred_element_type=F32) + shift
        weights = (-factor * labels * jax.nn.sigmoid(-labels * logits)).astype(BF16)
        return jnp.dot(weights, others, preferred_element_type=F32)

    embed_grad = weigh(embed_b, n.everyone[...].reshape(batch, width))
    pooled_grad = (embed_grad - embed * jnp.sum(embed * embed_grad, -1, keepdims=True)) / pooled_norm
    out_grad = pooled_grad * (1.0 / SEQ)
    n.own_grad[...] = out_grad
    grads.start(out_grad)
    grads.spread()
    grads.swap()
    grads.finish()

    def through_down(q):
        block = n.grads[q // 2, pl.ds((q % 2) * 4, 4)].reshape(-1, width)
        for x in range(EXP_DEV):
            back = lax.dot_general(block, n.w_down[x], (((1,), (1,)), ((), ())), preferred_element_type=F32)
            n.acc[x, pl.ds(q * 4, 4)] = back.reshape(4, N_ROW, 8, units)

    def deltas(r):
        n.q[r] = jnp.zeros(n.q.shape[1:], F32)

        def one(x):
            back = n.acc[x, :, r].reshape(records, units).astype(BF16)
            hidden_grad = jnp.dot(n.turned[r, x], back, preferred_element_type=F32)
            shape = (N_COL, capacity, units)
            hidden = n.hidden[x, :, r].reshape(slots, units).astype(F32)
            q = jnp.sum(hidden * hidden_grad, -1, keepdims=True)
            at = (slots, 128)
            q = jnp.where(iota(at, 1) == x * capacity + iota(at, 0) % capacity, q, 0.0)
            n.q[r] += jnp.sum(q.reshape(N_COL, capacity, 128), 1)
            gate_delta = hidden_grad * n.for_gate[x, :, r].reshape(slots, units).astype(F32)
            up_delta = hidden_grad * n.for_up[x, :, r].reshape(slots, units).astype(F32)
            n.for_gate[x, :, r] = gate_delta.astype(BF16).reshape(shape)
            n.for_up[x, :, r] = up_delta.astype(BF16).reshape(shape)
        loop(0, EXP_DEV, one)

    def backward(r):
        def one(x):
            total = fast(n.for_gate[x, :, r].reshape(slots, units), n.w_gate[x], ((1,), (1,)))
            total = total + fast(n.for_up[x, :, r].reshape(slots, units), n.w_up[x], ((1,), (1,)))
            n.back[x, :, r] = total.astype(BF16).reshape(N_COL, capacity, width)
        loop(0, EXP_DEV, one)

    def target(d, at_row):
        return n.back.at[:, (place + d) % N_COL, at_row]

    def far_back(rel, d):
        src = target(d, row_of(rel, 2))
        return remote(src, n.far_buf.at[rel, d], n.bf_send.at[rel, d], n.bf_recv.at[rel, d], row_of(0, near_of(d % 2)), col)

    def near_back(way, rel, d):
        src = target(d, row_of(rel, near_of(way)))
        return remote(
            src, n.near_buf.at[way, rel, d], n.bn_send.at[way, rel, d], n.bn_recv.at[way, rel, d],
            row_of(0, near_of(way)), col,
        )

    def from_across(step, d):
        if step == 0:
            return n.x_buf.at[d]
        return n.x_last.at[step % 4 - 1, d]

    def across_back(step, d):
        return remote(
            target(d, row_of(1, step)), from_across(step, d), n.bx_send.at[step % 4, d], n.bx_recv.at[step % 4, d],
            other_row, col,
        )

    def add_into(place_of_sum, *terms):
        for x in range(EXP_DEV):
            total = place_of_sum[x].astype(F32)
            for term in terms:
                total = total + term[x].astype(F32)
            place_of_sum[x] = total.astype(BF16)

    def q_row(d):
        to = (row + d) % N_ROW
        return remote(n.q.at[to], n.q_buf.at[d - 1], n.q1_send.at[d - 1], n.q1_recv.at[d - 1], to, col)

    embeds.spread()
    loop(0, 4, through_down)
    deltas(row_of(1, 2))
    backward(row_of(1, 2))
    loop(N_COL - X_BACK, N_COL, lambda d: far_back(1, d).start())
    loop(0, N_COL - X_BACK, lambda d: across_back(2, d).start())

    def other_deltas(i):
        r = row_of(1, 2)
        deltas((r + i) % N_ROW)

    loop(1, N_ROW, other_deltas)
    begin(N_ROW, q_row)
    loop(0, 2, lambda way: backward(row_of(1, near_of(way))))
    loop(N_COL - X_BACK, N_COL, lambda d: near_back(1 - d % 2, 1, d).start())
    loop(0, N_COL - X_BACK, lambda d: (across_back(1, d).start(), across_back(-1, d).start()))
    backward(row_of(0, 2))
    loop(N_COL - X_BACK, N_COL, lambda d: far_back(0, d).start())

    def far_first(d):
        across_back(2, d).wait_recv()
        add_into(target(d, row_of(0, 2)), from_across(2, d))
        far_back(0, d).start()

    loop(0, N_COL - X_BACK, far_first)
    loop(1, N_ROW, lambda d: q_row(d).wait_recv())
    total = n.q[row]
    for d in range(N_ROW - 1):
        total = total + n.q_buf[d]
    n.q_msg[...] = jnp.broadcast_to(total[:, None, :], n.q_msg.shape)
    n.q_in[place] = n.q_msg[place]

    def q_col(d):
        to = (place + d) % N_COL
        return remote(n.q_msg.at[to], n.q_in.at[place], n.q2_send.at[d - 1], n.q2_recv.at[d - 1], row, column_of(to))

    begin(N_COL, q_col)
    loop(0, 2, lambda way: backward(row_of(0, near_of(way))))
    loop(N_COL - X_BACK, N_COL, lambda d: near_back(1 - d % 2, 0, d).start())
    backward(other_row)
    loop(0, N_COL - X_BACK, lambda d: across_back(0, d).start())
    backward(row)
    embeds.relay()

    def far_added(rel, d):
        way = d % 2
        far_back(rel, d).wait_recv()
        add_into(target(d, row_of(rel, near_of(way))), n.far_buf.at[rel, d])
        near_back(way, rel, d).start()

    def near_first(d):
        for step in (1, -1):
            across_back(step, d).wait_recv()
            add_into(target(d, row_of(0, step)), from_across(step, d))
        near_back(1 - d % 2, 0, d).start()

    loop(N_COL - X_BACK, N_COL, lambda d: far_added(1, d))
    loop(0, N_COL - X_BACK, near_first)
    loop(0, N_COL - X_BACK, lambda d: far_added(0, d))
    loop(N_COL - X_BACK, N_COL, lambda d: far_added(0, d))
    embeds.swap()

    def weight_grads(x):
        dims = (((0,), (0,)), ((), ()))

        def one(t):
            at = pl.ds(pl.multiple_of(t * 256, 256), 256)
            rows = n.grid[x, :, :, :, at].reshape(-1, 256)
            n.d_gate[x, at] = lax.dot_general(
                rows, n.for_gate[x].reshape(-1, units), dims, preferred_element_type=F32
            )
            n.d_up[x, at] = lax.dot_general(
                rows, n.for_up[x].reshape(-1, units), dims, preferred_element_type=F32
            )
        loop(0, width // 256, one)

    loop(1, N_COL, lambda d: arrived(n.q_in.at[(place + N_COL - d) % N_COL], n.q2_recv.at[d - 1]))
    found = []
    for k in range(2):
        lines = exact(one_hot(to_place[k], N_COL), n.q_in[:, 0, :], ((1,), (0,)))
        found.append(jnp.sum(one_hot(in_line[k], 128) * lines, -1, keepdims=True))
    both = found[0] + found[1]
    score_grad = jnp.zeros((tok_count, 128), F32)
    for k in range(2):
        score_grad = score_grad + one_hot(ids[k], 128) * (found[k] - gates[k] * both)
    router_part = exact(score_grad.T[:experts], norm_in.astype(F32), ((1,), (0,)))
    n.dr[...] = jnp.zeros(n.dr.shape, F32)
    tiles = width // 128
    n.router_term[...] = exact(score_grad[:, :experts], n.router[...], ((1,), (0,)))
    for k in range(experts // 8 * tiles):
        i, j = k // tiles, k % tiles
        n.dr[k // 2, k % 2] = router_part[i * 8 : i * 8 + 8, j * 128 : (j + 1) * 128]

    def scatter(d):
        to = (col + d) % N_COL
        return remote(n.dr.at[to], n.dr_in.at[col], n.d1_send.at[d - 1], n.d1_recv.at[d - 1], row, to)

    def tell_row(d):
        at = n.dr_sum.at[row]
        return remote(at, at, n.d2_send.at[d - 1], n.d2_recv.at[d - 1], (row + d) % N_ROW, col)

    def tell_col(d):
        at = n.dr_out.at[col]
        return remote(at, at, n.d3_send.at[d - 1], n.d3_recv.at[d - 1], row, (col + d) % N_COL)

    begin(N_COL, scatter)
    n.dr_in[col] = n.dr[col]

    def crossed(d):
        near_back(0, 1, d).wait_recv()
        near_back(1, 1, d).wait_recv()
        add_into(target(d, other_row), n.near_buf.at[0, 1, d], n.near_buf.at[1, 1, d])
        across_back(0, d).start()

    loop(N_COL - X_BACK, N_COL, crossed)
    loop(1, N_COL, lambda d: arrived(n.dr_in.at[(col + N_COL - d) % N_COL], n.d1_recv.at[d - 1]))
    n.dr_sum[row] = jnp.sum(n.dr_in[...], 0)
    begin(N_ROW, tell_row)
    weight_grads(0)
    weight_grads(1)

    def down_grads(x):
        def one(t):
            at = pl.ds(pl.multiple_of(t * 128, 128), 128)
            n.d_down[x, at] = fast(
                n.hb[x, :, :, at].reshape(-1, 128), n.grads[...].reshape(batch, width), ((0,), (0,))
            )
        loop(0, units // 128, one)

    def home(d):
        return remote(
            target(d, row), n.slots.at[place], n.h_send.at[d], n.h_recv.at[d], row, column_of((place + d) % N_COL)
        )

    own_home = pltpu.make_async_copy(target(0, row), n.slots.at[place], n.own_sem)

    def complete(d):
        near_back(0, 0, d).wait_recv()
        near_back(1, 0, d).wait_recv()
        across_back(0, d).wait_recv()
        add_into(target(d, row), n.near_buf.at[0, 0, d], n.near_buf.at[1, 0, d], from_across(0, d))

        @pl.when(d != 0)
        def _():
            home(d).start()

        @pl.when(d == 0)
        def _():
            own_home.start()

    loop(0, N_COL - X_BACK, complete)
    loop(1, N_ROW, lambda d: arrived(n.dr_sum.at[(row + N_ROW - d) % N_ROW], n.d2_recv.at[d - 1]))
    n.dr_out[col] = jnp.sum(n.dr_sum[...], 0)
    begin(N_COL, tell_col)
    down_grads(0)
    down_grads(1)
    embeds.finish()
    text_grad = weigh(text_unit.astype(BF16), n.e_whole[...].reshape(batch, width))
    n.d_text[...] = (text_grad - text_unit * jnp.sum(text_unit * text_grad, -1, keepdims=True)) / text_norm
    loop(N_COL - X_BACK, N_COL, complete)

    def back_first(d):
        far_back(1, d).wait_send()
        for way in range(2):
            near_back(way, 1, d).wait_send()

    def back_all(d):
        far_back(0, d).wait_send()
        across_back(0, d).wait_send()
        for way in range(2):
            near_back(way, 0, d).wait_send()

    def back_last(d):
        for step in (-1, 1, 2):
            across_back(step, d).wait_send()

    pending.append(lambda: loop(N_COL - X_BACK, N_COL, back_first))
    pending.append(lambda: loop(0, N_COL, back_all))
    pending.append(lambda: loop(0, N_COL - X_BACK, back_last))
    pending.append(lambda: loop(1, N_COL, lambda d: home(d).wait_send()))

    loop(1, N_COL, lambda d: arrived(n.dr_out.at[(col + N_COL - d) % N_COL], n.d3_recv.at[d - 1]))
    for wait in pending:
        wait()
    loop(1, N_COL, lambda d: arrived(n.slots.at[source(d)], n.h_recv.at[d]))
    own_home.wait()
    for k in range(experts // 8 * tiles):
        i, j = k // tiles, k % tiles
        n.d_router[i * 8 : i * 8 + 8, j * 128 : (j + 1) * 128] = n.dr_out[k // 2, k % 2]
    input_sum = fast(hit, n.slots[...].reshape(-1, width), ((1,), (0,)))
    norm_grad = input_sum + n.router_term[...]
    normed = n.tokens[...].astype(F32) * inverse_rms
    out_grad = jnp.broadcast_to(n.own_grad[...][:, None, :], (8, SEQ, width)).reshape(tok_count, width)
    n.d_tokens[...] = out_grad + inverse_rms * (
        norm_grad - normed * jnp.mean(norm_grad * normed, -1, keepdims=True)
    )


def fused(ins):
    tok_count, width = ins["tokens"].shape
    units = ins["in_gate"].shape[-1]
    experts = EXP_DEV * N_COL
    capacity = max(2, 4 * tok_count // experts)
    slots, records = N_COL * capacity, N_COL * 8
    whole = (2, N_XZ, N_ROW * 8, width)
    block = (EXP_DEV, capacity, width)
    grid = (EXP_DEV, N_COL, N_ROW, capacity)
    outs = {
        "d_text": ((8, width), F32, VMEM),
        "d_tokens": ((tok_count, width), F32, VMEM),
        "d_gate": (ins["in_gate"].shape, F32, VMEM),
        "d_up": (ins["in_up"].shape, F32, VMEM),
        "d_down": (ins["in_down"].shape, F32, VMEM),
        "d_router": (ins["router"].shape, F32, VMEM),
    }
    scratch = {
        "w_gate": (ins["in_gate"].shape, BF16),
        "w_up": (ins["in_up"].shape, BF16),
        "w_down": (ins["in_down"].shape, BF16),
        "rows": ((N_COL, EXP_DEV, capacity, width), BF16),
        "meta": ((N_COL, 8, 128), F32),
        "own_grad": ((8, width), F32),
        "router_term": ((tok_count, width), F32),
        "slots": ((N_COL, EXP_DEV, capacity, width), BF16),
        "dr_out": ((N_COL, 2, 8, 128), F32),
        "grid": (grid + (width,), BF16),
        "table": ((N_COL, 8, 128), F32),
        "compact": ((N_ROW, N_COL // 4, 8, 128), F32),
        "t_stage": ((N_ROW, 8, width), F32),
        "everyone": ((2, 2, 4) + whole[2:], BF16),
        "turned": ((N_ROW, EXP_DEV, slots, records), BF16),
        "hidden": (grid + (units,), BF16),
        "for_gate": (grid + (units,), BF16),
        "for_up": (grid + (units,), BF16),
        "acc": ((EXP_DEV, N_COL, N_ROW, 8, units), F32),
        "hb": ((EXP_DEV, 4, N_ROW * records // 4, units), BF16),
        "sums_row": ((N_ROW, 8, width), F32),
        "from_row": ((N_ROW - 1, 8, width), F32),
        "e_stage": ((N_ROW, 8, width), F32),
        "e_whole": ((2, 2, 4) + whole[2:], BF16),
        "g_stage": ((N_ROW, 8, width), F32),
        "grads": (whole, BF16),
        "back": (grid + (width,), BF16),
        "far_buf": ((2, N_COL) + block, BF16),
        "near_buf": ((2, 2, N_COL) + block, BF16),
        "x_buf": ((N_COL,) + block, BF16),
        "x_last": ((3, N_COL - X_BACK) + block, BF16),
        "q": ((N_ROW, N_COL, 128), F32),
        "q_buf": ((N_ROW - 1, N_COL, 128), F32),
        "q_msg": ((N_COL, 8, 128), F32),
        "q_in": ((N_COL, 8, 128), F32),
        "dr": ((N_COL, 2, 8, 128), F32),
        "dr_in": ((N_COL, 2, 8, 128), F32),
        "dr_sum": ((N_ROW, 2, 8, 128), F32),
    }
    row, col, chips = (N_ROW - 1,), (N_COL - 1,), (N_XZ - 1,)
    sems = {
        "own_sem": (), "w_sem": (3,),
        "m_send": col, "m_recv": col, "a_send": col, "a_recv": (N_COL,), "c_send": row, "c_recv": row,
        "x_send": (4, N_COL), "x_recv": (4, N_COL), "n_send": (2, 2, N_COL), "n_recv": (2, 2, N_COL),
        "f_send": (2, N_COL), "f_recv": (2, N_COL),
        "s1": (), "r1": (), "s2": chips, "r2": chips, "s3": row, "r3": row,
        "bf_send": (2, N_COL), "bf_recv": (2, N_COL), "bn_send": (2, 2, N_COL), "bn_recv": (2, 2, N_COL),
        "bx_send": (4, N_COL), "bx_recv": (4, N_COL), "h_send": (N_COL,), "h_recv": (N_COL,),
        "q1_send": row, "q1_recv": row, "q2_send": col, "q2_recv": col,
        "d1_send": col, "d1_recv": col, "d2_send": row, "d2_recv": row, "d3_send": col, "d3_recv": col,
    }
    for letter in "teg":
        for kind in "sr":
            sems.update({letter + kind + "1": row, letter + kind + "2": chips, letter + kind + "3": (N_XZ,), letter + kind + "4": ()})
    names = list(ins) + list(outs) + list(scratch) + list(sems)
    result = pl.pallas_call(
        functools.partial(fused_kernel, names),
        out_shape=tuple(
            pltpu.VMEM(shape, dtype) if name in KEPT else jax.ShapeDtypeStruct(shape, dtype)
            for name, (shape, dtype, _) in outs.items()
        ),
        in_specs=[
            SMEM if name in ("log_scale", "bias", "loss_scale") else ANY if name.startswith("in_") else VMEM
            for name in ins
        ],
        out_specs=tuple(spec for _, _, spec in outs.values()),
        scratch_shapes=[pltpu.VMEM(shape, dtype) for shape, dtype in scratch.values()]
        + [pltpu.SemaphoreType.DMA(shape) for shape in sems.values()],
        compiler_params=pltpu.CompilerParams(
            collective_id=0, has_side_effects=True, vmem_limit_bytes=50 << 20
        ),
    )(*ins.values())
    return result


def body(tokens, expert_ids, text, w_gate, w_up, w_down, router, log_scale, bias, loss_scale):
    *grads, d_router = fused({
        "tokens": tokens, "ids": expert_ids.T, "text": text, "in_gate": w_gate, "in_up": w_up, "in_down": w_down,
        "router": router.T, "log_scale": log_scale, "bias": bias, "loss_scale": loss_scale,
    })
    return (*grads, d_router.T)


def solution(mesh):
    in_specs = (
        P(("row", "col"), None),
        P(("row", "col"), None),
        P(("row", "col"), None),
        P("col", None, "row"),
        P("col", None, "row"),
        P("col", "row", None),
        P(),
        P(),
        P(),
        P(),
    )
    out_specs = (
        P(("row", "col"), None),
        P(("row", "col"), None),
        P("col", None, "row"),
        P("col", None, "row"),
        P("col", "row", None),
        P(),
    )
    return jax.shard_map(body, mesh=mesh, in_specs=in_specs, out_specs=out_specs, check_vma=False)
```
